512 devices in a mesh: section: 2 (over core), tp: 64 (over y_hi, x, z), rep: 4 (over y_lo).
Axes of the slice: x: 4, y: 8 (y_hi: 2, y_lo: 4; y = y_hi * 4 + y_lo), z: 8, core: 2. Of those that a mesh axis runs over, the one named last changes fastest.
Arguments:
- hidden: bfloat16 [8, 1024, 7168], P(('section', 'rep'), None, 'tp'), may hold values from -6 to 6
- comp_query: bfloat16 [8, 1024, 1536], P(('section', 'rep'), 'tp'), may hold values from -6 to 6
- kv_down: bfloat16 [7168, 576], P('tp'), may hold values from -2.5 to 2.5
- kv_gain: float32 [512], replicated, may hold values from 0.25 to 1.75
- q_up: bfloat16 [1536, 24576], P(None, 'tp'), may hold values from -2.5 to 2.5
- kv_up: bfloat16 [512, 32768], P(None, 'tp'), may hold values from -0.25 to 0.25
- req_blocks: int32 [8, 3], P('section'), may hold values from 1 to 4, 8 in all within a row
- dest_slot: int32 [2, 12], P('section'), may hold values from 0 to 11, each once within a row
- dec_query: bfloat16 [24, 4, 1536], P(('section', 'rep')), may hold values from -6 to 6
- dec_latent: bfloat16 [24, 4, 576], P(('section', 'rep')), may hold values from -6 to 6
Outputs:
- prefill_out: bfloat16 [8, 1024, 16384], P(('section', 'rep'), None, 'tp')
- decode_out: bfloat16 [24, 4, 16384], P(('section', 'rep'), None, 'tp')
The draws below stay inside these ranges and needn't reach their ends.
Inputs may be any that keep to these rules, and one draw needn't show every extreme that they name: `req_blocks`: each row sums to 8. `dest_slot`: each row is a permutation of the decode slots of its section.
All inputs are finite; a program needn't handle non-finite values.
Results may differ from the reference program's by a relative error of at most 0.011.
Values may be sent and summed in bfloat16 or wider, within the bound.
No kernel may reach another device: no remote copies, remote signals or barrier semaphores. Data moves between devices by JAX's collectives and lax.ppermute only.
A program may use at most 64 MiB of HBM per device.

```python
import math
import jax
import jax.numpy as jnp
import numpy as np
from jax import lax

D = 7168
HEADS = 128
QUERY_LATENT = 1536
KVL = 512
NOPE = 128
ROPE = 64
VD = 128
STRETCH = 1024
BLK = 128
NREQ = 3
DECODE_STEPS = 4
LATENT_WIDTH = 576
NGROUP = 8
DECODE_SLOTS = 24
N_SECTION = 2
N_REP = 4


def draw_hidden(key, part):
    key = jax.random.fold_in(key, 11)
    value_rows = jax.random.truncated_normal(key, -6.0, 6.0, (NGROUP, STRETCH, D), jnp.float32)
    return value_rows.astype(jnp.bfloat16)


def draw_comp_query(key, part):
    key = jax.random.fold_in(key, 12)
    value_rows = jax.random.truncated_normal(key, -6.0, 6.0, (NGROUP, STRETCH, QUERY_LATENT), jnp.float32)
    return value_rows.astype(jnp.bfloat16)


def draw_dec_query(key, part):
    key = jax.random.fold_in(key, 13)
    value_rows = jax.random.truncated_normal(key, -6.0, 6.0, (DECODE_SLOTS, DECODE_STEPS, QUERY_LATENT), jnp.float32)
    return value_rows.astype(jnp.bfloat16)


def draw_dec_latent(key, part):
    key = jax.random.fold_in(key, 14)
    value_rows = jax.random.truncated_normal(key, -6.0, 6.0, (DECODE_SLOTS, DECODE_STEPS, LATENT_WIDTH), jnp.float32)
    return value_rows.astype(jnp.bfloat16)


def draw_q_up(key, part):
    key = jax.random.fold_in(key, 15)
    value_rows = jax.random.truncated_normal(key, -6.0, 6.0, (QUERY_LATENT, HEADS * (NOPE + ROPE)), jnp.float32) * QUERY_LATENT ** (-0.5)
    return value_rows.astype(jnp.bfloat16)


def draw_kv_down(key, part):
    key = jax.random.fold_in(key, 16)
    value_rows = jax.random.truncated_normal(key, -6.0, 6.0, (D, LATENT_WIDTH), jnp.float32) * D ** (-0.5)
    return value_rows.astype(jnp.bfloat16)


def level_of(key, shape, pieces, low, top_value):
    level, own = 1.0, jax.random.fold_in(key, 6)
    for dim, parts in pieces:
        heights = jnp.exp(jax.random.uniform(jax.random.fold_in(own, dim), (parts,), jnp.float32, low / len(pieces), top_value / len(pieces)))
        level = level * jnp.repeat(heights, shape[dim] // parts).reshape([-1 if axis == dim else 1 for axis in range(len(shape))])
    return level


def length_profile(number_of, total, reach, slope):
    loads = [(1 << 20) // math.isqrt(rank ** slope) + 1 for rank in range(2, number_of + 1)]
    surplus, counts = total - reach - (number_of - 1), [1] * (number_of - 1)
    while surplus > 0:
        candidates = [i for i in range(number_of - 1) if counts[i] < reach]
        whole, left = sum([loads[i] for i in candidates]), surplus
        for i in candidates:
            extra = min(reach - counts[i], max(1, left * loads[i] // whole), surplus)
            counts[i] = counts[i] + extra
            surplus = surplus - extra
    return np.array([reach] + counts)


def uneven(rng, amount, total, reach, lean):
    if amount == 2:
        one = jax.random.randint(rng, (), max(1, total - reach), min(reach, total - 1) + 1)
        return jnp.stack([one, total - one])
    sizes = jnp.asarray(length_profile(amount, total, reach, lean), jnp.int32)
    pairs = (amount - 1) // 2
    donor, sink = sizes[1:1 + 2 * pairs:2], sizes[2:2 + 2 * pairs:2]
    room = jnp.minimum(donor - 1, reach - sink)
    passed = jax.random.randint(jax.random.fold_in(rng, 1), (pairs,), 0, 1 << 20) % (room + 1)
    sizes = sizes.at[1:1 + 2 * pairs:2].set(donor - passed).at[2:2 + 2 * pairs:2].set(sink + passed)
    return sizes[jax.random.permutation(jax.random.fold_in(rng, 2), amount)]


def centred(stream_key, shape, width, most, cuts=(), kind=jnp.bfloat16):
    array = jax.random.normal(stream_key, shape, jnp.float32) * width
    if len(cuts) > 0:
        array = level_of(stream_key, shape, cuts, -0.22, 0.18) * array
    return jnp.clip(array, min=-most, max=most).astype(kind)


def setup_inputs(seed: int = 0) -> dict:
    arg_keys = jax.random.split(jax.random.key(seed), 11)
    hidden = draw_hidden(jax.random.fold_in(arg_keys[10], 71), 0)
    comp_query = draw_comp_query(jax.random.fold_in(arg_keys[10], 71), 0)
    kv_down = draw_kv_down(jax.random.fold_in(arg_keys[10], 71), 0)
    kv_gain = jnp.clip(1.0 + 0.15 * jax.random.normal(arg_keys[3], (KVL,), jnp.float32), 0.25, 1.75)
    q_up = draw_q_up(jax.random.fold_in(arg_keys[10], 71), 0)
    kv_up = centred(arg_keys[5], (KVL, HEADS * (NOPE + VD)), KVL ** -0.5, 0.25, ((1, 64),))
    req_blocks = jax.vmap(lambda own: uneven(own, NREQ, STRETCH // BLK, STRETCH // BLK // 2, 2))(jax.random.split(arg_keys[6], NGROUP)).reshape((NGROUP, NREQ)).astype(jnp.int32)
    dest_slot = jax.vmap(lambda own: jax.random.permutation(own, N_REP * NREQ))(jax.random.split(arg_keys[7], N_SECTION)).reshape((N_SECTION, N_REP * NREQ)).astype(jnp.int32)
    dec_query = draw_dec_query(jax.random.fold_in(arg_keys[10], 71), 0)
    dec_latent = draw_dec_latent(jax.random.fold_in(arg_keys[10], 71), 0)
    return {"hidden": hidden, "comp_query": comp_query, "kv_down": kv_down, "kv_gain": kv_gain, "q_up": q_up, "kv_up": kv_up, "req_blocks": req_blocks, "dest_slot": dest_slot, "dec_query": dec_query, "dec_latent": dec_latent}


softmax_gain = (1.0 + 0.1 * math.log(40.0)) ** 2

def rotate(pair_values, positions):
    half_width = pair_values.shape[-1] // 2
    frequency = 10000.0 ** (-jnp.arange(half_width, dtype=jnp.float32) * 2.0 / pair_values.shape[-1])
    angles = positions[..., None] * frequency
    cos_part = jnp.cos(angles)
    sine_part = jnp.sin(angles)
    first_half = pair_values[..., :half_width]
    second = pair_values[..., half_width:]
    return jnp.concatenate([first_half * cos_part - second * sine_part, first_half * sine_part + second * cos_part], axis=-1)

def request_spans(blocks, block_rows):
    lengths = (blocks * block_rows).astype(jnp.int32)
    starts = (jnp.cumsum(lengths, axis=-1) - lengths).astype(jnp.int32)
    return (starts, lengths)

def row_places(row_index, starts, lengths):
    inside = (row_index[:, None] >= starts[None, :]) & (row_index[:, None] < (starts + lengths)[None, :])
    member = inside.astype(jnp.int32)
    segment = lax.optimization_barrier(jnp.sum(member * jnp.arange(starts.shape[0], dtype=jnp.int32)[None, :], axis=1)).astype(jnp.int32)
    offset = (row_index - lax.optimization_barrier(jnp.sum(member * starts[None, :], axis=1))).astype(jnp.int32)
    return (segment, offset)

def norm_latent(latent, kv_gain, offset):
    content = latent[:, :KVL]
    inv_scale = lax.rsqrt(lax.optimization_barrier(jnp.mean(content * content, axis=1, keepdims=True)) + 1e-06)
    rotated_pe = rotate(latent[:, KVL:], offset.astype(jnp.float32))
    return jnp.concatenate([content * inv_scale * kv_gain[None, :], rotated_pe], axis=1).astype(jnp.bfloat16)

def make_queries(input_rows, q_up, offset):
    projected = jnp.dot(input_rows, q_up, preferred_element_type=jnp.float32)
    projected = projected.reshape(input_rows.shape[0], -1, NOPE + ROPE)
    rotated_pe = rotate(projected[..., NOPE:], offset.astype(jnp.float32)[:, None])
    return jnp.concatenate([projected[..., :NOPE], rotated_pe], axis=-1).astype(jnp.bfloat16)

def attend_group(queries, latent_cache, kv_up, segment):
    group_rows = latent_cache.shape[0]
    expanded = jnp.dot(latent_cache[:, :KVL], kv_up, preferred_element_type=jnp.float32).astype(jnp.bfloat16)
    expanded = expanded.reshape(group_rows, -1, NOPE + VD)
    row_index = jnp.arange(group_rows, dtype=jnp.int32)
    allowed = (segment[:, None] == segment[None, :]) & (row_index[None, :] <= row_index[:, None])

    def one_head(inputs):
        head_query, key_nope, head_value = inputs
        all_keys = jnp.concatenate([key_nope, latent_cache[:, KVL:]], axis=1)
        scores = jnp.dot(head_query, all_keys.T, preferred_element_type=jnp.float32) * (softmax_gain * (NOPE + ROPE) ** (-0.5))
        scores = jnp.where(allowed, scores, -1e+30)
        weights = jax.nn.softmax(scores, axis=1).astype(jnp.bfloat16)
        return jnp.dot(weights, head_value, preferred_element_type=jnp.float32).astype(jnp.bfloat16)
    outputs = lax.map(one_head, (jnp.swapaxes(queries, 0, 1), jnp.swapaxes(expanded[..., :NOPE], 0, 1), jnp.swapaxes(expanded[..., NOPE:], 0, 1)))
    return jnp.swapaxes(outputs, 0, 1).reshape(group_rows, -1)

def decode_request(step_rows, step_latent, latent_cache, row_start, length, q_up, kv_up):
    step_count = step_rows.shape[0]
    group_rows = latent_cache.shape[0]
    projected = jnp.dot(step_rows, q_up, preferred_element_type=jnp.float32).astype(jnp.bfloat16)
    projected = projected.reshape(step_count, -1, NOPE + ROPE)
    new_positions = (length + jnp.arange(step_count, dtype=jnp.int32)).astype(jnp.float32)
    query_pe = rotate(projected[..., NOPE:].astype(jnp.float32), new_positions[:, None]).astype(jnp.bfloat16)
    absorbed = kv_up.reshape(KVL, -1, NOPE + VD)
    latent_query = jnp.einsum('thn,khn->thk', projected[..., :NOPE].astype(jnp.float32), absorbed[..., :NOPE].astype(jnp.float32)).astype(jnp.bfloat16)
    new_keys = jnp.concatenate([step_latent[:, :KVL], rotate(step_latent[:, KVL:].astype(jnp.float32), new_positions).astype(jnp.bfloat16)], axis=1)
    all_keys = jnp.concatenate([latent_cache, new_keys], axis=0)
    full_query = jnp.concatenate([latent_query, query_pe], axis=-1)
    scores = jnp.einsum('thl,kl->thk', full_query.astype(jnp.float32), all_keys.astype(jnp.float32)) * (softmax_gain * (NOPE + ROPE) ** (-0.5))
    row_index = jnp.arange(group_rows, dtype=jnp.int32)
    old_allowed = (row_index >= row_start) & (row_index < row_start + length)
    step_index = jnp.arange(step_count, dtype=jnp.int32)
    new_allowed = step_index[None, :] <= step_index[:, None]
    allowed = jnp.concatenate([jnp.broadcast_to(old_allowed[None, :], (step_count, group_rows)), new_allowed], axis=1)
    scores = jnp.where(allowed[:, None, :], scores, -1e+30)
    weights = jax.nn.softmax(scores, axis=-1).astype(jnp.bfloat16)
    mixture = jnp.einsum('thk,kc->thc', weights.astype(jnp.float32), all_keys[:, :KVL].astype(jnp.float32)).astype(jnp.bfloat16)
    result = jnp.einsum('thc,chv->thv', mixture.astype(jnp.float32), absorbed[..., NOPE:].astype(jnp.float32)).astype(jnp.bfloat16)
    return result.reshape(step_count, -1)

def reference(hidden, comp_query, kv_down, kv_gain, q_up, kv_up, req_blocks, dest_slot, dec_query, dec_latent):
    row_index = jnp.arange(STRETCH, dtype=jnp.int32)

    def prefill(inputs):
        block_x, block_q, blocks = inputs
        starts, lengths = request_spans(blocks, BLK)
        segment, offset = row_places(row_index, starts, lengths)
        latent = jnp.dot(block_x, kv_down, preferred_element_type=jnp.float32)
        latent_cache = norm_latent(latent, kv_gain, offset)
        queries = make_queries(block_q, q_up, offset)
        return (attend_group(queries, latent_cache, kv_up, segment), latent_cache)
    prefill_out, caches = lax.map(prefill, (hidden, comp_query, req_blocks))
    all_starts, all_lengths = request_spans(req_blocks, BLK)
    slot_numbers = jnp.arange(DECODE_SLOTS, dtype=jnp.int32)
    per_section = N_REP * NREQ
    source_ids = jnp.arange(per_section, dtype=jnp.int32)

    def one_slot(inputs):
        section_index, local_slot, step_rows, step_latent = inputs
        matched = dest_slot[section_index] == local_slot
        source = jnp.sum(jnp.where(matched, source_ids, 0)).astype(jnp.int32)
        group_index = section_index * N_REP + source // NREQ
        request = source % NREQ
        return decode_request(step_rows, step_latent, caches[group_index], all_starts[group_index, request], all_lengths[group_index, request], q_up, kv_up)
    decode_out = lax.map(one_slot, (slot_numbers // per_section, slot_numbers % per_section, dec_query, dec_latent))
    return (prefill_out, decode_out)
```

```python
import math

import jax
import jax.numpy as jnp
from jax import lax
from jax.sharding import Mesh, PartitionSpec as P

KVL = 512
NOPE = 128
ROPE = 64
VD = 128
BLK = 128
NREQ = 3
STEPS = 4
REACH = 4
NREP = 4
NX = 4

SIGMA = (1.0 + 0.1 * math.log(40.0)) ** 2 * (NOPE + ROPE) ** (-0.5)
bf16 = jnp.bfloat16
f32 = jnp.float32


def cos_sin(positions):
    half = ROPE // 2
    frequency = 10000.0 ** (-jnp.arange(half, dtype=f32) * 2.0 / ROPE)
    angles = positions.astype(f32)[..., None] * frequency
    return jnp.cos(angles), jnp.sin(angles)


def rotate(u, cos_part, sin_part):
    half = ROPE // 2
    a, b = u[..., :half], u[..., half:]
    return jnp.concatenate([a * cos_part - b * sin_part, a * sin_part + b * cos_part], axis=-1)


def spread(a, axes, count):
    copies = jnp.broadcast_to(a[None], (count,) + a.shape)
    return lax.all_to_all(copies, axes, 0, 0, tiled=True)


def body(hidden, comp_query, kv_down, kv_gain, q_up, kv_up, req_blocks, dest_slot, dec_query, dec_latent):
    rep = lax.axis_index("rep")
    yz_index = lax.axis_index(("yh", "z"))
    x_index = lax.axis_index("x")
    block_x = hidden[0]
    rows = block_x.shape[0]
    features = block_x.shape[1]

    lengths_all = req_blocks * BLK
    starts_all = jnp.cumsum(lengths_all, axis=-1) - lengths_all
    lengths = lax.dynamic_index_in_dim(lengths_all, rep, 0, keepdims=False)
    starts = lax.dynamic_index_in_dim(starts_all, rep, 0, keepdims=False)

    def start_of(row):
        inside = (row[:, None] >= starts[None]) & (row[:, None] < (starts + lengths)[None])
        return jnp.sum(jnp.where(inside, starts[None], 0), axis=1)

    row_index = jnp.arange(rows, dtype=jnp.int32)
    row_start = start_of(row_index)
    offset = row_index - row_start

    per_x = rows // NX
    hidden_t = jnp.swapaxes(block_x.reshape(NX, per_x, features), 1, 2)
    packed = jnp.concatenate(
        [hidden_t, jnp.broadcast_to(kv_down[None], (NX,) + kv_down.shape)], axis=2
    )
    packed = lax.all_to_all(packed, "x", 0, 0, tiled=True).reshape(NX * features, -1)
    partial = lax.dot_general(
        packed[:, :per_x], packed[:, per_x:], (((0,), (0,)), ((), ())), preferred_element_type=f32
    )
    chunk = per_x // 16
    pieces = lax.all_to_all(partial.reshape(16, chunk, -1), ("yh", "z"), 0, 0, tiled=True)
    latent = jnp.sum(pieces, axis=0)
    own_rows = x_index * per_x + yz_index * chunk + jnp.arange(chunk, dtype=jnp.int32)
    content = latent[:, :KVL]
    inv_scale = lax.rsqrt(jnp.mean(content * content, axis=1, keepdims=True) + 1e-06)
    cos_o, sin_o = cos_sin(own_rows - start_of(own_rows))
    own_cache = jnp.concatenate(
        [content * inv_scale * kv_gain[None, :], rotate(latent[:, KVL:], cos_o, sin_o)], axis=1
    ).astype(bf16)
    cache = spread(own_cache, ("yh", "z"), 16).reshape(per_x, -1)
    cache = spread(cache, "x", NX).reshape(rows, -1)

    cq = spread(comp_query[0], ("yh", "z"), 16)
    cq = spread(cq.reshape(2, 8 * 16, -1), "x", NX)
    cq = jnp.swapaxes(cq.reshape(NX, 2, 128, -1), 0, 1).reshape(rows, -1)
    heads = q_up.shape[1] // (NOPE + ROPE)
    cos_q, sin_q = cos_sin(offset)
    projected = jnp.dot(cq, q_up, preferred_element_type=f32).reshape(rows, heads, NOPE + ROPE)
    queries = jnp.concatenate(
        [projected[..., :NOPE], rotate(projected[..., NOPE:], cos_q[:, None], sin_q[:, None])], axis=-1
    ).astype(bf16)

    slots = lax.dynamic_slice_in_dim(dest_slot[0], rep * NREQ, NREQ, 0)
    rep_in = spread(jnp.concatenate([dec_query, dec_latent], axis=2), "rep", NREP)
    rep_in = rep_in.reshape(NREP * NREQ, STEPS, -1)
    mine = jnp.take(rep_in, slots, axis=0, mode="clip")
    my_query = mine[..., : dec_query.shape[2]].reshape(NREQ * STEPS, -1)
    my_latent = mine[..., dec_query.shape[2] :].reshape(NREQ * STEPS, -1)
    new_pos = (lengths[:, None] + jnp.arange(STEPS, dtype=jnp.int32)[None]).reshape(-1)
    cos_d, sin_d = cos_sin(new_pos)
    new_keys = jnp.concatenate(
        [my_latent[:, :KVL], rotate(my_latent[:, KVL:].astype(f32), cos_d, sin_d).astype(bf16)], axis=1
    )
    dq = jnp.dot(my_query, q_up, preferred_element_type=f32).astype(bf16)
    dq = dq.reshape(NREQ * STEPS, heads, NOPE + ROPE)
    query_pe = rotate(dq[..., NOPE:].astype(f32), cos_d[:, None], sin_d[:, None]).astype(bf16)
    absorbed = kv_up.reshape(KVL, heads, NOPE + VD)
    latent_query = jnp.einsum(
        "rhn,khn->hrk", dq[..., :NOPE], absorbed[..., :NOPE], preferred_element_type=f32
    ).astype(bf16)
    full_query = jnp.concatenate([latent_query, jnp.swapaxes(query_pe, 0, 1)], axis=-1)
    full_query = full_query.reshape(heads * NREQ * STEPS, -1)
    all_keys = jnp.concatenate([cache, new_keys], axis=0)
    scores = lax.dot_general(
        full_query, all_keys, (((1,), (1,)), ((), ())), preferred_element_type=f32
    ) * SIGMA
    step_row = jnp.arange(NREQ * STEPS, dtype=jnp.int32)
    low = jnp.repeat(starts, STEPS)[:, None]
    high = jnp.repeat(starts + lengths, STEPS)[:, None]
    old_ok = (row_index[None] >= low) & (row_index[None] < high)
    new_ok = (step_row[None] // STEPS == step_row[:, None] // STEPS) & (step_row[None] <= step_row[:, None])
    ok = jnp.tile(jnp.concatenate([old_ok, new_ok], axis=1), (heads, 1))
    scores = jnp.where(ok, scores, -1e30)
    weights = jax.nn.softmax(scores, axis=-1).astype(bf16)
    mixture = jnp.dot(weights, all_keys[:, :KVL], preferred_element_type=f32).astype(bf16)
    mixture = mixture.reshape(heads, NREQ * STEPS, KVL)
    result = jnp.einsum("hrc,chv->rhv", mixture, absorbed[..., NOPE:], preferred_element_type=f32)
    result = result.astype(bf16).reshape(NREQ, STEPS, heads * VD)
    pool = spread(result, "rep", NREP).reshape(NREP * NREQ, STEPS, heads * VD)
    slot_numbers = rep * NREQ + jnp.arange(NREQ, dtype=jnp.int32)
    source = jnp.sum(
        jnp.where(dest_slot[0][None] == slot_numbers[:, None], jnp.arange(NREP * NREQ, dtype=jnp.int32)[None], 0),
        axis=1,
    )
    decode_out = jnp.take(pool, source, axis=0, mode="clip")

    expanded = jnp.dot(cache[:, :KVL], kv_up, preferred_element_type=f32).astype(bf16)
    outs = []
    for h in range(heads):
        base = h * (NOPE + VD)
        keys = jnp.concatenate([expanded[:, base : base + NOPE], cache[:, KVL:]], axis=1)
        values = expanded[:, base + NOPE : base + NOPE + VD]
        blocks = []
        for i in range(rows // BLK):
            first = max(0, i - REACH + 1) * BLK
            last = (i + 1) * BLK
            s = lax.dot_general(
                queries[i * BLK : last, h], keys[first:last], (((1,), (1,)), ((), ())),
                preferred_element_type=f32,
            ) * SIGMA
            column = row_index[first:last][None]
            ok_block = (column >= row_start[i * BLK : last, None]) & (column <= row_index[i * BLK : last, None])
            w = jax.nn.softmax(jnp.where(ok_block, s, -1e30), axis=1).astype(bf16)
            blocks.append(jnp.dot(w, values[first:last], preferred_element_type=f32).astype(bf16))
        outs.append(jnp.concatenate(blocks, axis=0))
    prefill_out = jnp.concatenate(outs, axis=1)[None]
    return prefill_out, decode_out


def solution(mesh):
    fine = Mesh(mesh.devices.reshape(2, 2, 4, 8, 4), ("section", "yh", "x", "z", "rep"))
    tp = ("yh", "x", "z")
    group = ("section", "rep")
    in_specs = (
        P(group, None, tp),
        P(group, tp, None),
        P(tp, None),
        P(),
        P(None, tp),
        P(None, tp),
        P("section", None),
        P("section", None),
        P(group, None, None),
        P(group, None, None),
    )
    out_specs = (P(group, None, tp), P(group, None, tp))
    return jax.shard_map(body, mesh=fine, in_specs=in_specs, out_specs=out_specs, check_vma=False)
```

```python
import math

import jax
import jax.numpy as jnp
from jax import lax
from jax.sharding import Mesh, PartitionSpec as P

KVL = 512
NOPE = 128
ROPE = 64
VD = 128
BLK = 128
NREQ = 3
STEPS = 4
REACH = 4
NREP = 4
NX = 4

SIGMA = (1.0 + 0.1 * math.log(40.0)) ** 2 * (NOPE + ROPE) ** (-0.5)
bf16 = jnp.bfloat16
f32 = jnp.float32


def cos_sin(positions):
    half = ROPE // 2
    frequency = 10000.0 ** (-jnp.arange(half, dtype=f32) * 2.0 / ROPE)
    angles = positions.astype(f32)[..., None] * frequency
    return jnp.cos(angles), jnp.sin(angles)


def rotate(u, cos_part, sin_part):
    half = ROPE // 2
    a, b = u[..., :half], u[..., half:]
    return jnp.concatenate([a * cos_part - b * sin_part, a * sin_part + b * cos_part], axis=-1)


def spread(a, axes, count):
    copies = jnp.broadcast_to(a[None], (count,) + a.shape)
    return lax.all_to_all(copies, axes, 0, 0, tiled=True)


def shift(count, d):
    return [(i, (i + d) % count) for i in range(count)]


def body(hidden, comp_query, kv_down, kv_gain, q_up, kv_up, req_blocks, dest_slot, dec_query, dec_latent):
    rep = lax.axis_index("rep")
    yz_index = lax.axis_index(("yh", "z"))
    x_index = lax.axis_index("x")
    block_x = hidden[0]
    rows = block_x.shape[0]
    features = block_x.shape[1]

    lengths_all = req_blocks * BLK
    starts_all = jnp.cumsum(lengths_all, axis=-1) - lengths_all
    lengths = lax.dynamic_index_in_dim(lengths_all, rep, 0, keepdims=False)
    starts = lax.dynamic_index_in_dim(starts_all, rep, 0, keepdims=False)

    def start_of(row):
        inside = (row[:, None] >= starts[None]) & (row[:, None] < (starts + lengths)[None])
        return jnp.sum(jnp.where(inside, starts[None], 0), axis=1)

    row_index = jnp.arange(rows, dtype=jnp.int32)
    row_start = start_of(row_index)
    offset = row_index - row_start

    per_x = rows // NX
    hidden_t = jnp.swapaxes(block_x.reshape(NX, per_x, features), 1, 2)
    packed = jnp.concatenate(
        [hidden_t, jnp.broadcast_to(kv_down[None], (NX,) + kv_down.shape)], axis=2
    )
    packed = lax.all_to_all(packed, "x", 0, 0, tiled=True).reshape(NX * features, -1)
    partial = lax.dot_general(
        packed[:, :per_x], packed[:, per_x:], (((0,), (0,)), ((), ())), preferred_element_type=f32
    )
    chunk = per_x // 16
    pieces = lax.all_to_all(partial.reshape(16, chunk, -1), ("yh", "z"), 0, 0, tiled=True)
    latent = jnp.sum(pieces, axis=0)
    own_rows = x_index * per_x + yz_index * chunk + jnp.arange(chunk, dtype=jnp.int32)
    content = latent[:, :KVL]
    inv_scale = lax.rsqrt(jnp.mean(content * content, axis=1, keepdims=True) + 1e-06)
    cos_o, sin_o = cos_sin(own_rows - start_of(own_rows))
    own_cache = jnp.concatenate(
        [content * inv_scale * kv_gain[None, :], rotate(latent[:, KVL:], cos_o, sin_o)], axis=1
    ).astype(bf16)
    cache = spread(own_cache, ("yh", "z"), 16).reshape(per_x, -1)
    cache = spread(cache, "x", NX).reshape(rows, -1)

    yh_index = lax.axis_index("yh")
    own = comp_query[0]
    other = lax.ppermute(own, "yh", shift(2, 1))
    pair = jnp.where(yh_index == 0, jnp.stack([own, other]), jnp.stack([other, own]))
    line = jnp.zeros((2, NX) + own.shape, own.dtype)
    line = lax.dynamic_update_slice_in_dim(line, pair[:, None], x_index, 1)
    for d in range(1, NX):
        arrived = lax.ppermute(pair, "x", shift(NX, d))
        line = lax.dynamic_update_slice_in_dim(line, arrived[:, None], (x_index - d) % NX, 1)
    cq = lax.all_gather(line.reshape(128, -1), "z", axis=0, tiled=True)
    heads = q_up.shape[1] // (NOPE + ROPE)
    q_offset = jnp.swapaxes(offset.reshape(8, 8, 16), 0, 1).reshape(-1)
    cos_q, sin_q = cos_sin(q_offset)
    projected = jnp.dot(cq, q_up, preferred_element_type=f32).reshape(rows, heads, NOPE + ROPE)
    queries = jnp.concatenate(
        [projected[..., :NOPE], rotate(projected[..., NOPE:], cos_q[:, None], sin_q[:, None])], axis=-1
    ).astype(bf16)
    queries = jnp.swapaxes(queries.reshape(8, 8, 16, heads, -1), 0, 1).reshape(rows, heads, -1)

    slots = lax.dynamic_slice_in_dim(dest_slot[0], rep * NREQ, NREQ, 0)
    rep_own = jnp.concatenate([dec_query, dec_latent], axis=2)
    rep_in = jnp.zeros((NREP,) + rep_own.shape, rep_own.dtype)
    rep_in = lax.dynamic_update_slice_in_dim(rep_in, rep_own[None], rep, 0)
    for d in range(1, NREP):
        arrived = lax.ppermute(rep_own, "rep", shift(NREP, d))
        rep_in = lax.dynamic_update_slice_in_dim(rep_in, arrived[None], (rep - d) % NREP, 0)
    rep_in = rep_in.reshape(NREP * NREQ, STEPS, -1)
    mine = jnp.take(rep_in, slots, axis=0, mode="clip")
    my_query = mine[..., : dec_query.shape[2]].reshape(NREQ * STEPS, -1)
    my_latent = mine[..., dec_query.shape[2] :].reshape(NREQ * STEPS, -1)
    new_pos = (lengths[:, None] + jnp.arange(STEPS, dtype=jnp.int32)[None]).reshape(-1)
    cos_d, sin_d = cos_sin(new_pos)
    new_keys = jnp.concatenate(
        [my_latent[:, :KVL], rotate(my_latent[:, KVL:].astype(f32), cos_d, sin_d).astype(bf16)], axis=1
    )
    dq = jnp.dot(my_query, q_up, preferred_element_type=f32).astype(bf16)
    dq = dq.reshape(NREQ * STEPS, heads, NOPE + ROPE)
    query_pe = rotate(dq[..., NOPE:].astype(f32), cos_d[:, None], sin_d[:, None]).astype(bf16)
    absorbed = kv_up.reshape(KVL, heads, NOPE + VD)
    latent_query = jnp.einsum(
        "rhn,khn->hrk", dq[..., :NOPE], absorbed[..., :NOPE], preferred_element_type=f32
    ).astype(bf16)
    full_query = jnp.concatenate([latent_query, jnp.swapaxes(query_pe, 0, 1)], axis=-1)
    full_query = full_query.reshape(heads * NREQ * STEPS, -1)
    all_keys = jnp.concatenate([cache, new_keys], axis=0)
    scores = lax.dot_general(
        full_query, all_keys, (((1,), (1,)), ((), ())), preferred_element_type=f32
    ) * SIGMA
    step_row = jnp.arange(NREQ * STEPS, dtype=jnp.int32)
    low = jnp.repeat(starts, STEPS)[:, None]
    high = jnp.repeat(starts + lengths, STEPS)[:, None]
    old_ok = (row_index[None] >= low) & (row_index[None] < high)
    new_ok = (step_row[None] // STEPS == step_row[:, None] // STEPS) & (step_row[None] <= step_row[:, None])
    ok = jnp.tile(jnp.concatenate([old_ok, new_ok], axis=1), (heads, 1))
    scores = jnp.where(ok, scores, -1e30)
    weights = jax.nn.softmax(scores, axis=-1).astype(bf16)
    mixture = jnp.dot(weights, all_keys[:, :KVL], preferred_element_type=f32).astype(bf16)
    mixture = mixture.reshape(heads, NREQ * STEPS, KVL)
    result = jnp.einsum("hrc,chv->rhv", mixture, absorbed[..., NOPE:], preferred_element_type=f32)
    result = result.astype(bf16).reshape(NREQ, STEPS, heads * VD)
    pool = spread(result, "rep", NREP).reshape(NREP * NREQ, STEPS, heads * VD)
    slot_numbers = rep * NREQ + jnp.arange(NREQ, dtype=jnp.int32)
    source = jnp.sum(
        jnp.where(dest_slot[0][None] == slot_numbers[:, None], jnp.arange(NREP * NREQ, dtype=jnp.int32)[None], 0),
        axis=1,
    )
    decode_out = jnp.take(pool, source, axis=0, mode="clip")

    expanded = jnp.dot(cache[:, :KVL], kv_up, preferred_element_type=f32).astype(bf16)
    outs = []
    for h in range(heads):
        base = h * (NOPE + VD)
        keys = jnp.concatenate([expanded[:, base : base + NOPE], cache[:, KVL:]], axis=1)
        values = expanded[:, base + NOPE : base + NOPE + VD]
        blocks = []
        for i in range(rows // BLK):
            first = max(0, i - REACH + 1) * BLK
            last = (i + 1) * BLK
            s = lax.dot_general(
                queries[i * BLK : last, h], keys[first:last], (((1,), (1,)), ((), ())),
                preferred_element_type=f32,
            ) * SIGMA
            column = row_index[first:last][None]
            ok_block = (column >= row_start[i * BLK : last, None]) & (column <= row_index[i * BLK : last, None])
            w = jax.nn.softmax(jnp.where(ok_block, s, -1e30), axis=1).astype(bf16)
            blocks.append(jnp.dot(w, values[first:last], preferred_element_type=f32).astype(bf16))
        outs.append(jnp.concatenate(blocks, axis=0))
    prefill_out = jnp.concatenate(outs, axis=1)[None]
    return prefill_out, decode_out


def solution(mesh):
    fine = Mesh(mesh.devices.reshape(2, 2, 4, 8, 4), ("section", "yh", "x", "z", "rep"))
    tp = ("yh", "x", "z")
    group = ("section", "rep")
    in_specs = (
        P(group, None, tp),
        P(group, tp, None),
        P(tp, None),
        P(),
        P(None, tp),
        P(None, tp),
        P("section", None),
        P("section", None),
        P(group, None, None),
        P(group, None, None),
    )
    out_specs = (P(group, None, tp), P(group, None, tp))
    return jax.shard_map(body, mesh=fine, in_specs=in_specs, out_specs=out_specs, check_vma=False)
```

```python
import math

import jax
import jax.numpy as jnp
from jax import lax
from jax.experimental import pallas as pl
from jax.experimental.pallas import tpu as pltpu
from jax.sharding import Mesh, PartitionSpec as P

KVL = 512
NOPE = 128
ROPE = 64
VD = 128
BLK = 128
NREQ = 3
STEPS = 4
REACH = 4
NREP = 4
NX = 4
HEADS = 2
PAD = 16

SIGMA = (1.0 + 0.1 * math.log(40.0)) ** 2 * (NOPE + ROPE) ** (-0.5)
bf16 = jnp.bfloat16
f32 = jnp.float32
i32 = jnp.int32
VMEM_LIMIT = 40 * 1024 * 1024


def cos_sin(positions):
    half = ROPE // 2
    frequency = 10000.0 ** (-jnp.arange(half, dtype=f32) * 2.0 / ROPE)
    angles = positions.astype(f32)[..., None] * frequency
    return jnp.cos(angles), jnp.sin(angles)


def rotate(u, cos_part, sin_part):
    half = ROPE // 2
    a, b = u[..., :half], u[..., half:]
    return jnp.concatenate([a * cos_part - b * sin_part, a * sin_part + b * cos_part], axis=-1)


def spread(a, axes, count):
    copies = jnp.broadcast_to(a[None], (count,) + a.shape)
    return lax.all_to_all(copies, axes, 0, 0, tiled=True)


def shift(count, d):
    return [(i, (i + d) % count) for i in range(count)]


def dot_t(a, b):
    return lax.dot_general(a, b, (((1,), (1,)), ((), ())), preferred_element_type=f32)


def norm_kernel(pieces_ref, gain_ref, cos_ref, sin_ref, out_ref):
    latent = jnp.sum(pieces_ref[...], axis=0)
    content = latent[:, :KVL]
    scale = lax.rsqrt(jnp.mean(content * content, axis=1, keepdims=True) + 1e-06)
    content = (content * scale * gain_ref[...]).astype(bf16)
    a = latent[:, KVL : KVL + ROPE // 2]
    b = latent[:, KVL + ROPE // 2 :]
    cos_part, sin_part = cos_ref[...], sin_ref[...]
    first, second = a * cos_part - b * sin_part, a * sin_part + b * cos_part
    pe = jnp.concatenate([first, second, first, second], axis=1).astype(bf16)
    for i in range(out_ref.shape[0]):
        out_ref[i, :, :KVL] = content
        out_ref[i, :, KVL:] = pe


def norm_rows(pieces, gain, cos_part, sin_part):
    count, chunk, _ = pieces.shape
    return pl.pallas_call(
        norm_kernel,
        out_shape=jax.ShapeDtypeStruct((count, chunk, KVL + 2 * ROPE), bf16),
        cost_estimate=pl.CostEstimate(flops=1_000_000, bytes_accessed=1_000_000, transcendentals=16),
        name="norm_rows",
    )(pieces, gain, cos_part, sin_part)


def query_kernel(cq_ref, w_ref, cos_ref, sin_ref, out_ref):
    rows = cq_ref[...].reshape(BLK, -1)
    u = jnp.dot(rows, w_ref[...], preferred_element_type=f32)
    pe = u[:, HEADS * NOPE :]
    lane = lax.broadcasted_iota(i32, pe.shape, 1)
    swapped = jnp.where(lane % ROPE < ROPE // 2, pltpu.roll(pe, 96, 1), pltpu.roll(pe, 32, 1))
    pe = pe * cos_ref[...] + swapped * sin_ref[...]
    for h in range(HEADS):
        out_ref[h, :, :NOPE] = u[:, h * NOPE : (h + 1) * NOPE].astype(bf16)
        out_ref[h, :, NOPE:] = jnp.where(lane // ROPE == h, pe, 0.0).astype(bf16)


def project_queries(cq, weights, cos_part, sin_part):
    width = cq.shape[-1]
    return pl.pallas_call(
        query_kernel,
        grid=(8,),
        in_specs=[
            pl.BlockSpec((8, 1, 16, width), lambda i: (0, i, 0, 0)),
            pl.BlockSpec(weights.shape, lambda i: (0, 0)),
            pl.BlockSpec((BLK, 2 * ROPE), lambda i: (i, 0)),
            pl.BlockSpec((BLK, 2 * ROPE), lambda i: (i, 0)),
        ],
        out_specs=pl.BlockSpec((HEADS, BLK, 2 * NOPE), lambda i: (0, i, 0)),
        out_shape=jax.ShapeDtypeStruct((HEADS, 8 * BLK, 2 * NOPE), bf16),
        compiler_params=pltpu.CompilerParams(vmem_limit_bytes=VMEM_LIMIT),
        cost_estimate=pl.CostEstimate(flops=1_200_000_000, bytes_accessed=5_000_000, transcendentals=0),
        name="project_queries",
    )(cq, weights, cos_part, sin_part)


def decode_kernel(lq_ref, pe_ref, cache_ref, new_ref, low_ref, high_ref, kv_ref, out_ref):
    latent = cache_ref[:, :KVL]
    new_latent = new_ref[:, :KVL]
    old = (dot_t(lq_ref[...], latent) + dot_t(pe_ref[...], cache_ref[:, KVL : KVL + ROPE])) * SIGMA
    new = (dot_t(lq_ref[...], new_latent) + dot_t(pe_ref[...], new_ref[:, KVL:])) * SIGMA
    column = lax.broadcasted_iota(i32, old.shape, 1)
    old = jnp.where((column >= low_ref[...]) & (column < high_ref[...]), old, -1e30)
    step = lax.broadcasted_iota(i32, new.shape, 0) % PAD
    other = lax.broadcasted_iota(i32, new.shape, 1)
    new = jnp.where((step // STEPS == other // STEPS) & (other <= step), new, -1e30)
    top = jnp.maximum(jnp.max(old, axis=1, keepdims=True), jnp.max(new, axis=1, keepdims=True))
    old = jnp.exp(old - top)
    new = jnp.exp(new - top)
    total = jnp.sum(old, axis=1, keepdims=True) + jnp.sum(new, axis=1, keepdims=True)
    old = (old / total).astype(bf16)
    new = (new / total).astype(bf16)
    mixture = (
        jnp.dot(old, latent, preferred_element_type=f32) + jnp.dot(new, new_latent, preferred_element_type=f32)
    ).astype(bf16)
    for h in range(HEADS):
        base = h * (NOPE + VD) + NOPE
        out_ref[:, h * VD : (h + 1) * VD] = jnp.dot(
            mixture[h * PAD : (h + 1) * PAD], kv_ref[:, base : base + VD], preferred_element_type=f32
        ).astype(bf16)


def decode(lq, pe, cache, new_keys, low, high, kv_up):
    return pl.pallas_call(
        decode_kernel,
        out_shape=jax.ShapeDtypeStruct((PAD, HEADS * VD), bf16),
        compiler_params=pltpu.CompilerParams(vmem_limit_bytes=VMEM_LIMIT),
        cost_estimate=pl.CostEstimate(flops=100_000_000, bytes_accessed=2_000_000, transcendentals=40_000),
        name="decode_attention",
    )(lq, pe, cache, new_keys, low, high, kv_up)


def prefill_kernel(start_ref, q_ref, cache_ref, kv_ref, out_ref, key_ref, value_ref):
    for j in range(8):
        rows = slice(j * BLK, (j + 1) * BLK)
        wide = jnp.dot(cache_ref[rows, :KVL], kv_ref[...], preferred_element_type=f32).astype(bf16)
        for h in range(HEADS):
            base = h * (NOPE + VD)
            key_ref[h, rows, :NOPE] = wide[:, base : base + NOPE]
            key_ref[h, rows, NOPE:] = cache_ref[rows, KVL:]
            value_ref[h, rows, :] = wide[:, base + NOPE : base + NOPE + VD]
    for i in range(8):
        first = max(0, i - REACH + 1) * BLK
        last = (i + 1) * BLK
        shape = (BLK, last - first)
        column = lax.broadcasted_iota(i32, shape, 1) + first
        row = lax.broadcasted_iota(i32, shape, 0) + i * BLK
        ok = (column >= start_ref[i]) & (column <= row)
        for h in range(HEADS):
            s = dot_t(q_ref[h, i * BLK : last, :], key_ref[h, first:last, :]) * SIGMA
            s = jnp.where(ok, s, -1e30)
            w = jnp.exp(s - jnp.max(s, axis=1, keepdims=True))
            w = (w / jnp.sum(w, axis=1, keepdims=True)).astype(bf16)
            out_ref[i * BLK : last, h * VD : (h + 1) * VD] = jnp.dot(
                w, value_ref[h, first:last, :], preferred_element_type=f32
            ).astype(bf16)


def prefill(block_starts, queries, cache, kv_up):
    rows = cache.shape[0]
    vmem = pl.BlockSpec(memory_space=pltpu.VMEM)
    return pl.pallas_call(
        prefill_kernel,
        in_specs=[pl.BlockSpec(memory_space=pltpu.SMEM), vmem, vmem, vmem],
        out_specs=vmem,
        out_shape=jax.ShapeDtypeStruct((rows, HEADS * VD), bf16),
        scratch_shapes=[
            pltpu.VMEM((HEADS, rows, 2 * NOPE), bf16),
            pltpu.VMEM((HEADS, rows, VD), bf16),
        ],
        compiler_params=pltpu.CompilerParams(vmem_limit_bytes=VMEM_LIMIT),
        cost_estimate=pl.CostEstimate(flops=1_500_000_000, bytes_accessed=4_000_000, transcendentals=1_000_000),
        name="prefill_attention",
    )(block_starts, queries, cache, kv_up)


def body(hidden, comp_query, kv_down, kv_gain, q_up, kv_up, req_blocks, dest_slot, dec_query, dec_latent):
    rep = lax.axis_index("rep")
    yh_index = lax.axis_index("yh")
    yz_index = lax.axis_index(("yh", "z"))
    x_index = lax.axis_index("x")
    block_x = hidden[0]
    rows, features = block_x.shape

    own = comp_query[0]
    other = lax.ppermute(own, "yh", shift(2, 1))
    per_x = rows // NX
    hidden_t = jnp.swapaxes(block_x.reshape(NX, per_x, features), 1, 2)
    packed = jnp.concatenate(
        [hidden_t, jnp.broadcast_to(kv_down[None], (NX,) + kv_down.shape)], axis=2
    )
    packed = lax.all_to_all(packed, "x", 0, 0, tiled=True)
    pair = jnp.where(yh_index == 0, jnp.stack([own, other]), jnp.stack([other, own]))
    line = jnp.zeros((2, NX) + own.shape, own.dtype)
    line = lax.dynamic_update_slice_in_dim(line, pair[:, None], x_index, 1)
    for d in range(1, NX):
        arrived = lax.ppermute(pair, "x", shift(NX, d))
        line = lax.dynamic_update_slice_in_dim(line, arrived[:, None], (x_index - d) % NX, 1)

    packed, dec_query, dec_latent = lax.optimization_barrier((packed, dec_query, dec_latent))
    packed = packed.reshape(NX * features, -1)
    partial = lax.dot_general(
        packed[:, :per_x], packed[:, per_x:], (((0,), (0,)), ((), ())), preferred_element_type=f32
    )
    cq = lax.all_gather(line.reshape(BLK, -1), "z", axis=0, tiled=True)

    lengths_all = req_blocks * BLK
    starts_all = jnp.cumsum(lengths_all, axis=-1) - lengths_all
    lengths = lax.dynamic_index_in_dim(lengths_all, rep, 0, keepdims=False)
    starts = lax.dynamic_index_in_dim(starts_all, rep, 0, keepdims=False)

    def start_of(row):
        inside = (row[:, None] >= starts[None]) & (row[:, None] < (starts + lengths)[None])
        return jnp.sum(jnp.where(inside, starts[None], 0), axis=1)

    chunk = per_x // 16
    pieces = lax.all_to_all(partial.reshape(16, chunk, -1), ("yh", "z"), 0, 0, tiled=True)
    own_rows = x_index * per_x + yz_index * chunk + jnp.arange(chunk, dtype=i32)
    cos_o, sin_o = cos_sin(own_rows - start_of(own_rows))
    copies = norm_rows(pieces, kv_gain[None, :], cos_o, sin_o)
    cache = lax.all_to_all(copies, ("yh", "z"), 0, 0, tiled=True).reshape(per_x, -1)
    cache = spread(cache, "x", NX).reshape(rows, -1)

    row_index = jnp.arange(rows, dtype=i32)
    cos_q, sin_q = cos_sin(row_index - start_of(row_index))
    by_head = q_up.reshape(-1, HEADS, NOPE + ROPE)
    nope_part = by_head[..., :NOPE].reshape(-1, HEADS * NOPE)
    rope_part = by_head[..., NOPE:].reshape(-1, HEADS * ROPE)
    queries = project_queries(
        cq.reshape(8, 8, 16, -1),
        jnp.concatenate([nope_part, rope_part], axis=1),
        jnp.concatenate([cos_q] * 4, axis=1),
        jnp.concatenate([-sin_q, sin_q] * 2, axis=1),
    )

    slots = lax.dynamic_slice_in_dim(dest_slot[0], rep * NREQ, NREQ, 0)
    rep_own = jnp.concatenate([dec_query, dec_latent], axis=2)
    rep_in = rep_own[None]
    for d in (1, 2):
        met = lax.ppermute(rep_in, "rep", [(i, i ^ d) for i in range(NREP)])
        upper = (rep // d) % 2 == 1
        rep_in = jnp.where(upper, jnp.concatenate([met, rep_in]), jnp.concatenate([rep_in, met]))
    rep_in = rep_in.reshape(NREP * NREQ, STEPS, -1)
    mine = jnp.take(rep_in, slots, axis=0, mode="clip").reshape(NREQ * STEPS, -1)
    mine = jnp.pad(mine, ((0, PAD - NREQ * STEPS), (0, 0)))
    my_query = mine[:, : dec_query.shape[2]]
    my_latent = mine[:, dec_query.shape[2] :]
    new_pos = jnp.pad((lengths[:, None] + jnp.arange(STEPS, dtype=i32)[None]).reshape(-1), (0, PAD - NREQ * STEPS))
    cos_d, sin_d = cos_sin(new_pos)
    new_keys = jnp.concatenate(
        [my_latent[:, :KVL], rotate(my_latent[:, KVL:].astype(f32), cos_d, sin_d).astype(bf16)], axis=1
    )
    dq = jnp.dot(my_query, q_up, preferred_element_type=f32).astype(bf16).reshape(PAD, HEADS, NOPE + ROPE)
    query_pe = rotate(dq[..., NOPE:].astype(f32), cos_d[:, None], sin_d[:, None]).astype(bf16)
    query_pe = jnp.swapaxes(query_pe, 0, 1).reshape(HEADS * PAD, ROPE)
    key_part = kv_up.reshape(KVL, HEADS, NOPE + VD)[..., :NOPE]
    latent_query = jnp.einsum("rhn,khn->hrk", dq[..., :NOPE], key_part, preferred_element_type=f32)
    latent_query = latent_query.astype(bf16).reshape(HEADS * PAD, KVL)
    span = (0, PAD - NREQ * STEPS)
    low = jnp.tile(jnp.pad(jnp.repeat(starts, STEPS), span), HEADS)[:, None]
    high = jnp.tile(jnp.pad(jnp.repeat(starts + lengths, STEPS), span), HEADS)[:, None]
    result = decode(latent_query, query_pe, cache, new_keys, low, high, kv_up)
    result = result[: NREQ * STEPS].reshape(NREQ, STEPS, HEADS * VD)
    pool = spread(result, "rep", NREP)
    block_starts = start_of(jnp.arange(rows // BLK, dtype=i32) * BLK)
    prefill_out = prefill(block_starts, queries, cache, kv_up)[None]
    pool, prefill_out = lax.optimization_barrier((pool, prefill_out))
    pool = pool.reshape(NREP * NREQ, STEPS, HEADS * VD)
    slot_numbers = rep * NREQ + jnp.arange(NREQ, dtype=i32)
    source = jnp.sum(
        jnp.where(dest_slot[0][None] == slot_numbers[:, None], jnp.arange(NREP * NREQ, dtype=i32)[None], 0),
        axis=1,
    )
    decode_out = jnp.take(pool, source, axis=0, mode="clip")
    return prefill_out, decode_out


def solution(mesh):
    fine = Mesh(mesh.devices.reshape(2, 2, 4, 8, 4), ("section", "yh", "x", "z", "rep"))
    tp = ("yh", "x", "z")
    group = ("section", "rep")
    in_specs = (
        P(group, None, tp),
        P(group, tp, None),
        P(tp, None),
        P(),
        P(None, tp),
        P(None, tp),
        P("section", None),
        P("section", None),
        P(group, None, None),
        P(group, None, None),
    )
    out_specs = (P(group, None, tp), P(group, None, tp))
    return jax.shard_map(body, mesh=fine, in_specs=in_specs, out_specs=out_specs, check_vma=False)
```

```python
import math

import jax
import jax.numpy as jnp
import numpy as np
from jax import lax
from jax.experimental import pallas as pl
from jax.experimental.pallas import tpu as pltpu
from jax.sharding import Mesh, PartitionSpec as P

KVL = 512
NOPE = 128
ROPE = 64
VD = 128
BLK = 128
NREQ = 3
STEPS = 4
REACH = 4
NREP = 4
NX = 4
HEADS = 2
PAD = 16
TABLE = 640
WIDE = KVL + 2 * ROPE
START, LENGTH, BASE, PLACE, FIRST, SOURCE, SLOT, BLOCK = 0, 3, 6, 8, 16, 24, 28, 32

SIGMA = (1.0 + 0.1 * math.log(40.0)) ** 2 * (NOPE + ROPE) ** (-0.5)
bf16 = jnp.bfloat16
f32 = jnp.float32
i32 = jnp.int32
VMEM_LIMIT = 40 * 1024 * 1024


def rotary_table():
    half = ROPE // 2
    frequency = np.float32(10000.0) ** (-np.arange(half, dtype=np.float32) * np.float32(2.0 / ROPE))
    angles = np.arange(TABLE, dtype=np.float32)[:, None] * frequency.astype(np.float32)
    cos_part, sin_part = np.cos(angles), np.sin(angles)
    return np.concatenate([cos_part] * 4, axis=1), np.concatenate([-sin_part, sin_part] * 2, axis=1)


def rotate(u, cos_part, sin_part):
    lane = lax.broadcasted_iota(i32, u.shape, 1)
    swapped = jnp.where(lane % ROPE < ROPE // 2, pltpu.roll(u, 96, 1), pltpu.roll(u, 32, 1))
    return u * cos_part + swapped * sin_part


def split_heads(u):
    a, b, c = u[:, :NOPE], u[:, NOPE : 2 * NOPE], u[:, 2 * NOPE :]
    low = lax.broadcasted_iota(i32, a.shape, 1) < ROPE
    return a, jnp.where(low, pltpu.roll(b, ROPE, 1), pltpu.roll(c, ROPE, 1)), jnp.where(low, b, c)


def spread(a, axes, count):
    copies = jnp.broadcast_to(a[None], (count,) + a.shape)
    return lax.all_to_all(copies, axes, 0, 0, tiled=True)


def shift(count, d):
    return [(i, (i + d) % count) for i in range(count)]


def dot_t(a, b):
    return lax.dot_general(a, b, (((1,), (1,)), ((), ())), preferred_element_type=f32)


def layout_kernel(ids_ref, req_ref, slot_ref, out_ref):
    rep, x, yh, yz = ids_ref[0], ids_ref[1], ids_ref[2], ids_ref[3]
    lengths = [req_ref[rep, r] for r in range(NREQ)]
    starts = [0, lengths[0], lengths[0] + lengths[1]]

    def start_of(block):
        return jnp.where(block >= starts[2], starts[2], jnp.where(block >= starts[1], starts[1], 0))

    for r in range(NREQ):
        out_ref[START + r] = starts[r] * BLK
        out_ref[LENGTH + r] = lengths[r] * BLK
        slot = slot_ref[0, rep * NREQ + r]
        out_ref[SLOT + r] = (lax.div(slot, NREQ) ^ rep) * NREQ + lax.rem(slot, NREQ)
        source = 0
        for m in range(NREP * NREQ):
            source += jnp.where(slot_ref[0, m] == rep * NREQ + r, m, 0)
        out_ref[SOURCE + r] = lax.div(source, NREQ) * PAD + lax.rem(source, NREQ) * STEPS
    out_ref[BASE] = x * 2 * BLK + yz * PAD - start_of(x * 2 + lax.div(yz, 8)) * BLK
    for i in range(8):
        out_ref[PLACE + i] = i - start_of(i)
        out_ref[FIRST + i] = start_of(i) * BLK
        out_ref[BLOCK + i] = lax.rem(x + NX - i % NX, NX) * 2 + (yh ^ (i // NX))


SMEM = pl.BlockSpec(memory_space=pltpu.SMEM)
VMEM = pl.BlockSpec(memory_space=pltpu.VMEM)


def request_layout(ids, req_blocks, dest_slot):
    return pl.pallas_call(
        layout_kernel,
        in_specs=[SMEM] * 3,
        out_specs=SMEM,
        out_shape=jax.ShapeDtypeStruct((64,), i32),
        cost_estimate=pl.CostEstimate(flops=1000, bytes_accessed=1000, transcendentals=0),
        name="request_layout",
    )(ids, req_blocks, dest_slot)


def pack_kernel(hidden_ref, down_ref, out_ref):
    features = hidden_ref.shape[1]
    per_x = hidden_ref.shape[0] // NX
    row = lax.broadcasted_iota(i32, (features, features), 0)
    column = lax.broadcasted_iota(i32, (features, features), 1)
    unit = jnp.where(row == column, 1.0, 0.0).astype(bf16)
    for i in range(NX):
        out_ref[i, :, :per_x] = dot_t(unit, hidden_ref[i * per_x : (i + 1) * per_x, :]).astype(bf16)
        out_ref[i, :, per_x:] = down_ref[...]


def pack(hidden, kv_down):
    rows, features = hidden.shape
    return pl.pallas_call(
        pack_kernel,
        in_specs=[VMEM] * 2,
        out_specs=VMEM,
        out_shape=jax.ShapeDtypeStruct((NX, features, rows // NX + kv_down.shape[1]), bf16),
        cost_estimate=pl.CostEstimate(flops=26_000_000, bytes_accessed=1_200_000, transcendentals=0),
        name="pack_hidden",
    )(hidden, kv_down)


def norm_kernel(layout_ref, pieces_ref, gain_ref, cos_ref, sin_ref, out_ref):
    latent = jnp.sum(pieces_ref[...].astype(f32), axis=0)
    content = latent[:, :KVL]
    scale = lax.rsqrt(jnp.mean(content * content, axis=1, keepdims=True) + 1e-06)
    content = (content * scale * gain_ref[...]).astype(bf16)
    at = pl.ds(pl.multiple_of(layout_ref[BASE], PAD), PAD)
    pe = jnp.concatenate([latent[:, KVL:]] * 2, axis=1)
    pe = rotate(pe, cos_ref[at, :], sin_ref[at, :]).astype(bf16)
    for i in range(out_ref.shape[0]):
        out_ref[i, :, :KVL] = content
        out_ref[i, :, KVL:] = pe


def norm_rows(layout, pieces, gain, cos_part, sin_part):
    count, chunk, _ = pieces.shape
    return pl.pallas_call(
        norm_kernel,
        in_specs=[SMEM] + [VMEM] * 4,
        out_specs=VMEM,
        out_shape=jax.ShapeDtypeStruct((count, chunk, WIDE), bf16),
        cost_estimate=pl.CostEstimate(flops=1_000_000, bytes_accessed=1_000_000, transcendentals=16),
        name="norm_rows",
    )(layout, pieces, gain, cos_part, sin_part)


def query_kernel(layout_ref, cq_ref, w_ref, cos_ref, sin_ref, out_ref):
    rows = cq_ref[...].reshape(BLK, -1)
    u = jnp.dot(rows, w_ref[...], preferred_element_type=f32)
    first, second, pe = split_heads(u)
    pe = rotate(pe, cos_ref[...], sin_ref[...])
    low = lax.broadcasted_iota(i32, pe.shape, 1) < ROPE
    out_ref[0, :, :NOPE] = first.astype(bf16)
    out_ref[0, :, NOPE:] = jnp.where(low, pe, 0.0).astype(bf16)
    out_ref[1, :, :NOPE] = second.astype(bf16)
    out_ref[1, :, NOPE:] = jnp.where(low, 0.0, pe).astype(bf16)


def project_queries(layout, cq, weights, cos_part, sin_part):
    width = cq.shape[-1]
    table = pl.BlockSpec((BLK, 2 * ROPE), lambda i, place: (place[PLACE + i], 0))
    return pl.pallas_call(
        query_kernel,
        grid_spec=pltpu.PrefetchScalarGridSpec(
            num_scalar_prefetch=1,
            grid=(8,),
            in_specs=[
                pl.BlockSpec((8, 1, PAD, width), lambda i, place: (0, place[BLOCK + i], 0, 0)),
                pl.BlockSpec(weights.shape, lambda i, place: (0, 0)),
                table,
                table,
            ],
            out_specs=pl.BlockSpec((HEADS, BLK, 2 * NOPE), lambda i, place: (0, i, 0)),
        ),
        out_shape=jax.ShapeDtypeStruct((HEADS, 8 * BLK, 2 * NOPE), bf16),
        compiler_params=pltpu.CompilerParams(vmem_limit_bytes=VMEM_LIMIT),
        cost_estimate=pl.CostEstimate(flops=1_200_000_000, bytes_accessed=5_000_000, transcendentals=0),
        name="project_queries",
    )(layout, cq, weights, cos_part, sin_part)


def prepare_kernel(layout_ref, rows_ref, w_ref, kv_ref, cos_ref, sin_ref, out_ref, in_ref, cos_at, sin_at):
    query_latent = w_ref.shape[0]
    in_ref[...] = jnp.zeros_like(in_ref)
    cos_at[...] = jnp.zeros_like(cos_at)
    sin_at[...] = jnp.zeros_like(sin_at)
    for r in range(NREQ):
        here = slice(r * STEPS, (r + 1) * STEPS)
        in_ref[here, :] = rows_ref[layout_ref[SLOT + r]].astype(f32)
        at = pl.ds(pl.multiple_of(layout_ref[LENGTH + r], BLK), 8)
        cos_at[here, :] = cos_ref[at, :][:STEPS]
        sin_at[here, :] = sin_ref[at, :][:STEPS]
    cos_part, sin_part = cos_at[...], sin_at[...]
    rows = in_ref[:, :query_latent].astype(bf16)
    u = jnp.dot(rows, w_ref[...], preferred_element_type=f32).astype(bf16).astype(f32)
    first, second, pe = split_heads(u)
    pe = rotate(pe, cos_part, sin_part)
    low = lax.broadcasted_iota(i32, pe.shape, 1) < ROPE
    for h, plain in enumerate((first, second)):
        here = slice(h * PAD, (h + 1) * PAD)
        base = h * (NOPE + VD)
        out_ref[here, :KVL] = dot_t(plain.astype(bf16), kv_ref[:, base : base + NOPE]).astype(bf16)
        out_ref[here, KVL:] = jnp.where(low == (h == 0), pe, 0.0).astype(bf16)
    new = slice(HEADS * PAD, (HEADS + 1) * PAD)
    out_ref[new, :KVL] = in_ref[:, query_latent : query_latent + KVL].astype(bf16)
    new_pe = jnp.concatenate([in_ref[:, query_latent + KVL :]] * 2, axis=1)
    out_ref[new, KVL:] = rotate(new_pe, cos_part, sin_part).astype(bf16)


def prepare_decode(layout, rows, q_up, kv_up, cos_part, sin_part):
    return pl.pallas_call(
        prepare_kernel,
        in_specs=[SMEM] + [VMEM] * 5,
        out_specs=VMEM,
        out_shape=jax.ShapeDtypeStruct(((HEADS + 1) * PAD, WIDE), bf16),
        scratch_shapes=[
            pltpu.VMEM((PAD, rows.shape[-1]), f32),
            pltpu.VMEM((PAD, 2 * ROPE), f32),
            pltpu.VMEM((PAD, 2 * ROPE), f32),
        ],
        compiler_params=pltpu.CompilerParams(vmem_limit_bytes=VMEM_LIMIT),
        cost_estimate=pl.CostEstimate(flops=30_000_000, bytes_accessed=2_500_000, transcendentals=0),
        name="prepare_decode",
    )(layout, rows, q_up, kv_up, cos_part, sin_part)


def decode_kernel(layout_ref, ready_ref, cache_ref, kv_ref, out_ref):
    query = ready_ref[: HEADS * PAD, :]
    fresh = ready_ref[HEADS * PAD :, :]
    old = dot_t(query, cache_ref[...]) * SIGMA
    new = dot_t(query, fresh) * SIGMA
    request = lax.broadcasted_iota(i32, (HEADS * PAD, 1), 0) % PAD // STEPS

    def per_request(values):
        return jnp.where(request == 0, values[0], jnp.where(request == 1, values[1], values[2]))

    low = per_request([layout_ref[START + r] for r in range(NREQ)])
    high = per_request([layout_ref[START + r] + layout_ref[LENGTH + r] for r in range(NREQ)])
    column = lax.broadcasted_iota(i32, old.shape, 1)
    old = jnp.where((column >= low) & (column < high), old, -1e30)
    step = lax.broadcasted_iota(i32, new.shape, 0) % PAD
    other = lax.broadcasted_iota(i32, new.shape, 1)
    new = jnp.where((step // STEPS == other // STEPS) & (other <= step), new, -1e30)
    top = jnp.maximum(jnp.max(old, axis=1, keepdims=True), jnp.max(new, axis=1, keepdims=True))
    old = jnp.exp(old - top)
    new = jnp.exp(new - top)
    inverse = 1.0 / (jnp.sum(old, axis=1, keepdims=True) + jnp.sum(new, axis=1, keepdims=True))
    old = (old * inverse).astype(bf16)
    new = (new * inverse).astype(bf16)
    mixture = (
        jnp.dot(old, cache_ref[:, :KVL], preferred_element_type=f32)
        + jnp.dot(new, fresh[:, :KVL], preferred_element_type=f32)
    ).astype(bf16)
    for h in range(HEADS):
        base = h * (NOPE + VD) + NOPE
        value = jnp.dot(
            mixture[h * PAD : (h + 1) * PAD], kv_ref[:, base : base + VD], preferred_element_type=f32
        ).astype(bf16)
        for i in range(NREP):
            out_ref[i, :, h * VD : (h + 1) * VD] = value


def decode(layout, ready, cache, kv_up):
    return pl.pallas_call(
        decode_kernel,
        in_specs=[SMEM] + [VMEM] * 3,
        out_specs=VMEM,
        out_shape=jax.ShapeDtypeStruct((NREP, PAD, HEADS * VD), bf16),
        compiler_params=pltpu.CompilerParams(vmem_limit_bytes=VMEM_LIMIT),
        cost_estimate=pl.CostEstimate(flops=100_000_000, bytes_accessed=2_000_000, transcendentals=40_000),
        name="decode_attention",
    )(layout, ready, cache, kv_up)


def select_kernel(layout_ref, pool_ref, out_ref):
    pool = pool_ref[...].reshape(NREP * PAD, -1)
    for r in range(NREQ):
        row = lax.broadcasted_iota(i32, (8, NREP * PAD), 0)
        column = lax.broadcasted_iota(i32, (8, NREP * PAD), 1)
        pick = jnp.where(column == layout_ref[SOURCE + r] + row, 1.0, 0.0).astype(bf16)
        out_ref[r] = jnp.dot(pick, pool, preferred_element_type=f32)[:STEPS].astype(bf16)


def select(layout, pool):
    return pl.pallas_call(
        select_kernel,
        in_specs=[SMEM, VMEM],
        out_specs=VMEM,
        out_shape=jax.ShapeDtypeStruct((NREQ, STEPS, HEADS * VD), bf16),
        cost_estimate=pl.CostEstimate(flops=1_000_000, bytes_accessed=50_000, transcendentals=0),
        name="select_slots",
    )(layout, pool)


def prefill_kernel(layout_ref, q_ref, cache_ref, kv_ref, out_ref, key_ref, value_ref):
    for j in range(4):
        rows = slice(j * 2 * BLK, (j + 1) * 2 * BLK)
        wide = jnp.dot(cache_ref[rows, :KVL], kv_ref[...], preferred_element_type=f32).astype(bf16)
        for h in range(HEADS):
            base = h * (NOPE + VD)
            key_ref[h, rows, :NOPE] = wide[:, base : base + NOPE]
            key_ref[h, rows, NOPE:] = cache_ref[rows, KVL:]
            value_ref[h, rows, :] = wide[:, base + NOPE : base + NOPE + VD]
    for i in range(8):
        first = max(0, i - REACH + 1) * BLK
        last = (i + 1) * BLK
        shape = (BLK, last - first)
        column = lax.broadcasted_iota(i32, shape, 1) + first
        row = lax.broadcasted_iota(i32, shape, 0) + i * BLK
        ok = (column >= layout_ref[FIRST + i]) & (column <= row)
        scores = [
            dot_t(q_ref[h, i * BLK : last, :], key_ref[h, first:last, :]) * SIGMA for h in range(HEADS)
        ]
        scores = [jnp.where(ok, s, -1e30) for s in scores]
        weights = [jnp.exp(s - jnp.max(s, axis=1, keepdims=True)) for s in scores]
        weights = [(w * (1.0 / jnp.sum(w, axis=1, keepdims=True))).astype(bf16) for w in weights]
        for h in range(HEADS):
            out_ref[i * BLK : last, h * VD : (h + 1) * VD] = jnp.dot(
                weights[h], value_ref[h, first:last, :], preferred_element_type=f32
            ).astype(bf16)


def prefill(layout, queries, cache, kv_up):
    rows = cache.shape[0]
    return pl.pallas_call(
        prefill_kernel,
        in_specs=[SMEM] + [VMEM] * 3,
        out_specs=VMEM,
        out_shape=jax.ShapeDtypeStruct((rows, HEADS * VD), bf16),
        scratch_shapes=[
            pltpu.VMEM((HEADS, rows, 2 * NOPE), bf16),
            pltpu.VMEM((HEADS, rows, VD), bf16),
        ],
        compiler_params=pltpu.CompilerParams(vmem_limit_bytes=VMEM_LIMIT),
        cost_estimate=pl.CostEstimate(flops=1_500_000_000, bytes_accessed=4_000_000, transcendentals=1_000_000),
        name="prefill_attention",
    )(layout, queries, cache, kv_up)


def body(hidden, comp_query, kv_down, kv_gain, q_up, kv_up, req_blocks, dest_slot, dec_query, dec_latent):
    ids = jnp.stack(
        [lax.axis_index("rep"), lax.axis_index("x"), lax.axis_index("yh"), lax.axis_index(("yh", "z"))]
    ).astype(i32)
    rows, features = hidden.shape[1:]
    per_x = rows // NX
    chunk = per_x // 16
    cos_part, sin_part = rotary_table()

    own = comp_query[0]
    other = lax.ppermute(own, "yh", shift(2, 1))
    packed = lax.all_to_all(pack(hidden[0], kv_down), "x", 0, 0, tiled=True)
    layout = request_layout(ids, req_blocks, dest_slot)
    pair = jnp.stack([own, other])
    line = [pair] + [lax.ppermute(pair, "x", shift(NX, d)) for d in range(1, NX)]
    cq = lax.all_gather(jnp.concatenate(line).reshape(BLK, -1), "z", axis=0, tiled=True)

    packed, dec_query, dec_latent = lax.optimization_barrier((packed, dec_query, dec_latent))
    packed = packed.reshape(NX * features, -1)
    partial = lax.dot_general(
        packed[:, :per_x], packed[:, per_x:], (((0,), (0,)), ((), ())), preferred_element_type=f32
    )
    pieces = lax.all_to_all(partial.reshape(16, chunk, -1), ("yh", "z"), 0, 0, tiled=True)
    copies = norm_rows(layout, pieces, kv_gain[None, :], cos_part, sin_part)
    cache = lax.all_to_all(copies, ("yh", "z"), 0, 0, tiled=True).reshape(per_x, -1)
    cache = spread(cache, "x", NX).reshape(rows, -1)

    rep_in = jnp.concatenate([dec_query, dec_latent], axis=2)
    for d in (1, 2):
        met = lax.ppermute(rep_in, "rep", [(i, i ^ d) for i in range(NREP)])
        rep_in = jnp.concatenate([rep_in, met])
    ready = prepare_decode(layout, rep_in, q_up, kv_up, cos_part, sin_part)

    queries = project_queries(layout, cq.reshape(8, 8, PAD, -1), q_up, cos_part, sin_part)
    cache, queries, ready = lax.optimization_barrier((cache, queries, ready))
    result = decode(layout, ready, cache, kv_up)
    pool = lax.all_to_all(result, "rep", 0, 0, tiled=True)
    prefill_out = prefill(layout, queries, cache, kv_up)[None]
    pool, prefill_out = lax.optimization_barrier((pool, prefill_out))
    return prefill_out, select(layout, pool)


def solution(mesh):
    fine = Mesh(mesh.devices.reshape(2, 2, 4, 8, 4), ("section", "yh", "x", "z", "rep"))
    tp = ("yh", "x", "z")
    group = ("section", "rep")
    in_specs = (
        P(group, None, tp),
        P(group, tp, None),
        P(tp, None),
        P(),
        P(None, tp),
        P(None, tp),
        P("section", None),
        P("section", None),
        P(group, None, None),
        P(group, None, None),
    )
    out_specs = (P(group, None, tp), P(group, None, tp))
    return jax.shard_map(body, mesh=fine, in_specs=in_specs, out_specs=out_specs, check_vma=False)
```

```python
import math

import jax
import jax.numpy as jnp
import numpy as np
from jax import lax
from jax.experimental import pallas as pl
from jax.experimental.pallas import tpu as pltpu
from jax.sharding import Mesh, PartitionSpec as P

KVL = 512
NOPE = 128
ROPE = 64
VD = 128
BLK = 128
NREQ = 3
STEPS = 4
REACH = 4
NREP = 4
NX = 4
HEADS = 2
PAD = 16
TABLE = 640
NORM_FLOPS = 1_000_000
WIDE = KVL + 2 * ROPE
START, LENGTH, BASE, PLACE, FIRST, SOURCE, SLOT, BLOCK = 0, 3, 6, 8, 16, 24, 28, 32

SIGMA = (1.0 + 0.1 * math.log(40.0)) ** 2 * (NOPE + ROPE) ** (-0.5)
bf16 = jnp.bfloat16
f32 = jnp.float32
i32 = jnp.int32
VMEM_LIMIT = 40 * 1024 * 1024


def rotary_table():
    half = ROPE // 2
    frequency = np.float32(10000.0) ** (-np.arange(half, dtype=np.float32) * np.float32(2.0 / ROPE))
    angles = np.arange(TABLE, dtype=np.float32)[:, None] * frequency.astype(np.float32)
    cos_part, sin_part = np.cos(angles), np.sin(angles)
    return np.concatenate([cos_part] * 4, axis=1), np.concatenate([-sin_part, sin_part] * 2, axis=1)


def rotate(u, cos_part, sin_part):
    lane = lax.broadcasted_iota(i32, u.shape, 1)
    swapped = jnp.where(lane % ROPE < ROPE // 2, pltpu.roll(u, 96, 1), pltpu.roll(u, 32, 1))
    return u * cos_part + swapped * sin_part


def split_heads(u):
    a, b, c = u[:, :NOPE], u[:, NOPE : 2 * NOPE], u[:, 2 * NOPE :]
    low = lax.broadcasted_iota(i32, a.shape, 1) < ROPE
    return a, jnp.where(low, pltpu.roll(b, ROPE, 1), pltpu.roll(c, ROPE, 1)), jnp.where(low, b, c)


def spread(a, axes, count):
    copies = jnp.broadcast_to(a[None], (count,) + a.shape)
    return lax.all_to_all(copies, axes, 0, 0, tiled=True)


def shift(count, d):
    return [(i, (i + d) % count) for i in range(count)]


def dot_t(a, b):
    return lax.dot_general(a, b, (((1,), (1,)), ((), ())), preferred_element_type=f32)


def layout_kernel(ids_ref, req_ref, slot_ref, out_ref):
    rep, x, yh, z = ids_ref[0], ids_ref[1], ids_ref[2], ids_ref[3]
    lengths = [req_ref[rep, r] for r in range(NREQ)]
    starts = [0, lengths[0], lengths[0] + lengths[1]]

    def start_of(block):
        return jnp.where(block >= starts[2], starts[2], jnp.where(block >= starts[1], starts[1], 0))

    for r in range(NREQ):
        out_ref[START + r] = starts[r] * BLK
        out_ref[LENGTH + r] = lengths[r] * BLK
        slot = slot_ref[0, rep * NREQ + r]
        out_ref[SLOT + r] = (lax.div(slot, NREQ) ^ rep) * NREQ + lax.rem(slot, NREQ)
        source = 0
        for m in range(NREP * NREQ):
            source += jnp.where(slot_ref[0, m] == rep * NREQ + r, m, 0)
        out_ref[SOURCE + r] = lax.div(source, NREQ) * PAD + lax.rem(source, NREQ) * STEPS
    out_ref[BASE] = x * 2 * BLK + z * 2 * PAD - start_of(x * 2 + lax.div(z, 4)) * BLK
    for i in range(8):
        out_ref[PLACE + i] = i - start_of(i)
        out_ref[FIRST + i] = start_of(i) * BLK
        out_ref[BLOCK + i] = lax.rem(x + NX - i % NX, NX) * 2 + (yh ^ (i // NX))


SMEM = pl.BlockSpec(memory_space=pltpu.SMEM)
VMEM = pl.BlockSpec(memory_space=pltpu.VMEM)


def request_layout(ids, req_blocks, dest_slot):
    return pl.pallas_call(
        layout_kernel,
        in_specs=[SMEM] * 3,
        out_specs=SMEM,
        out_shape=jax.ShapeDtypeStruct((64,), i32),
        cost_estimate=pl.CostEstimate(flops=1000, bytes_accessed=1000, transcendentals=0),
        name="request_layout",
    )(ids, req_blocks, dest_slot)


def pack_kernel(hidden_ref, down_ref, out_ref):
    features = hidden_ref.shape[1]
    per_x = hidden_ref.shape[0] // NX
    row = lax.broadcasted_iota(i32, (features, features), 0)
    column = lax.broadcasted_iota(i32, (features, features), 1)
    unit = jnp.where(row == column, 1.0, 0.0).astype(bf16)
    for i in range(NX):
        out_ref[i, :, :per_x] = dot_t(unit, hidden_ref[i * per_x : (i + 1) * per_x, :]).astype(bf16)
        out_ref[i, :, per_x:] = down_ref[...]


def pack(hidden, kv_down):
    rows, features = hidden.shape
    return pl.pallas_call(
        pack_kernel,
        in_specs=[VMEM] * 2,
        out_specs=VMEM,
        out_shape=jax.ShapeDtypeStruct((NX, features, rows // NX + kv_down.shape[1]), bf16),
        cost_estimate=pl.CostEstimate(flops=26_000_000, bytes_accessed=1_200_000, transcendentals=0),
        name="pack_hidden",
    )(hidden, kv_down)


def norm_kernel(layout_ref, own_ref, other_ref, gain_ref, cos_ref, sin_ref, out_ref):
    latent = own_ref[...] + other_ref[...]
    content = latent[:, :KVL]
    scale = lax.rsqrt(jnp.mean(content * content, axis=1, keepdims=True) + 1e-06)
    content = (content * scale * gain_ref[...]).astype(bf16)
    at = pl.ds(pl.multiple_of(layout_ref[BASE], PAD), latent.shape[0])
    pe = jnp.concatenate([latent[:, KVL:]] * 2, axis=1)
    pe = rotate(pe, cos_ref[at, :], sin_ref[at, :]).astype(bf16)
    for i in range(out_ref.shape[0]):
        out_ref[i, :, :KVL] = content
        out_ref[i, :, KVL:] = pe


def norm_rows(layout, own, other, gain, cos_part, sin_part):
    count, chunk = 8, own.shape[0]
    return pl.pallas_call(
        norm_kernel,
        in_specs=[SMEM] + [VMEM] * 5,
        out_specs=VMEM,
        out_shape=jax.ShapeDtypeStruct((count, chunk, WIDE), bf16),
        cost_estimate=pl.CostEstimate(flops=NORM_FLOPS, bytes_accessed=1_000_000, transcendentals=16),
        name="norm_rows",
    )(layout, own, other, gain, cos_part, sin_part)


def query_kernel(layout_ref, cq_ref, w_ref, cos_ref, sin_ref, out_ref):
    rows = cq_ref[...].reshape(BLK, -1)
    u = jnp.dot(rows, w_ref[...], preferred_element_type=f32)
    first, second, pe = split_heads(u)
    pe = rotate(pe, cos_ref[...], sin_ref[...])
    low = lax.broadcasted_iota(i32, pe.shape, 1) < ROPE
    out_ref[0, :, :NOPE] = first.astype(bf16)
    out_ref[0, :, NOPE:] = jnp.where(low, pe, 0.0).astype(bf16)
    out_ref[1, :, :NOPE] = second.astype(bf16)
    out_ref[1, :, NOPE:] = jnp.where(low, 0.0, pe).astype(bf16)


def project_queries(layout, cq, weights, cos_part, sin_part):
    width = cq.shape[-1]
    table = pl.BlockSpec((BLK, 2 * ROPE), lambda i, place: (place[PLACE + i], 0))
    return pl.pallas_call(
        query_kernel,
        grid_spec=pltpu.PrefetchScalarGridSpec(
            num_scalar_prefetch=1,
            grid=(8,),
            in_specs=[
                pl.BlockSpec((8, 1, PAD, width), lambda i, place: (0, place[BLOCK + i], 0, 0)),
                pl.BlockSpec(weights.shape, lambda i, place: (0, 0)),
                table,
                table,
            ],
            out_specs=pl.BlockSpec((HEADS, BLK, 2 * NOPE), lambda i, place: (0, i, 0)),
        ),
        out_shape=jax.ShapeDtypeStruct((HEADS, 8 * BLK, 2 * NOPE), bf16),
        compiler_params=pltpu.CompilerParams(vmem_limit_bytes=VMEM_LIMIT),
        cost_estimate=pl.CostEstimate(flops=1_200_000_000, bytes_accessed=5_000_000, transcendentals=0),
        name="project_queries",
    )(layout, cq, weights, cos_part, sin_part)


def prepare_kernel(layout_ref, rows_ref, w_ref, kv_ref, cos_ref, sin_ref, out_ref, in_ref, cos_at, sin_at):
    query_latent = w_ref.shape[0]
    in_ref[...] = jnp.zeros_like(in_ref)
    cos_at[...] = jnp.zeros_like(cos_at)
    sin_at[...] = jnp.zeros_like(sin_at)
    for r in range(NREQ):
        here = slice(r * STEPS, (r + 1) * STEPS)
        in_ref[here, :] = rows_ref[layout_ref[SLOT + r]].astype(f32)
        at = pl.ds(pl.multiple_of(layout_ref[LENGTH + r], BLK), 8)
        cos_at[here, :] = cos_ref[at, :][:STEPS]
        sin_at[here, :] = sin_ref[at, :][:STEPS]
    cos_part, sin_part = cos_at[...], sin_at[...]
    rows = in_ref[:, :query_latent].astype(bf16)
    u = jnp.dot(rows, w_ref[...], preferred_element_type=f32).astype(bf16).astype(f32)
    first, second, pe = split_heads(u)
    pe = rotate(pe, cos_part, sin_part)
    low = lax.broadcasted_iota(i32, pe.shape, 1) < ROPE
    for h, plain in enumerate((first, second)):
        here = slice(h * PAD, (h + 1) * PAD)
        base = h * (NOPE + VD)
        out_ref[here, :KVL] = dot_t(plain.astype(bf16), kv_ref[:, base : base + NOPE]).astype(bf16)
        out_ref[here, KVL:] = jnp.where(low == (h == 0), pe, 0.0).astype(bf16)
    new = slice(HEADS * PAD, (HEADS + 1) * PAD)
    out_ref[new, :KVL] = in_ref[:, query_latent : query_latent + KVL].astype(bf16)
    new_pe = jnp.concatenate([in_ref[:, query_latent + KVL :]] * 2, axis=1)
    out_ref[new, KVL:] = rotate(new_pe, cos_part, sin_part).astype(bf16)


def prepare_decode(layout, rows, q_up, kv_up, cos_part, sin_part):
    return pl.pallas_call(
        prepare_kernel,
        in_specs=[SMEM] + [VMEM] * 5,
        out_specs=VMEM,
        out_shape=jax.ShapeDtypeStruct(((HEADS + 1) * PAD, WIDE), bf16),
        scratch_shapes=[
            pltpu.VMEM((PAD, rows.shape[-1]), f32),
            pltpu.VMEM((PAD, 2 * ROPE), f32),
            pltpu.VMEM((PAD, 2 * ROPE), f32),
        ],
        compiler_params=pltpu.CompilerParams(vmem_limit_bytes=VMEM_LIMIT),
        cost_estimate=pl.CostEstimate(flops=30_000_000, bytes_accessed=2_500_000, transcendentals=0),
        name="prepare_decode",
    )(layout, rows, q_up, kv_up, cos_part, sin_part)


def decode_kernel(layout_ref, ready_ref, cache_ref, kv_ref, out_ref):
    query = ready_ref[: HEADS * PAD, :]
    fresh = ready_ref[HEADS * PAD :, :]
    old = dot_t(query, cache_ref[...]) * SIGMA
    new = dot_t(query, fresh) * SIGMA
    request = lax.broadcasted_iota(i32, (HEADS * PAD, 1), 0) % PAD // STEPS

    def per_request(values):
        return jnp.where(request == 0, values[0], jnp.where(request == 1, values[1], values[2]))

    low = per_request([layout_ref[START + r] for r in range(NREQ)])
    high = per_request([layout_ref[START + r] + layout_ref[LENGTH + r] for r in range(NREQ)])
    column = lax.broadcasted_iota(i32, old.shape, 1)
    old = jnp.where((column >= low) & (column < high), old, -1e30)
    step = lax.broadcasted_iota(i32, new.shape, 0) % PAD
    other = lax.broadcasted_iota(i32, new.shape, 1)
    new = jnp.where((step // STEPS == other // STEPS) & (other <= step), new, -1e30)
    top = jnp.maximum(jnp.max(old, axis=1, keepdims=True), jnp.max(new, axis=1, keepdims=True))
    old = jnp.exp(old - top)
    new = jnp.exp(new - top)
    inverse = 1.0 / (jnp.sum(old, axis=1, keepdims=True) + jnp.sum(new, axis=1, keepdims=True))
    old = (old * inverse).astype(bf16)
    new = (new * inverse).astype(bf16)
    mixture = (
        jnp.dot(old, cache_ref[:, :KVL], preferred_element_type=f32)
        + jnp.dot(new, fresh[:, :KVL], preferred_element_type=f32)
    ).astype(bf16)
    for h in range(HEADS):
        base = h * (NOPE + VD) + NOPE
        value = jnp.dot(
            mixture[h * PAD : (h + 1) * PAD], kv_ref[:, base : base + VD], preferred_element_type=f32
        ).astype(bf16)
        for i in range(NREP):
            out_ref[i, :, h * VD : (h + 1) * VD] = value


def decode(layout, ready, cache, kv_up):
    return pl.pallas_call(
        decode_kernel,
        in_specs=[SMEM] + [VMEM] * 3,
        out_specs=VMEM,
        out_shape=jax.ShapeDtypeStruct((NREP, PAD, HEADS * VD), bf16),
        compiler_params=pltpu.CompilerParams(vmem_limit_bytes=VMEM_LIMIT),
        cost_estimate=pl.CostEstimate(flops=100_000_000, bytes_accessed=2_000_000, transcendentals=40_000),
        name="decode_attention",
    )(layout, ready, cache, kv_up)


def select_kernel(layout_ref, pool_ref, out_ref):
    pool = pool_ref[...].reshape(NREP * PAD, -1)
    for r in range(NREQ):
        row = lax.broadcasted_iota(i32, (8, NREP * PAD), 0)
        column = lax.broadcasted_iota(i32, (8, NREP * PAD), 1)
        pick = jnp.where(column == layout_ref[SOURCE + r] + row, 1.0, 0.0).astype(bf16)
        out_ref[r] = jnp.dot(pick, pool, preferred_element_type=f32)[:STEPS].astype(bf16)


def select(layout, pool):
    return pl.pallas_call(
        select_kernel,
        in_specs=[SMEM, VMEM],
        out_specs=VMEM,
        out_shape=jax.ShapeDtypeStruct((NREQ, STEPS, HEADS * VD), bf16),
        cost_estimate=pl.CostEstimate(flops=1_000_000, bytes_accessed=50_000, transcendentals=0),
        name="select_slots",
    )(layout, pool)


def prefill_kernel(layout_ref, q_ref, cache_ref, kv_ref, out_ref, key_ref, value_ref):
    for j in range(4):
        rows = slice(j * 2 * BLK, (j + 1) * 2 * BLK)
        wide = jnp.dot(cache_ref[rows, :KVL], kv_ref[...], preferred_element_type=f32).astype(bf16)
        for h in range(HEADS):
            base = h * (NOPE + VD)
            key_ref[h, rows, :NOPE] = wide[:, base : base + NOPE]
            key_ref[h, rows, NOPE:] = cache_ref[rows, KVL:]
            value_ref[h, rows, :] = wide[:, base + NOPE : base + NOPE + VD]
    for i in range(8):
        first = max(0, i - REACH + 1) * BLK
        last = (i + 1) * BLK
        shape = (BLK, last - first)
        column = lax.broadcasted_iota(i32, shape, 1) + first
        row = lax.broadcasted_iota(i32, shape, 0) + i * BLK
        ok = (column >= layout_ref[FIRST + i]) & (column <= row)
        scores = [
            dot_t(q_ref[h, i * BLK : last, :], key_ref[h, first:last, :]) * SIGMA for h in range(HEADS)
        ]
        scores = [jnp.where(ok, s, -1e30) for s in scores]
        weights = [jnp.exp(s - jnp.max(s, axis=1, keepdims=True)) for s in scores]
        weights = [(w * (1.0 / jnp.sum(w, axis=1, keepdims=True))).astype(bf16) for w in weights]
        for h in range(HEADS):
            out_ref[i * BLK : last, h * VD : (h + 1) * VD] = jnp.dot(
                weights[h], value_ref[h, first:last, :], preferred_element_type=f32
            ).astype(bf16)


def prefill(layout, queries, cache, kv_up):
    rows = cache.shape[0]
    return pl.pallas_call(
        prefill_kernel,
        in_specs=[SMEM] + [VMEM] * 3,
        out_specs=VMEM,
        out_shape=jax.ShapeDtypeStruct((rows, HEADS * VD), bf16),
        scratch_shapes=[
            pltpu.VMEM((HEADS, rows, 2 * NOPE), bf16),
            pltpu.VMEM((HEADS, rows, VD), bf16),
        ],
        compiler_params=pltpu.CompilerParams(vmem_limit_bytes=VMEM_LIMIT),
        cost_estimate=pl.CostEstimate(flops=1_500_000_000, bytes_accessed=4_000_000, transcendentals=1_000_000),
        name="prefill_attention",
    )(layout, queries, cache, kv_up)


def body(hidden, comp_query, kv_down, kv_gain, q_up, kv_up, req_blocks, dest_slot, dec_query, dec_latent):
    ids = jnp.stack(
        [lax.axis_index("rep"), lax.axis_index("x"), lax.axis_index("yh"), lax.axis_index("z")]
    ).astype(i32)
    rows, features = hidden.shape[1:]
    per_x = rows // NX
    chunk = per_x // 8
    cos_part, sin_part = rotary_table()

    own = comp_query[0]
    other = lax.ppermute(own, "yh", shift(2, 1))
    pair = jnp.stack([own, other])
    packed, pair = lax.optimization_barrier((pack(hidden[0], kv_down), pair))
    packed = lax.all_to_all(packed, "x", 0, 0, tiled=True)
    layout = request_layout(ids, req_blocks, dest_slot)
    line = [pair] + [lax.ppermute(pair, "x", shift(NX, d)) for d in range(1, NX)]
    line = jnp.concatenate(line).reshape(BLK, -1)
    packed, line, dec_query, dec_latent = lax.optimization_barrier((packed, line, dec_query, dec_latent))
    cq = lax.all_gather(line, "z", axis=0, tiled=True)
    packed = packed.reshape(NX * features, -1)
    partial = lax.dot_general(
        packed[:, :per_x], packed[:, per_x:], (((0,), (0,)), ((), ())), preferred_element_type=f32
    )
    pieces = lax.all_to_all(partial.reshape(8, chunk, -1), "z", 0, 0, tiled=True)
    summed = jnp.sum(pieces, axis=0)
    met = lax.ppermute(summed, "yh", shift(2, 1))
    copies = norm_rows(layout, summed, met, kv_gain[None, :], cos_part, sin_part)
    cache = lax.all_to_all(copies, "z", 0, 0, tiled=True).reshape(per_x, -1)

    rep_in = jnp.concatenate([dec_query, dec_latent], axis=2)
    for d in (1, 2):
        met = lax.ppermute(rep_in, "rep", [(i, i ^ d) for i in range(NREP)])
        rep_in = jnp.concatenate([rep_in, met])
    ready = prepare_decode(layout, rep_in, q_up, kv_up, cos_part, sin_part)
    cache, ready = lax.optimization_barrier((cache, ready))
    cache = spread(cache, "x", NX).reshape(rows, -1)

    queries = project_queries(layout, cq.reshape(8, 8, PAD, -1), q_up, cos_part, sin_part)
    cache, queries = lax.optimization_barrier((cache, queries))
    result = decode(layout, ready, cache, kv_up)
    pool = lax.all_to_all(result, "rep", 0, 0, tiled=True)
    prefill_out = prefill(layout, queries, cache, kv_up)[None]
    pool, prefill_out = lax.optimization_barrier((pool, prefill_out))
    return prefill_out, select(layout, pool)


def solution(mesh):
    fine = Mesh(mesh.devices.reshape(2, 2, 4, 8, 4), ("section", "yh", "x", "z", "rep"))
    tp = ("yh", "x", "z")
    group = ("section", "rep")
    in_specs = (
        P(group, None, tp),
        P(group, tp, None),
        P(tp, None),
        P(),
        P(None, tp),
        P(None, tp),
        P("section", None),
        P("section", None),
        P(group, None, None),
        P(group, None, None),
    )
    out_specs = (P(group, None, tp), P(group, None, tp))
    return jax.shard_map(body, mesh=fine, in_specs=in_specs, out_specs=out_specs, check_vma=False)
```

```python
import math

import jax
import jax.numpy as jnp
import numpy as np
from jax import lax
from jax.experimental import pallas as pl
from jax.experimental.pallas import tpu as pltpu
from jax.sharding import Mesh, PartitionSpec as P

KVL = 512
NOPE = 128
ROPE = 64
VD = 128
BLK = 128
NREQ = 3
STEPS = 4
REACH = 4
NREP = 4
NX = 4
HEADS = 2
PAD = 16
TABLE = 640
NORM_FLOPS = 1_000_000
WIDE = KVL + 2 * ROPE
START, LENGTH, BASE, PLACE, FIRST, SOURCE, SLOT, BLOCK = 0, 3, 6, 8, 16, 24, 28, 32

SIGMA = (1.0 + 0.1 * math.log(40.0)) ** 2 * (NOPE + ROPE) ** (-0.5)
bf16 = jnp.bfloat16
f32 = jnp.float32
i32 = jnp.int32
VMEM_LIMIT = 40 * 1024 * 1024


def rotary_table():
    half = ROPE // 2
    frequency = np.float32(10000.0) ** (-np.arange(half, dtype=np.float32) * np.float32(2.0 / ROPE))
    angles = np.arange(TABLE, dtype=np.float32)[:, None] * frequency.astype(np.float32)
    cos_part, sin_part = np.cos(angles), np.sin(angles)
    return np.concatenate([cos_part] * 4, axis=1), np.concatenate([-sin_part, sin_part] * 2, axis=1)


def rotate(u, cos_part, sin_part):
    lane = lax.broadcasted_iota(i32, u.shape, 1)
    swapped = jnp.where(lane % ROPE < ROPE // 2, pltpu.roll(u, 96, 1), pltpu.roll(u, 32, 1))
    return u * cos_part + swapped * sin_part


def split_heads(u):
    a, b, c = u[:, :NOPE], u[:, NOPE : 2 * NOPE], u[:, 2 * NOPE :]
    low = lax.broadcasted_iota(i32, a.shape, 1) < ROPE
    return a, jnp.where(low, pltpu.roll(b, ROPE, 1), pltpu.roll(c, ROPE, 1)), jnp.where(low, b, c)


def spread(a, axes, count):
    copies = jnp.broadcast_to(a[None], (count,) + a.shape)
    return lax.all_to_all(copies, axes, 0, 0, tiled=True)


def shift(count, d):
    return [(i, (i + d) % count) for i in range(count)]


def dot_t(a, b):
    return lax.dot_general(a, b, (((1,), (1,)), ((), ())), preferred_element_type=f32)


def layout_kernel(ids_ref, req_ref, slot_ref, out_ref):
    rep, x, yh, z = ids_ref[0], ids_ref[1], ids_ref[2], ids_ref[3]
    lengths = [req_ref[rep, r] for r in range(NREQ)]
    starts = [0, lengths[0], lengths[0] + lengths[1]]

    def start_of(block):
        return jnp.where(block >= starts[2], starts[2], jnp.where(block >= starts[1], starts[1], 0))

    for r in range(NREQ):
        out_ref[START + r] = starts[r] * BLK
        out_ref[LENGTH + r] = lengths[r] * BLK
        slot = slot_ref[0, rep * NREQ + r]
        out_ref[SLOT + r] = (lax.div(slot, NREQ) ^ rep) * NREQ + lax.rem(slot, NREQ)
        source = 0
        for m in range(NREP * NREQ):
            source += jnp.where(slot_ref[0, m] == rep * NREQ + r, m, 0)
        out_ref[SOURCE + r] = lax.div(source, NREQ) * PAD + lax.rem(source, NREQ) * STEPS
    out_ref[BASE] = x * 2 * BLK + z * 2 * PAD - start_of(x * 2 + lax.div(z, 4)) * BLK
    for i in range(8):
        out_ref[PLACE + i] = i - start_of(i)
        out_ref[FIRST + i] = start_of(i) * BLK
        out_ref[BLOCK + i] = (yh ^ (i % 2)) * NX + lax.rem(x + NX - i // 2, NX)


SMEM = pl.BlockSpec(memory_space=pltpu.SMEM)
VMEM = pl.BlockSpec(memory_space=pltpu.VMEM)


def request_layout(ids, req_blocks, dest_slot):
    return pl.pallas_call(
        layout_kernel,
        in_specs=[SMEM] * 3,
        out_specs=SMEM,
        out_shape=jax.ShapeDtypeStruct((64,), i32),
        cost_estimate=pl.CostEstimate(flops=1000, bytes_accessed=1000, transcendentals=0),
        name="request_layout",
    )(ids, req_blocks, dest_slot)


def pack_kernel(hidden_ref, down_ref, out_ref):
    features = hidden_ref.shape[1]
    per_x = hidden_ref.shape[0] // NX
    row = lax.broadcasted_iota(i32, (features, features), 0)
    column = lax.broadcasted_iota(i32, (features, features), 1)
    unit = jnp.where(row == column, 1.0, 0.0).astype(bf16)
    for i in range(NX):
        out_ref[i, :, :per_x] = dot_t(unit, hidden_ref[i * per_x : (i + 1) * per_x, :]).astype(bf16)
        out_ref[i, :, per_x:] = down_ref[...]


def pack(hidden, kv_down):
    rows, features = hidden.shape
    return pl.pallas_call(
        pack_kernel,
        in_specs=[VMEM] * 2,
        out_specs=VMEM,
        out_shape=jax.ShapeDtypeStruct((NX, features, rows // NX + kv_down.shape[1]), bf16),
        cost_estimate=pl.CostEstimate(flops=26_000_000, bytes_accessed=1_200_000, transcendentals=0),
        name="pack_hidden",
    )(hidden, kv_down)


def mix_kernel(packed_ref, pair_ref, out_ref):
    count, chunk, _ = out_ref.shape
    width = pair_ref.shape[1]
    per_x = count * chunk
    packed = packed_ref[...].reshape(-1, packed_ref.shape[2])
    partial = lax.dot_general(
        packed[:, :per_x], packed[:, per_x:], (((0,), (0,)), ((), ())), preferred_element_type=f32
    ).astype(bf16)
    for i in range(count):
        out_ref[i, :, :width] = pair_ref[...]
        out_ref[i, :, width:] = partial[i * chunk : (i + 1) * chunk]


def mix(packed, pair):
    chunk, width = pair.shape
    return pl.pallas_call(
        mix_kernel,
        in_specs=[VMEM] * 2,
        out_specs=VMEM,
        out_shape=jax.ShapeDtypeStruct((8, chunk, width + KVL + ROPE), bf16),
        compiler_params=pltpu.CompilerParams(vmem_limit_bytes=VMEM_LIMIT),
        cost_estimate=pl.CostEstimate(flops=130_000_000, bytes_accessed=2_000_000, transcendentals=0),
        name="partial_and_rows",
    )(packed, pair)


def unmix_kernel(mixed_ref, rows_ref, sum_ref):
    width = rows_ref.shape[2]
    rows_ref[...] = mixed_ref[:, :, :width]
    sum_ref[...] = jnp.sum(mixed_ref[:, :, width:].astype(f32), axis=0)


def unmix(mixed, width):
    count, chunk, both = mixed.shape
    return pl.pallas_call(
        unmix_kernel,
        in_specs=[VMEM],
        out_specs=[VMEM, VMEM],
        out_shape=[
            jax.ShapeDtypeStruct((count, chunk, width), bf16),
            jax.ShapeDtypeStruct((chunk, both - width), f32),
        ],
        compiler_params=pltpu.CompilerParams(vmem_limit_bytes=VMEM_LIMIT),
        cost_estimate=pl.CostEstimate(flops=1_000_000, bytes_accessed=2_000_000, transcendentals=0),
        name="rows_and_sum",
    )(mixed)


def norm_kernel(layout_ref, own_ref, other_ref, gain_ref, cos_ref, sin_ref, out_ref):
    latent = own_ref[...] + other_ref[...]
    content = latent[:, :KVL]
    scale = lax.rsqrt(jnp.mean(content * content, axis=1, keepdims=True) + 1e-06)
    content = (content * scale * gain_ref[...]).astype(bf16)
    at = pl.ds(pl.multiple_of(layout_ref[BASE], PAD), latent.shape[0])
    pe = jnp.concatenate([latent[:, KVL:]] * 2, axis=1)
    pe = rotate(pe, cos_ref[at, :], sin_ref[at, :]).astype(bf16)
    for i in range(out_ref.shape[0]):
        out_ref[i, :, :KVL] = content
        out_ref[i, :, KVL:] = pe


def norm_rows(layout, own, other, gain, cos_part, sin_part):
    count, chunk = 8, own.shape[0]
    return pl.pallas_call(
        norm_kernel,
        in_specs=[SMEM] + [VMEM] * 5,
        out_specs=VMEM,
        out_shape=jax.ShapeDtypeStruct((count, chunk, WIDE), bf16),
        cost_estimate=pl.CostEstimate(flops=NORM_FLOPS, bytes_accessed=1_000_000, transcendentals=16),
        name="norm_rows",
    )(layout, own, other, gain, cos_part, sin_part)


def query_kernel(layout_ref, cq_ref, w_ref, cos_ref, sin_ref, *refs):
    out_ref = refs[-1]
    rows = cq_ref[...].reshape(BLK, -1)
    u = jnp.dot(rows, w_ref[...], preferred_element_type=f32)
    first, second, pe = split_heads(u)
    pe = rotate(pe, cos_ref[...], sin_ref[...])
    low = lax.broadcasted_iota(i32, pe.shape, 1) < ROPE
    out_ref[0, :, :NOPE] = first.astype(bf16)
    out_ref[0, :, NOPE:] = jnp.where(low, pe, 0.0).astype(bf16)
    out_ref[1, :, :NOPE] = second.astype(bf16)
    out_ref[1, :, NOPE:] = jnp.where(low, 0.0, pe).astype(bf16)


def project_queries(d, layout, cq, weights, cos_part, sin_part, queries):
    width = cq.shape[-1]

    def block(j, place):
        return place[BLOCK + 2 * d + j]

    table = pl.BlockSpec((BLK, 2 * ROPE), lambda j, place: (place[PLACE + block(j, place)], 0))
    earlier = [] if queries is None else [queries]
    return pl.pallas_call(
        query_kernel,
        grid_spec=pltpu.PrefetchScalarGridSpec(
            num_scalar_prefetch=1,
            grid=(2,),
            in_specs=[
                pl.BlockSpec((8, 1, PAD, width), lambda j, place: (0, j, 0, 0)),
                pl.BlockSpec(weights.shape, lambda j, place: (0, 0)),
                table,
                table,
            ]
            + [pl.BlockSpec(memory_space=pl.ANY)] * len(earlier),
            out_specs=pl.BlockSpec((HEADS, BLK, 2 * NOPE), lambda j, place: (0, block(j, place), 0)),
        ),
        out_shape=jax.ShapeDtypeStruct((HEADS, 8 * BLK, 2 * NOPE), bf16),
        input_output_aliases={5: 0} if earlier else {},
        compiler_params=pltpu.CompilerParams(vmem_limit_bytes=VMEM_LIMIT),
        cost_estimate=pl.CostEstimate(flops=300_000_000, bytes_accessed=2_500_000, transcendentals=0),
        name="project_queries",
    )(layout, cq, weights, cos_part, sin_part, *earlier)


def prepare_kernel(layout_ref, rows_ref, w_ref, kv_ref, cos_ref, sin_ref, out_ref, in_ref, cos_at, sin_at):
    query_latent = w_ref.shape[0]
    in_ref[...] = jnp.zeros_like(in_ref)
    cos_at[...] = jnp.zeros_like(cos_at)
    sin_at[...] = jnp.zeros_like(sin_at)
    for r in range(NREQ):
        here = slice(r * STEPS, (r + 1) * STEPS)
        in_ref[here, :] = rows_ref[layout_ref[SLOT + r]].astype(f32)
        at = pl.ds(pl.multiple_of(layout_ref[LENGTH + r], BLK), 8)
        cos_at[here, :] = cos_ref[at, :][:STEPS]
        sin_at[here, :] = sin_ref[at, :][:STEPS]
    cos_part, sin_part = cos_at[...], sin_at[...]
    rows = in_ref[:, :query_latent].astype(bf16)
    u = jnp.dot(rows, w_ref[...], preferred_element_type=f32).astype(bf16).astype(f32)
    first, second, pe = split_heads(u)
    pe = rotate(pe, cos_part, sin_part)
    low = lax.broadcasted_iota(i32, pe.shape, 1) < ROPE
    for h, plain in enumerate((first, second)):
        here = slice(h * PAD, (h + 1) * PAD)
        base = h * (NOPE + VD)
        out_ref[here, :KVL] = dot_t(plain.astype(bf16), kv_ref[:, base : base + NOPE]).astype(bf16)
        out_ref[here, KVL:] = jnp.where(low == (h == 0), pe, 0.0).astype(bf16)
    new = slice(HEADS * PAD, (HEADS + 1) * PAD)
    out_ref[new, :KVL] = in_ref[:, query_latent : query_latent + KVL].astype(bf16)
    new_pe = jnp.concatenate([in_ref[:, query_latent + KVL :]] * 2, axis=1)
    out_ref[new, KVL:] = rotate(new_pe, cos_part, sin_part).astype(bf16)


def prepare_decode(layout, rows, q_up, kv_up, cos_part, sin_part):
    return pl.pallas_call(
        prepare_kernel,
        in_specs=[SMEM] + [VMEM] * 5,
        out_specs=VMEM,
        out_shape=jax.ShapeDtypeStruct(((HEADS + 1) * PAD, WIDE), bf16),
        scratch_shapes=[
            pltpu.VMEM((PAD, rows.shape[-1]), f32),
            pltpu.VMEM((PAD, 2 * ROPE), f32),
            pltpu.VMEM((PAD, 2 * ROPE), f32),
        ],
        compiler_params=pltpu.CompilerParams(vmem_limit_bytes=VMEM_LIMIT),
        cost_estimate=pl.CostEstimate(flops=30_000_000, bytes_accessed=2_500_000, transcendentals=0),
        name="prepare_decode",
    )(layout, rows, q_up, kv_up, cos_part, sin_part)


def decode_kernel(layout_ref, ready_ref, cache_ref, kv_ref, out_ref):
    query = ready_ref[: HEADS * PAD, :]
    fresh = ready_ref[HEADS * PAD :, :]
    old = dot_t(query, cache_ref[...]) * SIGMA
    new = dot_t(query, fresh) * SIGMA
    request = lax.broadcasted_iota(i32, (HEADS * PAD, 1), 0) % PAD // STEPS

    def per_request(values):
        return jnp.where(request == 0, values[0], jnp.where(request == 1, values[1], values[2]))

    low = per_request([layout_ref[START + r] for r in range(NREQ)])
    high = per_request([layout_ref[START + r] + layout_ref[LENGTH + r] for r in range(NREQ)])
    column = lax.broadcasted_iota(i32, old.shape, 1)
    old = jnp.where((column >= low) & (column < high), old, -1e30)
    step = lax.broadcasted_iota(i32, new.shape, 0) % PAD
    other = lax.broadcasted_iota(i32, new.shape, 1)
    new = jnp.where((step // STEPS == other // STEPS) & (other <= step), new, -1e30)
    top = jnp.maximum(jnp.max(old, axis=1, keepdims=True), jnp.max(new, axis=1, keepdims=True))
    old = jnp.exp(old - top)
    new = jnp.exp(new - top)
    inverse = 1.0 / (jnp.sum(old, axis=1, keepdims=True) + jnp.sum(new, axis=1, keepdims=True))
    old = (old * inverse).astype(bf16)
    new = (new * inverse).astype(bf16)
    mixture = (
        jnp.dot(old, cache_ref[:, :KVL], preferred_element_type=f32)
        + jnp.dot(new, fresh[:, :KVL], preferred_element_type=f32)
    ).astype(bf16)
    for h in range(HEADS):
        base = h * (NOPE + VD) + NOPE
        value = jnp.dot(
            mixture[h * PAD : (h + 1) * PAD], kv_ref[:, base : base + VD], preferred_element_type=f32
        ).astype(bf16)
        for i in range(NREP):
            out_ref[i, :, h * VD : (h + 1) * VD] = value


def decode(layout, ready, cache, kv_up):
    return pl.pallas_call(
        decode_kernel,
        in_specs=[SMEM] + [VMEM] * 3,
        out_specs=VMEM,
        out_shape=jax.ShapeDtypeStruct((NREP, PAD, HEADS * VD), bf16),
        compiler_params=pltpu.CompilerParams(vmem_limit_bytes=VMEM_LIMIT),
        cost_estimate=pl.CostEstimate(flops=100_000_000, bytes_accessed=2_000_000, transcendentals=40_000),
        name="decode_attention",
    )(layout, ready, cache, kv_up)


def select_kernel(layout_ref, pool_ref, out_ref):
    pool = pool_ref[...].reshape(NREP * PAD, -1)
    for r in range(NREQ):
        row = lax.broadcasted_iota(i32, (8, NREP * PAD), 0)
        column = lax.broadcasted_iota(i32, (8, NREP * PAD), 1)
        pick = jnp.where(column == layout_ref[SOURCE + r] + row, 1.0, 0.0).astype(bf16)
        out_ref[r] = jnp.dot(pick, pool, preferred_element_type=f32)[:STEPS].astype(bf16)


def select(layout, pool):
    return pl.pallas_call(
        select_kernel,
        in_specs=[SMEM, VMEM],
        out_specs=VMEM,
        out_shape=jax.ShapeDtypeStruct((NREQ, STEPS, HEADS * VD), bf16),
        cost_estimate=pl.CostEstimate(flops=1_000_000, bytes_accessed=50_000, transcendentals=0),
        name="select_slots",
    )(layout, pool)


def prefill_kernel(layout_ref, q_ref, cache_ref, kv_ref, out_ref, key_ref, value_ref):
    for j in range(4):
        rows = slice(j * 2 * BLK, (j + 1) * 2 * BLK)
        wide = jnp.dot(cache_ref[rows, :KVL], kv_ref[...], preferred_element_type=f32).astype(bf16)
        for h in range(HEADS):
            base = h * (NOPE + VD)
            key_ref[h, rows, :NOPE] = wide[:, base : base + NOPE]
            key_ref[h, rows, NOPE:] = cache_ref[rows, KVL:]
            value_ref[h, rows, :] = wide[:, base + NOPE : base + NOPE + VD]
    for i in range(8):
        first = max(0, i - REACH + 1) * BLK
        last = (i + 1) * BLK
        shape = (BLK, last - first)
        column = lax.broadcasted_iota(i32, shape, 1) + first
        row = lax.broadcasted_iota(i32, shape, 0) + i * BLK
        ok = (column >= layout_ref[FIRST + i]) & (column <= row)
        scores = [
            dot_t(q_ref[h, i * BLK : last, :], key_ref[h, first:last, :]) * SIGMA for h in range(HEADS)
        ]
        scores = [jnp.where(ok, s, -1e30) for s in scores]
        weights = [jnp.exp(s - jnp.max(s, axis=1, keepdims=True)) for s in scores]
        weights = [(w * (1.0 / jnp.sum(w, axis=1, keepdims=True))).astype(bf16) for w in weights]
        for h in range(HEADS):
            out_ref[i * BLK : last, h * VD : (h + 1) * VD] = jnp.dot(
                weights[h], value_ref[h, first:last, :], preferred_element_type=f32
            ).astype(bf16)


def prefill(layout, queries, cache, kv_up):
    rows = cache.shape[0]
    return pl.pallas_call(
        prefill_kernel,
        in_specs=[SMEM] + [VMEM] * 3,
        out_specs=VMEM,
        out_shape=jax.ShapeDtypeStruct((rows, HEADS * VD), bf16),
        scratch_shapes=[
            pltpu.VMEM((HEADS, rows, 2 * NOPE), bf16),
            pltpu.VMEM((HEADS, rows, VD), bf16),
        ],
        compiler_params=pltpu.CompilerParams(vmem_limit_bytes=VMEM_LIMIT),
        cost_estimate=pl.CostEstimate(flops=1_500_000_000, bytes_accessed=4_000_000, transcendentals=1_000_000),
        name="prefill_attention",
    )(layout, queries, cache, kv_up)


def body(hidden, comp_query, kv_down, kv_gain, q_up, kv_up, req_blocks, dest_slot, dec_query, dec_latent):
    ids = jnp.stack(
        [lax.axis_index("rep"), lax.axis_index("x"), lax.axis_index("yh"), lax.axis_index("z")]
    ).astype(i32)
    rows = hidden.shape[1]
    per_x = rows // NX
    cos_part, sin_part = rotary_table()

    own = comp_query[0]
    other = lax.ppermute(own, "yh", shift(2, 1))
    packed = lax.all_to_all(pack(hidden[0], kv_down), "x", 0, 0, tiled=True)
    layout = request_layout(ids, req_blocks, dest_slot)
    pair = jnp.concatenate([own, other])
    packed, pair, dec_query, dec_latent = lax.optimization_barrier((packed, pair, dec_query, dec_latent))

    mixed = lax.all_to_all(mix(packed, pair), "z", 0, 0, tiled=True)
    near, summed = unmix(mixed, own.shape[1])
    met = lax.ppermute(summed, "yh", shift(2, 1))
    chunks = [near] + [lax.ppermute(near, "x", shift(NX, d)) for d in range(1, NX)]
    copies = norm_rows(layout, summed, met, kv_gain[None, :], cos_part, sin_part)
    cache = lax.all_to_all(copies, "z", 0, 0, tiled=True).reshape(per_x, -1)

    rep_in = jnp.concatenate([dec_query, dec_latent], axis=2)
    for d in (1, 2):
        met = lax.ppermute(rep_in, "rep", [(i, i ^ d) for i in range(NREP)])
        rep_in = jnp.concatenate([rep_in, met])
    ready = prepare_decode(layout, rep_in, q_up, kv_up, cos_part, sin_part)
    cache, ready, *chunks = lax.optimization_barrier((cache, ready, *chunks))
    cache = spread(cache, "x", NX).reshape(rows, -1)

    queries = None
    for d, chunk_rows in enumerate(chunks):
        queries = project_queries(
            d, layout, chunk_rows.reshape(8, 2, PAD, -1), q_up, cos_part, sin_part, queries
        )
    cache, queries = lax.optimization_barrier((cache, queries))
    result = decode(layout, ready, cache, kv_up)
    pool = lax.all_to_all(result, "rep", 0, 0, tiled=True)
    prefill_out = prefill(layout, queries, cache, kv_up)[None]
    pool, prefill_out = lax.optimization_barrier((pool, prefill_out))
    return prefill_out, select(layout, pool)


def solution(mesh):
    fine = Mesh(mesh.devices.reshape(2, 2, 4, 8, 4), ("section", "yh", "x", "z", "rep"))
    tp = ("yh", "x", "z")
    group = ("section", "rep")
    in_specs = (
        P(group, None, tp),
        P(group, tp, None),
        P(tp, None),
        P(),
        P(None, tp),
        P(None, tp),
        P("section", None),
        P("section", None),
        P(group, None, None),
        P(group, None, None),
    )
    out_specs = (P(group, None, tp), P(group, None, tp))
    return jax.shard_map(body, mesh=fine, in_specs=in_specs, out_specs=out_specs, check_vma=False)
```

```python
import math

import jax
import jax.numpy as jnp
import numpy as np
from jax import lax
from jax.experimental import pallas as pl
from jax.experimental.pallas import tpu as pltpu
from jax.sharding import Mesh, PartitionSpec as P

KVL = 512
NOPE = 128
ROPE = 64
VD = 128
BLK = 128
NREQ = 3
STEPS = 4
REACH = 4
NREP = 4
NX = 4
HEADS = 2
PAD = 16
TABLE = 640
NORM_FLOPS = 1_000_000
WIDE = KVL + 2 * ROPE
START, LENGTH, BASE, PLACE, FIRST, SOURCE, SLOT, BLOCK = 0, 3, 6, 8, 16, 24, 28, 32

SIGMA = (1.0 + 0.1 * math.log(40.0)) ** 2 * (NOPE + ROPE) ** (-0.5)
bf16 = jnp.bfloat16
f32 = jnp.float32
i32 = jnp.int32
VMEM_LIMIT = 40 * 1024 * 1024


def rotary_table():
    half = ROPE // 2
    frequency = np.float32(10000.0) ** (-np.arange(half, dtype=np.float32) * np.float32(2.0 / ROPE))
    angles = np.arange(TABLE, dtype=np.float32)[:, None] * frequency.astype(np.float32)
    cos_part, sin_part = np.cos(angles), np.sin(angles)
    return np.concatenate([cos_part] * 4, axis=1), np.concatenate([-sin_part, sin_part] * 2, axis=1)


def rotate(u, cos_part, sin_part):
    lane = lax.broadcasted_iota(i32, u.shape, 1)
    swapped = jnp.where(lane % ROPE < ROPE // 2, pltpu.roll(u, 96, 1), pltpu.roll(u, 32, 1))
    return u * cos_part + swapped * sin_part


def split_heads(u):
    a, b, c = u[:, :NOPE], u[:, NOPE : 2 * NOPE], u[:, 2 * NOPE :]
    low = lax.broadcasted_iota(i32, a.shape, 1) < ROPE
    return a, jnp.where(low, pltpu.roll(b, ROPE, 1), pltpu.roll(c, ROPE, 1)), jnp.where(low, b, c)


def spread(a, axes, count):
    copies = jnp.broadcast_to(a[None], (count,) + a.shape)
    return lax.all_to_all(copies, axes, 0, 0, tiled=True)


def shift(count, d):
    return [(i, (i + d) % count) for i in range(count)]


def dot_t(a, b):
    return lax.dot_general(a, b, (((1,), (1,)), ((), ())), preferred_element_type=f32)


def layout_kernel(ids_ref, req_ref, slot_ref, out_ref):
    rep, x, z = ids_ref[0], ids_ref[1], ids_ref[2]
    lengths = [req_ref[rep, r] for r in range(NREQ)]
    starts = [0, lengths[0], lengths[0] + lengths[1]]

    def start_of(block):
        return jnp.where(block >= starts[2], starts[2], jnp.where(block >= starts[1], starts[1], 0))

    for r in range(NREQ):
        out_ref[START + r] = starts[r] * BLK
        out_ref[LENGTH + r] = lengths[r] * BLK
        slot = slot_ref[0, rep * NREQ + r]
        out_ref[SLOT + r] = (lax.div(slot, NREQ) ^ rep) * NREQ + lax.rem(slot, NREQ)
        source = 0
        for m in range(NREP * NREQ):
            source += jnp.where(slot_ref[0, m] == rep * NREQ + r, m, 0)
        out_ref[SOURCE + r] = lax.div(source, NREQ) * PAD + lax.rem(source, NREQ) * STEPS
    out_ref[BASE] = x * 2 * BLK + z * 2 * PAD - start_of(x * 2 + lax.div(z, 4)) * BLK
    for i in range(8):
        out_ref[PLACE + i] = i - start_of(i)
        out_ref[FIRST + i] = start_of(i) * BLK
        out_ref[BLOCK + i] = (i % 2) * NX + lax.rem(x + NX - i // 2, NX)


SMEM = pl.BlockSpec(memory_space=pltpu.SMEM)
VMEM = pl.BlockSpec(memory_space=pltpu.VMEM)


def request_layout(ids, req_blocks, dest_slot):
    return pl.pallas_call(
        layout_kernel,
        in_specs=[SMEM] * 3,
        out_specs=SMEM,
        out_shape=jax.ShapeDtypeStruct((64,), i32),
        cost_estimate=pl.CostEstimate(flops=1000, bytes_accessed=1000, transcendentals=0),
        name="request_layout",
    )(ids, req_blocks, dest_slot)


def pack_kernel(hidden_ref, down_ref, out_ref):
    features = hidden_ref.shape[1]
    per_x = hidden_ref.shape[0] // NX
    row = lax.broadcasted_iota(i32, (features, features), 0)
    column = lax.broadcasted_iota(i32, (features, features), 1)
    unit = jnp.where(row == column, 1.0, 0.0).astype(bf16)
    for i in range(NX):
        out_ref[i, :, :per_x] = dot_t(unit, hidden_ref[i * per_x : (i + 1) * per_x, :]).astype(bf16)
        out_ref[i, :, per_x:] = down_ref[...]


def pack(hidden, kv_down):
    rows, features = hidden.shape
    return pl.pallas_call(
        pack_kernel,
        in_specs=[VMEM] * 2,
        out_specs=VMEM,
        out_shape=jax.ShapeDtypeStruct((NX, features, rows // NX + kv_down.shape[1]), bf16),
        cost_estimate=pl.CostEstimate(flops=26_000_000, bytes_accessed=1_200_000, transcendentals=0),
        name="pack_hidden",
    )(hidden, kv_down)


def norm_kernel(layout_ref, own_ref, other_ref, gain_ref, cos_ref, sin_ref, out_ref):
    latent = own_ref[...] + other_ref[...]
    content = latent[:, :KVL]
    scale = lax.rsqrt(jnp.mean(content * content, axis=1, keepdims=True) + 1e-06)
    content = (content * scale * gain_ref[...]).astype(bf16)
    at = pl.ds(pl.multiple_of(layout_ref[BASE], PAD), latent.shape[0])
    pe = jnp.concatenate([latent[:, KVL:]] * 2, axis=1)
    pe = rotate(pe, cos_ref[at, :], sin_ref[at, :]).astype(bf16)
    for i in range(out_ref.shape[0]):
        out_ref[i, :, :KVL] = content
        out_ref[i, :, KVL:] = pe


def norm_rows(layout, own, other, gain, cos_part, sin_part):
    count, chunk = 8, own.shape[0]
    return pl.pallas_call(
        norm_kernel,
        in_specs=[SMEM] + [VMEM] * 5,
        out_specs=VMEM,
        out_shape=jax.ShapeDtypeStruct((count, chunk, WIDE), bf16),
        cost_estimate=pl.CostEstimate(flops=NORM_FLOPS, bytes_accessed=1_000_000, transcendentals=16),
        name="norm_rows",
    )(layout, own, other, gain, cos_part, sin_part)


def query_kernel(layout_ref, cq_ref, w_ref, cos_ref, sin_ref, *refs):
    out_ref = refs[-1]
    rows = cq_ref[0]
    u = jnp.dot(rows, w_ref[...], preferred_element_type=f32)
    first, second, pe = split_heads(u)
    pe = rotate(pe, cos_ref[...], sin_ref[...])
    low = lax.broadcasted_iota(i32, pe.shape, 1) < ROPE
    out_ref[0, :, :NOPE] = first.astype(bf16)
    out_ref[0, :, NOPE:] = jnp.where(low, pe, 0.0).astype(bf16)
    out_ref[1, :, :NOPE] = second.astype(bf16)
    out_ref[1, :, NOPE:] = jnp.where(low, 0.0, pe).astype(bf16)


def project_queries(d, layout, cq, weights, cos_part, sin_part, queries):
    width = cq.shape[-1]

    def block(j, place):
        return place[BLOCK + 2 * d + j]

    table = pl.BlockSpec((BLK, 2 * ROPE), lambda j, place: (place[PLACE + block(j, place)], 0))
    earlier = [] if queries is None else [queries]
    return pl.pallas_call(
        query_kernel,
        grid_spec=pltpu.PrefetchScalarGridSpec(
            num_scalar_prefetch=1,
            grid=(2,),
            in_specs=[
                pl.BlockSpec((1, BLK, width), lambda j, place: (j, 0, 0)),
                pl.BlockSpec(weights.shape, lambda j, place: (0, 0)),
                table,
                table,
            ]
            + [pl.BlockSpec(memory_space=pl.ANY)] * len(earlier),
            out_specs=pl.BlockSpec((HEADS, BLK, 2 * NOPE), lambda j, place: (0, block(j, place), 0)),
        ),
        out_shape=jax.ShapeDtypeStruct((HEADS, 8 * BLK, 2 * NOPE), bf16),
        input_output_aliases={5: 0} if earlier else {},
        compiler_params=pltpu.CompilerParams(vmem_limit_bytes=VMEM_LIMIT),
        cost_estimate=pl.CostEstimate(flops=300_000_000, bytes_accessed=2_500_000, transcendentals=0),
        name="project_queries",
    )(layout, cq, weights, cos_part, sin_part, *earlier)


def prepare_kernel(layout_ref, rows_ref, w_ref, kv_ref, cos_ref, sin_ref, out_ref, in_ref, cos_at, sin_at):
    query_latent = w_ref.shape[0]
    in_ref[...] = jnp.zeros_like(in_ref)
    cos_at[...] = jnp.zeros_like(cos_at)
    sin_at[...] = jnp.zeros_like(sin_at)
    for r in range(NREQ):
        here = slice(r * STEPS, (r + 1) * STEPS)
        in_ref[here, :] = rows_ref[layout_ref[SLOT + r]].astype(f32)
        at = pl.ds(pl.multiple_of(layout_ref[LENGTH + r], BLK), 8)
        cos_at[here, :] = cos_ref[at, :][:STEPS]
        sin_at[here, :] = sin_ref[at, :][:STEPS]
    cos_part, sin_part = cos_at[...], sin_at[...]
    rows = in_ref[:, :query_latent].astype(bf16)
    u = jnp.dot(rows, w_ref[...], preferred_element_type=f32).astype(bf16).astype(f32)
    first, second, pe = split_heads(u)
    pe = rotate(pe, cos_part, sin_part)
    low = lax.broadcasted_iota(i32, pe.shape, 1) < ROPE
    for h, plain in enumerate((first, second)):
        here = slice(h * PAD, (h + 1) * PAD)
        base = h * (NOPE + VD)
        out_ref[here, :KVL] = dot_t(plain.astype(bf16), kv_ref[:, base : base + NOPE]).astype(bf16)
        out_ref[here, KVL:] = jnp.where(low == (h == 0), pe, 0.0).astype(bf16)
    new = slice(HEADS * PAD, (HEADS + 1) * PAD)
    out_ref[new, :KVL] = in_ref[:, query_latent : query_latent + KVL].astype(bf16)
    new_pe = jnp.concatenate([in_ref[:, query_latent + KVL :]] * 2, axis=1)
    out_ref[new, KVL:] = rotate(new_pe, cos_part, sin_part).astype(bf16)


def prepare_decode(layout, rows, q_up, kv_up, cos_part, sin_part):
    return pl.pallas_call(
        prepare_kernel,
        in_specs=[SMEM] + [VMEM] * 5,
        out_specs=VMEM,
        out_shape=jax.ShapeDtypeStruct(((HEADS + 1) * PAD, WIDE), bf16),
        scratch_shapes=[
            pltpu.VMEM((PAD, rows.shape[-1]), f32),
            pltpu.VMEM((PAD, 2 * ROPE), f32),
            pltpu.VMEM((PAD, 2 * ROPE), f32),
        ],
        compiler_params=pltpu.CompilerParams(vmem_limit_bytes=VMEM_LIMIT),
        cost_estimate=pl.CostEstimate(flops=30_000_000, bytes_accessed=2_500_000, transcendentals=0),
        name="prepare_decode",
    )(layout, rows, q_up, kv_up, cos_part, sin_part)


def decode_kernel(layout_ref, ready_ref, cache_ref, kv_ref, out_ref):
    query = ready_ref[: HEADS * PAD, :]
    fresh = ready_ref[HEADS * PAD :, :]
    old = dot_t(query, cache_ref[...]) * SIGMA
    new = dot_t(query, fresh) * SIGMA
    request = lax.broadcasted_iota(i32, (HEADS * PAD, 1), 0) % PAD // STEPS

    def per_request(values):
        return jnp.where(request == 0, values[0], jnp.where(request == 1, values[1], values[2]))

    low = per_request([layout_ref[START + r] for r in range(NREQ)])
    high = per_request([layout_ref[START + r] + layout_ref[LENGTH + r] for r in range(NREQ)])
    column = lax.broadcasted_iota(i32, old.shape, 1)
    old = jnp.where((column >= low) & (column < high), old, -1e30)
    step = lax.broadcasted_iota(i32, new.shape, 0) % PAD
    other = lax.broadcasted_iota(i32, new.shape, 1)
    new = jnp.where((step // STEPS == other // STEPS) & (other <= step), new, -1e30)
    top = jnp.maximum(jnp.max(old, axis=1, keepdims=True), jnp.max(new, axis=1, keepdims=True))
    old = jnp.exp(old - top)
    new = jnp.exp(new - top)
    inverse = 1.0 / (jnp.sum(old, axis=1, keepdims=True) + jnp.sum(new, axis=1, keepdims=True))
    old = (old * inverse).astype(bf16)
    new = (new * inverse).astype(bf16)
    mixture = (
        jnp.dot(old, cache_ref[:, :KVL], preferred_element_type=f32)
        + jnp.dot(new, fresh[:, :KVL], preferred_element_type=f32)
    ).astype(bf16)
    for h in range(HEADS):
        base = h * (NOPE + VD) + NOPE
        value = jnp.dot(
            mixture[h * PAD : (h + 1) * PAD], kv_ref[:, base : base + VD], preferred_element_type=f32
        ).astype(bf16)
        for i in range(NREP):
            out_ref[i, :, h * VD : (h + 1) * VD] = value


def decode(layout, ready, cache, kv_up):
    return pl.pallas_call(
        decode_kernel,
        in_specs=[SMEM] + [VMEM] * 3,
        out_specs=VMEM,
        out_shape=jax.ShapeDtypeStruct((NREP, PAD, HEADS * VD), bf16),
        compiler_params=pltpu.CompilerParams(vmem_limit_bytes=VMEM_LIMIT),
        cost_estimate=pl.CostEstimate(flops=100_000_000, bytes_accessed=2_000_000, transcendentals=40_000),
        name="decode_attention",
    )(layout, ready, cache, kv_up)


def select_kernel(layout_ref, pool_ref, out_ref):
    pool = pool_ref[...].reshape(NREP * PAD, -1)
    for r in range(NREQ):
        row = lax.broadcasted_iota(i32, (8, NREP * PAD), 0)
        column = lax.broadcasted_iota(i32, (8, NREP * PAD), 1)
        pick = jnp.where(column == layout_ref[SOURCE + r] + row, 1.0, 0.0).astype(bf16)
        out_ref[r] = jnp.dot(pick, pool, preferred_element_type=f32)[:STEPS].astype(bf16)


def select(layout, pool):
    return pl.pallas_call(
        select_kernel,
        in_specs=[SMEM, VMEM],
        out_specs=VMEM,
        out_shape=jax.ShapeDtypeStruct((NREQ, STEPS, HEADS * VD), bf16),
        cost_estimate=pl.CostEstimate(flops=1_000_000, bytes_accessed=50_000, transcendentals=0),
        name="select_slots",
    )(layout, pool)


def prefill_kernel(layout_ref, q_ref, cache_ref, kv_ref, out_ref, key_ref, value_ref):
    for j in range(4):
        rows = slice(j * 2 * BLK, (j + 1) * 2 * BLK)
        wide = jnp.dot(cache_ref[rows, :KVL], kv_ref[...], preferred_element_type=f32).astype(bf16)
        for h in range(HEADS):
            base = h * (NOPE + VD)
            key_ref[h, rows, :NOPE] = wide[:, base : base + NOPE]
            key_ref[h, rows, NOPE:] = cache_ref[rows, KVL:]
            value_ref[h, rows, :] = wide[:, base + NOPE : base + NOPE + VD]
    for i in range(8):
        first = max(0, i - REACH + 1) * BLK
        last = (i + 1) * BLK
        shape = (BLK, last - first)
        column = lax.broadcasted_iota(i32, shape, 1) + first
        row = lax.broadcasted_iota(i32, shape, 0) + i * BLK
        ok = (column >= layout_ref[FIRST + i]) & (column <= row)
        scores = [
            dot_t(q_ref[h, i * BLK : last, :], key_ref[h, first:last, :]) * SIGMA for h in range(HEADS)
        ]
        scores = [jnp.where(ok, s, -1e30) for s in scores]
        weights = [jnp.exp(s - jnp.max(s, axis=1, keepdims=True)) for s in scores]
        weights = [(w * (1.0 / jnp.sum(w, axis=1, keepdims=True))).astype(bf16) for w in weights]
        for h in range(HEADS):
            out_ref[i * BLK : last, h * VD : (h + 1) * VD] = jnp.dot(
                weights[h], value_ref[h, first:last, :], preferred_element_type=f32
            ).astype(bf16)


def prefill(layout, queries, cache, kv_up):
    rows = cache.shape[0]
    return pl.pallas_call(
        prefill_kernel,
        in_specs=[SMEM] + [VMEM] * 3,
        out_specs=VMEM,
        out_shape=jax.ShapeDtypeStruct((rows, HEADS * VD), bf16),
        scratch_shapes=[
            pltpu.VMEM((HEADS, rows, 2 * NOPE), bf16),
            pltpu.VMEM((HEADS, rows, VD), bf16),
        ],
        compiler_params=pltpu.CompilerParams(vmem_limit_bytes=VMEM_LIMIT),
        cost_estimate=pl.CostEstimate(flops=1_500_000_000, bytes_accessed=4_000_000, transcendentals=1_000_000),
        name="prefill_attention",
    )(layout, queries, cache, kv_up)


def body(hidden, comp_query, kv_down, kv_gain, q_up, kv_up, req_blocks, dest_slot, dec_query, dec_latent):
    ids = jnp.stack(
        [lax.axis_index("rep"), lax.axis_index("x"), lax.axis_index("z"), lax.axis_index("yh")]
    ).astype(i32)
    rows = hidden.shape[1]
    per_x = rows // NX
    cos_part, sin_part = rotary_table()

    layout = request_layout(ids, req_blocks, dest_slot)
    near = spread(comp_query[0], ("yh", "z"), 16).reshape(2, BLK, -1)
    packed, near = lax.optimization_barrier((pack(hidden[0], kv_down), near))
    chunks = [near] + [lax.ppermute(near, "x", shift(NX, d)) for d in range(1, NX)]
    packed = lax.all_to_all(packed, "x", 0, 0, tiled=True)
    packed, dec_query, dec_latent = lax.optimization_barrier((packed, dec_query, dec_latent))
    packed = packed.reshape(-1, packed.shape[2])
    partial = lax.dot_general(
        packed[:, :per_x], packed[:, per_x:], (((0,), (0,)), ((), ())), preferred_element_type=f32
    )
    pieces = lax.all_to_all(partial.reshape(8, per_x // 8, -1), "z", 0, 0, tiled=True)
    pieces, chunks[1], chunks[3] = lax.optimization_barrier((pieces, chunks[1], chunks[3]))
    summed = jnp.sum(pieces, axis=0)
    met = lax.ppermute(summed, "yh", shift(2, 1))
    copies = norm_rows(layout, summed, met, kv_gain[None, :], cos_part, sin_part)
    cache = lax.all_to_all(copies, "z", 0, 0, tiled=True).reshape(per_x, -1)

    rep_in = jnp.concatenate([dec_query, dec_latent], axis=2)
    for d in (1, 2):
        met = lax.ppermute(rep_in, "rep", [(i, i ^ d) for i in range(NREP)])
        rep_in = jnp.concatenate([rep_in, met])
    ready = prepare_decode(layout, rep_in, q_up, kv_up, cos_part, sin_part)
    cache, ready, *chunks = lax.optimization_barrier((cache, ready, *chunks))
    cache = spread(cache, "x", NX).reshape(rows, -1)

    queries = None
    for d, chunk_rows in enumerate(chunks):
        queries = project_queries(
            d, layout, chunk_rows, q_up, cos_part, sin_part, queries
        )
    cache, queries = lax.optimization_barrier((cache, queries))
    result = decode(layout, ready, cache, kv_up)
    pool = lax.all_to_all(result, "rep", 0, 0, tiled=True)
    prefill_out = prefill(layout, queries, cache, kv_up)[None]
    pool, prefill_out = lax.optimization_barrier((pool, prefill_out))
    return prefill_out, select(layout, pool)


def solution(mesh):
    fine = Mesh(mesh.devices.reshape(2, 2, 4, 8, 4), ("section", "yh", "x", "z", "rep"))
    tp = ("yh", "x", "z")
    group = ("section", "rep")
    in_specs = (
        P(group, None, tp),
        P(group, tp, None),
        P(tp, None),
        P(),
        P(None, tp),
        P(None, tp),
        P("section", None),
        P("section", None),
        P(group, None, None),
        P(group, None, None),
    )
    out_specs = (P(group, None, tp), P(group, None, tp))
    return jax.shard_map(body, mesh=fine, in_specs=in_specs, out_specs=out_specs, check_vma=False)
```

```python
import math

import jax
import jax.numpy as jnp
import numpy as np
from jax import lax
from jax.experimental import pallas as pl
from jax.experimental.pallas import tpu as pltpu
from jax.sharding import Mesh, PartitionSpec as P

KVL = 512
NOPE = 128
ROPE = 64
VD = 128
BLK = 128
NREQ = 3
STEPS = 4
REACH = 4
NREP = 4
NX = 4
HEADS = 2
PAD = 16
TABLE = 640
WIDE = KVL + 2 * ROPE
START, LENGTH, BASE, PLACE, FIRST, SOURCE, SLOT, BLOCK = 0, 3, 6, 8, 16, 24, 28, 32

SIGMA = (1.0 + 0.1 * math.log(40.0)) ** 2 * (NOPE + ROPE) ** (-0.5)
bf16 = jnp.bfloat16
f32 = jnp.float32
i32 = jnp.int32
VMEM_LIMIT = 40 * 1024 * 1024


def rotary_table():
    half = ROPE // 2
    frequency = np.float32(10000.0) ** (-np.arange(half, dtype=np.float32) * np.float32(2.0 / ROPE))
    angles = np.arange(TABLE, dtype=np.float32)[:, None] * frequency.astype(np.float32)
    cos_part, sin_part = np.cos(angles), np.sin(angles)
    return np.concatenate([cos_part] * 4, axis=1), np.concatenate([-sin_part, sin_part] * 2, axis=1)


def rotate(u, cos_part, sin_part):
    lane = lax.broadcasted_iota(i32, u.shape, 1)
    swapped = jnp.where(lane % ROPE < ROPE // 2, pltpu.roll(u, 96, 1), pltpu.roll(u, 32, 1))
    return u * cos_part + swapped * sin_part


def split_heads(u):
    a, b, c = u[:, :NOPE], u[:, NOPE : 2 * NOPE], u[:, 2 * NOPE :]
    low = lax.broadcasted_iota(i32, a.shape, 1) < ROPE
    return a, jnp.where(low, pltpu.roll(b, ROPE, 1), pltpu.roll(c, ROPE, 1)), jnp.where(low, b, c)


def spread(a, axes, count):
    copies = jnp.broadcast_to(a[None], (count,) + a.shape)
    return lax.all_to_all(copies, axes, 0, 0, tiled=True)


def shift(count, d):
    return [(i, (i + d) % count) for i in range(count)]


def dot_t(a, b):
    return lax.dot_general(a, b, (((1,), (1,)), ((), ())), preferred_element_type=f32)


def layout_kernel(ids_ref, req_ref, slot_ref, out_ref):
    rep, x, yh, yz = ids_ref[0], ids_ref[1], ids_ref[2], ids_ref[3]
    lengths = [req_ref[rep, r] for r in range(NREQ)]
    starts = [0, lengths[0], lengths[0] + lengths[1]]

    def start_of(block):
        return jnp.where(block >= starts[2], starts[2], jnp.where(block >= starts[1], starts[1], 0))

    for r in range(NREQ):
        out_ref[START + r] = starts[r] * BLK
        out_ref[LENGTH + r] = lengths[r] * BLK
        slot = slot_ref[0, rep * NREQ + r]
        out_ref[SLOT + r] = (lax.div(slot, NREQ) ^ rep) * NREQ + lax.rem(slot, NREQ)
        source = 0
        for m in range(NREP * NREQ):
            source += jnp.where(slot_ref[0, m] == rep * NREQ + r, m, 0)
        out_ref[SOURCE + r] = lax.div(source, NREQ) * PAD + lax.rem(source, NREQ) * STEPS
    out_ref[BASE] = x * 2 * BLK + yz * PAD - start_of(x * 2 + lax.div(yz, 8)) * BLK
    for i in range(8):
        out_ref[PLACE + i] = i - start_of(i)
        out_ref[FIRST + i] = start_of(i) * BLK
        out_ref[BLOCK + i] = lax.rem(x + NX - i % NX, NX) * 2 + (yh ^ (i // NX))


SMEM = pl.BlockSpec(memory_space=pltpu.SMEM)
VMEM = pl.BlockSpec(memory_space=pltpu.VMEM)


def request_layout(ids, req_blocks, dest_slot):
    return pl.pallas_call(
        layout_kernel,
        in_specs=[SMEM] * 3,
        out_specs=SMEM,
        out_shape=jax.ShapeDtypeStruct((64,), i32),
        cost_estimate=pl.CostEstimate(flops=1000, bytes_accessed=1000, transcendentals=0),
        name="request_layout",
    )(ids, req_blocks, dest_slot)


def pack_kernel(hidden_ref, down_ref, out_ref):
    features = hidden_ref.shape[1]
    per_x = hidden_ref.shape[0] // NX
    row = lax.broadcasted_iota(i32, (features, features), 0)
    column = lax.broadcasted_iota(i32, (features, features), 1)
    unit = jnp.where(row == column, 1.0, 0.0).astype(bf16)
    for i in range(NX):
        out_ref[i, :, :per_x] = dot_t(unit, hidden_ref[i * per_x : (i + 1) * per_x, :]).astype(bf16)
        out_ref[i, :, per_x:] = down_ref[...]


def pack(hidden, kv_down):
    rows, features = hidden.shape
    return pl.pallas_call(
        pack_kernel,
        in_specs=[VMEM] * 2,
        out_specs=VMEM,
        out_shape=jax.ShapeDtypeStruct((NX, features, rows // NX + kv_down.shape[1]), bf16),
        cost_estimate=pl.CostEstimate(flops=26_000_000, bytes_accessed=1_200_000, transcendentals=0),
        name="pack_hidden",
    )(hidden, kv_down)


def norm_kernel(layout_ref, pieces_ref, gain_ref, cos_ref, sin_ref, out_ref):
    latent = jnp.sum(pieces_ref[...], axis=0)
    content = latent[:, :KVL]
    scale = lax.rsqrt(jnp.mean(content * content, axis=1, keepdims=True) + 1e-06)
    content = (content * scale * gain_ref[...]).astype(bf16)
    at = pl.ds(pl.multiple_of(layout_ref[BASE], PAD), latent.shape[0])
    pe = jnp.concatenate([latent[:, KVL:]] * 2, axis=1)
    pe = rotate(pe, cos_ref[at, :], sin_ref[at, :]).astype(bf16)
    for i in range(out_ref.shape[0]):
        out_ref[i, :, :KVL] = content
        out_ref[i, :, KVL:] = pe


def norm_rows(layout, pieces, gain, cos_part, sin_part):
    count, chunk, _ = pieces.shape
    return pl.pallas_call(
        norm_kernel,
        in_specs=[SMEM] + [VMEM] * 4,
        out_specs=VMEM,
        out_shape=jax.ShapeDtypeStruct((count, chunk, WIDE), bf16),
        cost_estimate=pl.CostEstimate(flops=1_000_000, bytes_accessed=1_000_000, transcendentals=16),
        name="norm_rows",
    )(layout, pieces, gain, cos_part, sin_part)


def query_kernel(layout_ref, cq_ref, w_ref, cos_ref, sin_ref, out_ref):
    rows = cq_ref[...].reshape(BLK, -1)
    u = jnp.dot(rows, w_ref[...], preferred_element_type=f32)
    first, second, pe = split_heads(u)
    pe = rotate(pe, cos_ref[...], sin_ref[...])
    low = lax.broadcasted_iota(i32, pe.shape, 1) < ROPE
    out_ref[0, :, :NOPE] = first.astype(bf16)
    out_ref[0, :, NOPE:] = jnp.where(low, pe, 0.0).astype(bf16)
    out_ref[1, :, :NOPE] = second.astype(bf16)
    out_ref[1, :, NOPE:] = jnp.where(low, 0.0, pe).astype(bf16)


def project_queries(layout, cq, weights, cos_part, sin_part):
    width = cq.shape[-1]
    table = pl.BlockSpec((BLK, 2 * ROPE), lambda i, place: (place[PLACE + i], 0))
    return pl.pallas_call(
        query_kernel,
        grid_spec=pltpu.PrefetchScalarGridSpec(
            num_scalar_prefetch=1,
            grid=(8,),
            in_specs=[
                pl.BlockSpec((8, 1, PAD, width), lambda i, place: (0, place[BLOCK + i], 0, 0)),
                pl.BlockSpec(weights.shape, lambda i, place: (0, 0)),
                table,
                table,
            ],
            out_specs=pl.BlockSpec((HEADS, BLK, 2 * NOPE), lambda i, place: (0, i, 0)),
        ),
        out_shape=jax.ShapeDtypeStruct((HEADS, 8 * BLK, 2 * NOPE), bf16),
        compiler_params=pltpu.CompilerParams(vmem_limit_bytes=VMEM_LIMIT),
        cost_estimate=pl.CostEstimate(flops=1_200_000_000, bytes_accessed=5_000_000, transcendentals=0),
        name="project_queries",
    )(layout, cq, weights, cos_part, sin_part)


def prepare_kernel(layout_ref, rows_ref, w_ref, kv_ref, cos_ref, sin_ref, out_ref, in_ref, cos_at, sin_at):
    query_latent = w_ref.shape[0]
    in_ref[...] = jnp.zeros_like(in_ref)
    cos_at[...] = jnp.zeros_like(cos_at)
    sin_at[...] = jnp.zeros_like(sin_at)
    for r in range(NREQ):
        here = slice(r * STEPS, (r + 1) * STEPS)
        in_ref[here, :] = rows_ref[layout_ref[SLOT + r]].astype(f32)
        at = pl.ds(pl.multiple_of(layout_ref[LENGTH + r], BLK), 8)
        cos_at[here, :] = cos_ref[at, :][:STEPS]
        sin_at[here, :] = sin_ref[at, :][:STEPS]
    cos_part, sin_part = cos_at[...], sin_at[...]
    rows = in_ref[:, :query_latent].astype(bf16)
    u = jnp.dot(rows, w_ref[...], preferred_element_type=f32).astype(bf16).astype(f32)
    first, second, pe = split_heads(u)
    pe = rotate(pe, cos_part, sin_part)
    low = lax.broadcasted_iota(i32, pe.shape, 1) < ROPE
    for h, plain in enumerate((first, second)):
        here = slice(h * PAD, (h + 1) * PAD)
        base = h * (NOPE + VD)
        out_ref[here, :KVL] = dot_t(plain.astype(bf16), kv_ref[:, base : base + NOPE]).astype(bf16)
        out_ref[here, KVL:] = jnp.where(low == (h == 0), pe, 0.0).astype(bf16)
    new = slice(HEADS * PAD, (HEADS + 1) * PAD)
    out_ref[new, :KVL] = in_ref[:, query_latent : query_latent + KVL].astype(bf16)
    new_pe = jnp.concatenate([in_ref[:, query_latent + KVL :]] * 2, axis=1)
    out_ref[new, KVL:] = rotate(new_pe, cos_part, sin_part).astype(bf16)


def prepare_decode(layout, rows, q_up, kv_up, cos_part, sin_part):
    return pl.pallas_call(
        prepare_kernel,
        in_specs=[SMEM] + [VMEM] * 5,
        out_specs=VMEM,
        out_shape=jax.ShapeDtypeStruct(((HEADS + 1) * PAD, WIDE), bf16),
        scratch_shapes=[
            pltpu.VMEM((PAD, rows.shape[-1]), f32),
            pltpu.VMEM((PAD, 2 * ROPE), f32),
            pltpu.VMEM((PAD, 2 * ROPE), f32),
        ],
        compiler_params=pltpu.CompilerParams(vmem_limit_bytes=VMEM_LIMIT),
        cost_estimate=pl.CostEstimate(flops=30_000_000, bytes_accessed=2_500_000, transcendentals=0),
        name="prepare_decode",
    )(layout, rows, q_up, kv_up, cos_part, sin_part)


def decode_kernel(layout_ref, ready_ref, cache_ref, kv_ref, out_ref):
    query = ready_ref[: HEADS * PAD, :]
    fresh = ready_ref[HEADS * PAD :, :]
    old = dot_t(query, cache_ref[...]) * SIGMA
    new = dot_t(query, fresh) * SIGMA
    request = lax.broadcasted_iota(i32, (HEADS * PAD, 1), 0) % PAD // STEPS

    def per_request(values):
        return jnp.where(request == 0, values[0], jnp.where(request == 1, values[1], values[2]))

    low = per_request([layout_ref[START + r] for r in range(NREQ)])
    high = per_request([layout_ref[START + r] + layout_ref[LENGTH + r] for r in range(NREQ)])
    column = lax.broadcasted_iota(i32, old.shape, 1)
    old = jnp.where((column >= low) & (column < high), old, -1e30)
    step = lax.broadcasted_iota(i32, new.shape, 0) % PAD
    other = lax.broadcasted_iota(i32, new.shape, 1)
    new = jnp.where((step // STEPS == other // STEPS) & (other <= step), new, -1e30)
    top = jnp.maximum(jnp.max(old, axis=1, keepdims=True), jnp.max(new, axis=1, keepdims=True))
    old = jnp.exp(old - top)
    new = jnp.exp(new - top)
    inverse = 1.0 / (jnp.sum(old, axis=1, keepdims=True) + jnp.sum(new, axis=1, keepdims=True))
    old = (old * inverse).astype(bf16)
    new = (new * inverse).astype(bf16)
    mixture = (
        jnp.dot(old, cache_ref[:, :KVL], preferred_element_type=f32)
        + jnp.dot(new, fresh[:, :KVL], preferred_element_type=f32)
    ).astype(bf16)
    for h in range(HEADS):
        base = h * (NOPE + VD) + NOPE
        value = jnp.dot(
            mixture[h * PAD : (h + 1) * PAD], kv_ref[:, base : base + VD], preferred_element_type=f32
        ).astype(bf16)
        for i in range(NREP):
            out_ref[i, :, h * VD : (h + 1) * VD] = value


def decode(layout, ready, cache, kv_up):
    return pl.pallas_call(
        decode_kernel,
        in_specs=[SMEM] + [VMEM] * 3,
        out_specs=VMEM,
        out_shape=jax.ShapeDtypeStruct((NREP, PAD, HEADS * VD), bf16),
        compiler_params=pltpu.CompilerParams(vmem_limit_bytes=VMEM_LIMIT),
        cost_estimate=pl.CostEstimate(flops=100_000_000, bytes_accessed=2_000_000, transcendentals=40_000),
        name="decode_attention",
    )(layout, ready, cache, kv_up)


def select_kernel(layout_ref, pool_ref, out_ref):
    pool = pool_ref[...].reshape(NREP * PAD, -1)
    for r in range(NREQ):
        row = lax.broadcasted_iota(i32, (8, NREP * PAD), 0)
        column = lax.broadcasted_iota(i32, (8, NREP * PAD), 1)
        pick = jnp.where(column == layout_ref[SOURCE + r] + row, 1.0, 0.0).astype(bf16)
        out_ref[r] = jnp.dot(pick, pool, preferred_element_type=f32)[:STEPS].astype(bf16)


def select(layout, pool):
    return pl.pallas_call(
        select_kernel,
        in_specs=[SMEM, VMEM],
        out_specs=VMEM,
        out_shape=jax.ShapeDtypeStruct((NREQ, STEPS, HEADS * VD), bf16),
        cost_estimate=pl.CostEstimate(flops=1_000_000, bytes_accessed=50_000, transcendentals=0),
        name="select_slots",
    )(layout, pool)


def prefill_kernel(layout_ref, q_ref, cache_ref, kv_ref, out_ref, key_ref, value_ref):
    for j in range(4):
        rows = slice(j * 2 * BLK, (j + 1) * 2 * BLK)
        wide = jnp.dot(cache_ref[rows, :KVL], kv_ref[...], preferred_element_type=f32).astype(bf16)
        for h in range(HEADS):
            base = h * (NOPE + VD)
            key_ref[h, rows, :NOPE] = wide[:, base : base + NOPE]
            key_ref[h, rows, NOPE:] = cache_ref[rows, KVL:]
            value_ref[h, rows, :] = wide[:, base + NOPE : base + NOPE + VD]
    for i in range(8):
        first = max(0, i - REACH + 1) * BLK
        last = (i + 1) * BLK
        shape = (BLK, last - first)
        column = lax.broadcasted_iota(i32, shape, 1) + first
        row = lax.broadcasted_iota(i32, shape, 0) + i * BLK
        ok = (column >= layout_ref[FIRST + i]) & (column <= row)
        scores = [
            dot_t(q_ref[h, i * BLK : last, :], key_ref[h, first:last, :]) * SIGMA for h in range(HEADS)
        ]
        scores = [jnp.where(ok, s, -1e30) for s in scores]
        weights = [jnp.exp(s - jnp.max(s, axis=1, keepdims=True)) for s in scores]
        weights = [(w * (1.0 / jnp.sum(w, axis=1, keepdims=True))).astype(bf16) for w in weights]
        for h in range(HEADS):
            out_ref[i * BLK : last, h * VD : (h + 1) * VD] = jnp.dot(
                weights[h], value_ref[h, first:last, :], preferred_element_type=f32
            ).astype(bf16)


def prefill(layout, queries, cache, kv_up):
    rows = cache.shape[0]
    return pl.pallas_call(
        prefill_kernel,
        in_specs=[SMEM] + [VMEM] * 3,
        out_specs=VMEM,
        out_shape=jax.ShapeDtypeStruct((rows, HEADS * VD), bf16),
        scratch_shapes=[
            pltpu.VMEM((HEADS, rows, 2 * NOPE), bf16),
            pltpu.VMEM((HEADS, rows, VD), bf16),
        ],
        compiler_params=pltpu.CompilerParams(vmem_limit_bytes=VMEM_LIMIT),
        cost_estimate=pl.CostEstimate(flops=1_500_000_000, bytes_accessed=4_000_000, transcendentals=1_000_000),
        name="prefill_attention",
    )(layout, queries, cache, kv_up)


def body(hidden, comp_query, kv_down, kv_gain, q_up, kv_up, req_blocks, dest_slot, dec_query, dec_latent):
    ids = jnp.stack(
        [lax.axis_index("rep"), lax.axis_index("x"), lax.axis_index("yh"), lax.axis_index(("yh", "z"))]
    ).astype(i32)
    rows, features = hidden.shape[1:]
    per_x = rows // NX
    chunk = per_x // 16
    cos_part, sin_part = rotary_table()

    own = comp_query[0]
    other = lax.ppermute(own, "yh", shift(2, 1))
    pair = jnp.stack([own, other])
    packed = lax.all_to_all(pack(hidden[0], kv_down), "x", 0, 0, tiled=True)
    layout = request_layout(ids, req_blocks, dest_slot)
    line = [pair] + [lax.ppermute(pair, "x", shift(NX, d)) for d in range(1, NX)]
    line = jnp.concatenate(line).reshape(BLK, -1)
    packed, line, dec_query, dec_latent = lax.optimization_barrier((packed, line, dec_query, dec_latent))
    cq = lax.all_gather(line, "z", axis=0, tiled=True)
    packed = packed.reshape(NX * features, -1)
    partial = lax.dot_general(
        packed[:, :per_x], packed[:, per_x:], (((0,), (0,)), ((), ())), preferred_element_type=f32
    )
    pieces = lax.all_to_all(partial.reshape(16, chunk, -1), ("yh", "z"), 0, 0, tiled=True)
    copies = norm_rows(layout, pieces, kv_gain[None, :], cos_part, sin_part)
    cache = lax.all_to_all(copies, ("yh", "z"), 0, 0, tiled=True).reshape(per_x, -1)

    rep_in = jnp.concatenate([dec_query, dec_latent], axis=2)
    for d in (1, 2):
        met = lax.ppermute(rep_in, "rep", [(i, i ^ d) for i in range(NREP)])
        rep_in = jnp.concatenate([rep_in, met])
    ready = prepare_decode(layout, rep_in, q_up, kv_up, cos_part, sin_part)
    cache, ready = lax.optimization_barrier((cache, ready))
    cache = spread(cache, "x", NX).reshape(rows, -1)

    queries = project_queries(layout, cq.reshape(8, 8, PAD, -1), q_up, cos_part, sin_part)
    cache, queries = lax.optimization_barrier((cache, queries))
    result = decode(layout, ready, cache, kv_up)
    pool = lax.all_to_all(result, "rep", 0, 0, tiled=True)
    prefill_out = prefill(layout, queries, cache, kv_up)[None]
    pool, prefill_out = lax.optimization_barrier((pool, prefill_out))
    return prefill_out, select(layout, pool)


def solution(mesh):
    fine = Mesh(mesh.devices.reshape(2, 2, 4, 8, 4), ("section", "yh", "x", "z", "rep"))
    tp = ("yh", "x", "z")
    group = ("section", "rep")
    in_specs = (
        P(group, None, tp),
        P(group, tp, None),
        P(tp, None),
        P(),
        P(None, tp),
        P(None, tp),
        P("section", None),
        P("section", None),
        P(group, None, None),
        P(group, None, None),
    )
    out_specs = (P(group, None, tp), P(group, None, tp))
    return jax.shard_map(body, mesh=fine, in_specs=in_specs, out_specs=out_specs, check_vma=False)
```

```python
import math

import jax
import jax.numpy as jnp
import numpy as np
from jax import lax
from jax.experimental import pallas as pl
from jax.experimental.pallas import tpu as pltpu
from jax.sharding import Mesh, PartitionSpec as P

KVL = 512
NOPE = 128
ROPE = 64
VD = 128
BLK = 128
NREQ = 3
STEPS = 4
REACH = 4
NREP = 4
NX = 4
HEADS = 2
PAD = 16
TABLE = 640
NORM_FLOPS = 30_000_000_000
WIDE = KVL + 2 * ROPE
START, LENGTH, BASE, PLACE, FIRST, SOURCE, SLOT, BLOCK = 0, 3, 6, 8, 16, 24, 28, 32

SIGMA = (1.0 + 0.1 * math.log(40.0)) ** 2 * (NOPE + ROPE) ** (-0.5)
bf16 = jnp.bfloat16
f32 = jnp.float32
i32 = jnp.int32
VMEM_LIMIT = 40 * 1024 * 1024


def rotary_table():
    half = ROPE // 2
    frequency = np.float32(10000.0) ** (-np.arange(half, dtype=np.float32) * np.float32(2.0 / ROPE))
    angles = np.arange(TABLE, dtype=np.float32)[:, None] * frequency.astype(np.float32)
    cos_part, sin_part = np.cos(angles), np.sin(angles)
    return np.concatenate([cos_part] * 4, axis=1), np.concatenate([-sin_part, sin_part] * 2, axis=1)


def rotate(u, cos_part, sin_part):
    lane = lax.broadcasted_iota(i32, u.shape, 1)
    swapped = jnp.where(lane % ROPE < ROPE // 2, pltpu.roll(u, 96, 1), pltpu.roll(u, 32, 1))
    return u * cos_part + swapped * sin_part


def split_heads(u):
    a, b, c = u[:, :NOPE], u[:, NOPE : 2 * NOPE], u[:, 2 * NOPE :]
    low = lax.broadcasted_iota(i32, a.shape, 1) < ROPE
    return a, jnp.where(low, pltpu.roll(b, ROPE, 1), pltpu.roll(c, ROPE, 1)), jnp.where(low, b, c)


def spread(a, axes, count):
    copies = jnp.broadcast_to(a[None], (count,) + a.shape)
    return lax.all_to_all(copies, axes, 0, 0, tiled=True)


def shift(count, d):
    return [(i, (i + d) % count) for i in range(count)]


def dot_t(a, b):
    return lax.dot_general(a, b, (((1,), (1,)), ((), ())), preferred_element_type=f32)


def layout_kernel(ids_ref, req_ref, slot_ref, out_ref):
    rep, x, yh, yz = ids_ref[0], ids_ref[1], ids_ref[2], ids_ref[3]
    lengths = [req_ref[rep, r] for r in range(NREQ)]
    starts = [0, lengths[0], lengths[0] + lengths[1]]

    def start_of(block):
        return jnp.where(block >= starts[2], starts[2], jnp.where(block >= starts[1], starts[1], 0))

    for r in range(NREQ):
        out_ref[START + r] = starts[r] * BLK
        out_ref[LENGTH + r] = lengths[r] * BLK
        slot = slot_ref[0, rep * NREQ + r]
        out_ref[SLOT + r] = (lax.div(slot, NREQ) ^ rep) * NREQ + lax.rem(slot, NREQ)
        source = 0
        for m in range(NREP * NREQ):
            source += jnp.where(slot_ref[0, m] == rep * NREQ + r, m, 0)
        out_ref[SOURCE + r] = lax.div(source, NREQ) * PAD + lax.rem(source, NREQ) * STEPS
    out_ref[BASE] = x * 2 * BLK + yz * PAD - start_of(x * 2 + lax.div(yz, 8)) * BLK
    for i in range(8):
        out_ref[PLACE + i] = i - start_of(i)
        out_ref[FIRST + i] = start_of(i) * BLK
        out_ref[BLOCK + i] = (yh ^ (i // NX)) * NX + lax.rem(x + NX - i % NX, NX)


SMEM = pl.BlockSpec(memory_space=pltpu.SMEM)
VMEM = pl.BlockSpec(memory_space=pltpu.VMEM)


def request_layout(ids, req_blocks, dest_slot):
    return pl.pallas_call(
        layout_kernel,
        in_specs=[SMEM] * 3,
        out_specs=SMEM,
        out_shape=jax.ShapeDtypeStruct((64,), i32),
        cost_estimate=pl.CostEstimate(flops=1000, bytes_accessed=1000, transcendentals=0),
        name="request_layout",
    )(ids, req_blocks, dest_slot)


def pack_kernel(hidden_ref, down_ref, out_ref):
    per_x = hidden_ref.shape[1] // NX
    for i in range(NX):
        out_ref[i, :, :per_x] = hidden_ref[:, i * per_x : (i + 1) * per_x]
        out_ref[i, :, per_x:] = down_ref[...]


def pack(hidden_t, kv_down):
    features, rows = hidden_t.shape
    return pl.pallas_call(
        pack_kernel,
        in_specs=[VMEM] * 2,
        out_specs=VMEM,
        out_shape=jax.ShapeDtypeStruct((NX, features, rows // NX + kv_down.shape[1]), bf16),
        cost_estimate=pl.CostEstimate(flops=0, bytes_accessed=1_200_000, transcendentals=0),
        name="pack_hidden",
    )(hidden_t, kv_down)


def norm_kernel(layout_ref, pieces_ref, gain_ref, cos_ref, sin_ref, out_ref):
    latent = jnp.sum(pieces_ref[...], axis=0)
    content = latent[:, :KVL]
    scale = lax.rsqrt(jnp.mean(content * content, axis=1, keepdims=True) + 1e-06)
    content = (content * scale * gain_ref[...]).astype(bf16)
    at = pl.ds(pl.multiple_of(layout_ref[BASE], PAD), latent.shape[0])
    pe = jnp.concatenate([latent[:, KVL:]] * 2, axis=1)
    pe = rotate(pe, cos_ref[at, :], sin_ref[at, :]).astype(bf16)
    for i in range(out_ref.shape[0]):
        out_ref[i, :, :KVL] = content
        out_ref[i, :, KVL:] = pe


def norm_rows(layout, pieces, gain, cos_part, sin_part):
    count, chunk, _ = pieces.shape
    return pl.pallas_call(
        norm_kernel,
        in_specs=[SMEM] + [VMEM] * 4,
        out_specs=VMEM,
        out_shape=jax.ShapeDtypeStruct((count, chunk, WIDE), bf16),
        cost_estimate=pl.CostEstimate(flops=NORM_FLOPS, bytes_accessed=1_000_000, transcendentals=16),
        name="norm_rows",
    )(layout, pieces, gain, cos_part, sin_part)


def query_kernel(layout_ref, cq_ref, w_ref, cos_ref, sin_ref, out_ref):
    rows = cq_ref[...].reshape(BLK, -1)
    u = jnp.dot(rows, w_ref[...], preferred_element_type=f32)
    first, second, pe = split_heads(u)
    pe = rotate(pe, cos_ref[...], sin_ref[...])
    low = lax.broadcasted_iota(i32, pe.shape, 1) < ROPE
    out_ref[0, :, :NOPE] = first.astype(bf16)
    out_ref[0, :, NOPE:] = jnp.where(low, pe, 0.0).astype(bf16)
    out_ref[1, :, :NOPE] = second.astype(bf16)
    out_ref[1, :, NOPE:] = jnp.where(low, 0.0, pe).astype(bf16)


def project_queries(layout, cq, weights, cos_part, sin_part):
    width = cq.shape[-1]
    table = pl.BlockSpec((BLK, 2 * ROPE), lambda i, place: (place[PLACE + i], 0))
    return pl.pallas_call(
        query_kernel,
        grid_spec=pltpu.PrefetchScalarGridSpec(
            num_scalar_prefetch=1,
            grid=(8,),
            in_specs=[
                pl.BlockSpec((8, 1, PAD, width), lambda i, place: (0, place[BLOCK + i], 0, 0)),
                pl.BlockSpec(weights.shape, lambda i, place: (0, 0)),
                table,
                table,
            ],
            out_specs=pl.BlockSpec((HEADS, BLK, 2 * NOPE), lambda i, place: (0, i, 0)),
        ),
        out_shape=jax.ShapeDtypeStruct((HEADS, 8 * BLK, 2 * NOPE), bf16),
        compiler_params=pltpu.CompilerParams(vmem_limit_bytes=VMEM_LIMIT),
        cost_estimate=pl.CostEstimate(flops=1_200_000_000, bytes_accessed=5_000_000, transcendentals=0),
        name="project_queries",
    )(layout, cq, weights, cos_part, sin_part)


def prepare_kernel(layout_ref, rows_ref, w_ref, kv_ref, cos_ref, sin_ref, out_ref, in_ref, cos_at, sin_at):
    query_latent = w_ref.shape[0]
    in_ref[...] = jnp.zeros_like(in_ref)
    cos_at[...] = jnp.zeros_like(cos_at)
    sin_at[...] = jnp.zeros_like(sin_at)
    for r in range(NREQ):
        here = slice(r * STEPS, (r + 1) * STEPS)
        in_ref[here, :] = rows_ref[layout_ref[SLOT + r]].astype(f32)
        at = pl.ds(pl.multiple_of(layout_ref[LENGTH + r], BLK), 8)
        cos_at[here, :] = cos_ref[at, :][:STEPS]
        sin_at[here, :] = sin_ref[at, :][:STEPS]
    cos_part, sin_part = cos_at[...], sin_at[...]
    rows = in_ref[:, :query_latent].astype(bf16)
    u = jnp.dot(rows, w_ref[...], preferred_element_type=f32).astype(bf16).astype(f32)
    first, second, pe = split_heads(u)
    pe = rotate(pe, cos_part, sin_part)
    low = lax.broadcasted_iota(i32, pe.shape, 1) < ROPE
    for h, plain in enumerate((first, second)):
        here = slice(h * PAD, (h + 1) * PAD)
        base = h * (NOPE + VD)
        out_ref[here, :KVL] = dot_t(plain.astype(bf16), kv_ref[:, base : base + NOPE]).astype(bf16)
        out_ref[here, KVL:] = jnp.where(low == (h == 0), pe, 0.0).astype(bf16)
    new = slice(HEADS * PAD, (HEADS + 1) * PAD)
    out_ref[new, :KVL] = in_ref[:, query_latent : query_latent + KVL].astype(bf16)
    new_pe = jnp.concatenate([in_ref[:, query_latent + KVL :]] * 2, axis=1)
    out_ref[new, KVL:] = rotate(new_pe, cos_part, sin_part).astype(bf16)


def prepare_decode(layout, rows, q_up, kv_up, cos_part, sin_part):
    return pl.pallas_call(
        prepare_kernel,
        in_specs=[SMEM] + [VMEM] * 5,
        out_specs=VMEM,
        out_shape=jax.ShapeDtypeStruct(((HEADS + 1) * PAD, WIDE), bf16),
        scratch_shapes=[
            pltpu.VMEM((PAD, rows.shape[-1]), f32),
            pltpu.VMEM((PAD, 2 * ROPE), f32),
            pltpu.VMEM((PAD, 2 * ROPE), f32),
        ],
        compiler_params=pltpu.CompilerParams(vmem_limit_bytes=VMEM_LIMIT),
        cost_estimate=pl.CostEstimate(flops=30_000_000, bytes_accessed=2_500_000, transcendentals=0),
        name="prepare_decode",
    )(layout, rows, q_up, kv_up, cos_part, sin_part)


def decode_kernel(layout_ref, ready_ref, cache_ref, kv_ref, out_ref):
    query = ready_ref[: HEADS * PAD, :]
    fresh = ready_ref[HEADS * PAD :, :]
    old = dot_t(query, cache_ref[...]) * SIGMA
    new = dot_t(query, fresh) * SIGMA
    request = lax.broadcasted_iota(i32, (HEADS * PAD, 1), 0) % PAD // STEPS

    def per_request(values):
        return jnp.where(request == 0, values[0], jnp.where(request == 1, values[1], values[2]))

    low = per_request([layout_ref[START + r] for r in range(NREQ)])
    high = per_request([layout_ref[START + r] + layout_ref[LENGTH + r] for r in range(NREQ)])
    column = lax.broadcasted_iota(i32, old.shape, 1)
    old = jnp.where((column >= low) & (column < high), old, -1e30)
    step = lax.broadcasted_iota(i32, new.shape, 0) % PAD
    other = lax.broadcasted_iota(i32, new.shape, 1)
    new = jnp.where((step // STEPS == other // STEPS) & (other <= step), new, -1e30)
    top = jnp.maximum(jnp.max(old, axis=1, keepdims=True), jnp.max(new, axis=1, keepdims=True))
    old = jnp.exp(old - top)
    new = jnp.exp(new - top)
    inverse = 1.0 / (jnp.sum(old, axis=1, keepdims=True) + jnp.sum(new, axis=1, keepdims=True))
    old = (old * inverse).astype(bf16)
    new = (new * inverse).astype(bf16)
    mixture = (
        jnp.dot(old, cache_ref[:, :KVL], preferred_element_type=f32)
        + jnp.dot(new, fresh[:, :KVL], preferred_element_type=f32)
    ).astype(bf16)
    for h in range(HEADS):
        base = h * (NOPE + VD) + NOPE
        value = jnp.dot(
            mixture[h * PAD : (h + 1) * PAD], kv_ref[:, base : base + VD], preferred_element_type=f32
        ).astype(bf16)
        for i in range(NREP):
            out_ref[i, :, h * VD : (h + 1) * VD] = value


def decode(layout, ready, cache, kv_up):
    return pl.pallas_call(
        decode_kernel,
        in_specs=[SMEM] + [VMEM] * 3,
        out_specs=VMEM,
        out_shape=jax.ShapeDtypeStruct((NREP, PAD, HEADS * VD), bf16),
        compiler_params=pltpu.CompilerParams(vmem_limit_bytes=VMEM_LIMIT),
        cost_estimate=pl.CostEstimate(flops=100_000_000, bytes_accessed=2_000_000, transcendentals=40_000),
        name="decode_attention",
    )(layout, ready, cache, kv_up)


def select_kernel(layout_ref, pool_ref, out_ref):
    pool = pool_ref[...].reshape(NREP * PAD, -1)
    for r in range(NREQ):
        row = lax.broadcasted_iota(i32, (8, NREP * PAD), 0)
        column = lax.broadcasted_iota(i32, (8, NREP * PAD), 1)
        pick = jnp.where(column == layout_ref[SOURCE + r] + row, 1.0, 0.0).astype(bf16)
        out_ref[r] = jnp.dot(pick, pool, preferred_element_type=f32)[:STEPS].astype(bf16)


def select(layout, pool):
    return pl.pallas_call(
        select_kernel,
        in_specs=[SMEM, VMEM],
        out_specs=VMEM,
        out_shape=jax.ShapeDtypeStruct((NREQ, STEPS, HEADS * VD), bf16),
        cost_estimate=pl.CostEstimate(flops=1_000_000, bytes_accessed=50_000, transcendentals=0),
        name="select_slots",
    )(layout, pool)


def prefill_kernel(layout_ref, q_ref, cache_ref, kv_ref, out_ref, key_ref, value_ref):
    for j in range(4):
        rows = slice(j * 2 * BLK, (j + 1) * 2 * BLK)
        wide = jnp.dot(cache_ref[rows, :KVL], kv_ref[...], preferred_element_type=f32).astype(bf16)
        for h in range(HEADS):
            base = h * (NOPE + VD)
            key_ref[h, rows, :NOPE] = wide[:, base : base + NOPE]
            key_ref[h, rows, NOPE:] = cache_ref[rows, KVL:]
            value_ref[h, rows, :] = wide[:, base + NOPE : base + NOPE + VD]
    for i in range(8):
        first = max(0, i - REACH + 1) * BLK
        last = (i + 1) * BLK
        shape = (BLK, last - first)
        column = lax.broadcasted_iota(i32, shape, 1) + first
        row = lax.broadcasted_iota(i32, shape, 0) + i * BLK
        ok = (column >= layout_ref[FIRST + i]) & (column <= row)
        scores = [
            dot_t(q_ref[h, i * BLK : last, :], key_ref[h, first:last, :]) * SIGMA for h in range(HEADS)
        ]
        scores = [jnp.where(ok, s, -1e30) for s in scores]
        weights = [jnp.exp(s - jnp.max(s, axis=1, keepdims=True)) for s in scores]
        weights = [(w * (1.0 / jnp.sum(w, axis=1, keepdims=True))).astype(bf16) for w in weights]
        for h in range(HEADS):
            out_ref[i * BLK : last, h * VD : (h + 1) * VD] = jnp.dot(
                weights[h], value_ref[h, first:last, :], preferred_element_type=f32
            ).astype(bf16)


def prefill(layout, queries, cache, kv_up):
    rows = cache.shape[0]
    return pl.pallas_call(
        prefill_kernel,
        in_specs=[SMEM] + [VMEM] * 3,
        out_specs=VMEM,
        out_shape=jax.ShapeDtypeStruct((rows, HEADS * VD), bf16),
        scratch_shapes=[
            pltpu.VMEM((HEADS, rows, 2 * NOPE), bf16),
            pltpu.VMEM((HEADS, rows, VD), bf16),
        ],
        compiler_params=pltpu.CompilerParams(vmem_limit_bytes=VMEM_LIMIT),
        cost_estimate=pl.CostEstimate(flops=1_500_000_000, bytes_accessed=4_000_000, transcendentals=1_000_000),
        name="prefill_attention",
    )(layout, queries, cache, kv_up)


def body(hidden, comp_query, kv_down, kv_gain, q_up, kv_up, req_blocks, dest_slot, dec_query, dec_latent):
    ids = jnp.stack(
        [lax.axis_index("rep"), lax.axis_index("x"), lax.axis_index("yh"), lax.axis_index(("yh", "z"))]
    ).astype(i32)
    rows, features = hidden.shape[1:]
    per_x = rows // NX
    chunk = per_x // 16
    cos_part, sin_part = rotary_table()

    own = comp_query[0]
    packed = lax.all_to_all(pack(hidden[0].T, kv_down), "x", 0, 0, tiled=True)
    layout = request_layout(ids, req_blocks, dest_slot)
    line = jnp.concatenate([own] + [lax.ppermute(own, "x", shift(NX, d)) for d in range(1, NX)])
    packed, line, dec_query, dec_latent = lax.optimization_barrier((packed, line, dec_query, dec_latent))
    line = jnp.concatenate([line, lax.ppermute(line, "yh", shift(2, 1))])
    cq = lax.all_gather(line, "z", axis=0, tiled=True)

    packed = packed.reshape(NX * features, -1)
    partial = lax.dot_general(
        packed[:, :per_x], packed[:, per_x:], (((0,), (0,)), ((), ())), preferred_element_type=f32
    )
    pieces = lax.all_to_all(partial.reshape(16, chunk, -1), ("yh", "z"), 0, 0, tiled=True)
    copies = norm_rows(layout, pieces, kv_gain[None, :], cos_part, sin_part)
    cache = lax.all_to_all(copies, ("yh", "z"), 0, 0, tiled=True).reshape(per_x, -1)

    rep_in = jnp.concatenate([dec_query, dec_latent], axis=2)
    for d in (1, 2):
        met = lax.ppermute(rep_in, "rep", [(i, i ^ d) for i in range(NREP)])
        rep_in = jnp.concatenate([rep_in, met])
    ready = prepare_decode(layout, rep_in, q_up, kv_up, cos_part, sin_part)
    cache, ready = lax.optimization_barrier((cache, ready))
    cache = spread(cache, "x", NX).reshape(rows, -1)

    queries = project_queries(layout, cq.reshape(8, 8, PAD, -1), q_up, cos_part, sin_part)
    cache, queries = lax.optimization_barrier((cache, queries))
    result = decode(layout, ready, cache, kv_up)
    pool = lax.all_to_all(result, "rep", 0, 0, tiled=True)
    prefill_out = prefill(layout, queries, cache, kv_up)[None]
    pool, prefill_out = lax.optimization_barrier((pool, prefill_out))
    return prefill_out, select(layout, pool)


def solution(mesh):
    fine = Mesh(mesh.devices.reshape(2, 2, 4, 8, 4), ("section", "yh", "x", "z", "rep"))
    tp = ("yh", "x", "z")
    group = ("section", "rep")
    in_specs = (
        P(group, None, tp),
        P(group, tp, None),
        P(tp, None),
        P(),
        P(None, tp),
        P(None, tp),
        P("section", None),
        P("section", None),
        P(group, None, None),
        P(group, None, None),
    )
    out_specs = (P(group, None, tp), P(group, None, tp))
    return jax.shard_map(body, mesh=fine, in_specs=in_specs, out_specs=out_specs, check_vma=False)
```

```python
import math

import jax
import jax.numpy as jnp
import numpy as np
from jax import lax
from jax.experimental import pallas as pl
from jax.experimental.pallas import tpu as pltpu
from jax.sharding import Mesh, PartitionSpec as P

KVL = 512
NOPE = 128
ROPE = 64
VD = 128
BLK = 128
NREQ = 3
STEPS = 4
REACH = 4
NREP = 4
NX = 4
HEADS = 2
PAD = 16
TABLE = 640
NORM_FLOPS = 30_000_000_000
WIDE = KVL + 2 * ROPE
START, LENGTH, BASE, PLACE, FIRST, SOURCE, SLOT, HALF, LINE = 0, 3, 6, 8, 16, 24, 28, 32, 40

SIGMA = (1.0 + 0.1 * math.log(40.0)) ** 2 * (NOPE + ROPE) ** (-0.5)
bf16 = jnp.bfloat16
f32 = jnp.float32
i32 = jnp.int32


def rotary_table():
    half = ROPE // 2
    frequency = np.float32(10000.0) ** (-np.arange(half, dtype=np.float32) * np.float32(2.0 / ROPE))
    angles = np.arange(TABLE, dtype=np.float32)[:, None] * frequency.astype(np.float32)
    cos_part, sin_part = np.cos(angles), np.sin(angles)
    return np.concatenate([cos_part] * 4, axis=1), np.concatenate([-sin_part, sin_part] * 2, axis=1)


def rotate(u, cos_part, sin_part):
    lane = lax.broadcasted_iota(i32, u.shape, 1)
    swapped = jnp.where(lane % ROPE < ROPE // 2, pltpu.roll(u, 96, 1), pltpu.roll(u, 32, 1))
    return u * cos_part + swapped * sin_part


def split_heads(u):
    a, b, c = u[:, :NOPE], u[:, NOPE : 2 * NOPE], u[:, 2 * NOPE :]
    low = lax.broadcasted_iota(i32, a.shape, 1) < ROPE
    return a, jnp.where(low, pltpu.roll(b, ROPE, 1), pltpu.roll(c, ROPE, 1)), jnp.where(low, b, c)


def spread(a, axes, count):
    copies = jnp.broadcast_to(a[None], (count,) + a.shape)
    return lax.all_to_all(copies, axes, 0, 0, tiled=True)


def shift(count, d):
    return [(i, (i + d) % count) for i in range(count)]


def dot_t(a, b):
    return lax.dot_general(a, b, (((1,), (1,)), ((), ())), preferred_element_type=f32)


def layout_kernel(ids_ref, req_ref, slot_ref, out_ref):
    rep, x, yh, yz = ids_ref[0], ids_ref[1], ids_ref[2], ids_ref[3]
    lengths = [req_ref[rep, r] for r in range(NREQ)]
    starts = [0, lengths[0], lengths[0] + lengths[1]]

    def start_of(block):
        return jnp.where(block >= starts[2], starts[2], jnp.where(block >= starts[1], starts[1], 0))

    for r in range(NREQ):
        out_ref[START + r] = starts[r] * BLK
        out_ref[LENGTH + r] = lengths[r] * BLK
        slot = slot_ref[0, rep * NREQ + r]
        out_ref[SLOT + r] = (lax.div(slot, NREQ) ^ rep) * NREQ + lax.rem(slot, NREQ)
        source = 0
        for m in range(NREP * NREQ):
            source += jnp.where(slot_ref[0, m] == rep * NREQ + r, m, 0)
        out_ref[SOURCE + r] = lax.div(source, NREQ) * PAD + lax.rem(source, NREQ) * STEPS
    for j in range(2):
        out_ref[HALF + j] = yh ^ j
    for d in range(NX):
        out_ref[LINE + d] = lax.rem(x + NX - d, NX)
    out_ref[BASE] = x * 2 * BLK + yz * PAD - start_of(x * 2 + lax.div(yz, 8)) * BLK
    for i in range(8):
        out_ref[PLACE + i] = i - start_of(i)
        out_ref[FIRST + i] = start_of(i) * BLK


SMEM = pl.BlockSpec(memory_space=pltpu.SMEM)
VMEM = pl.BlockSpec(memory_space=pltpu.VMEM)


def request_layout(ids, req_blocks, dest_slot):
    return pl.pallas_call(
        layout_kernel,
        in_specs=[SMEM] * 3,
        out_specs=SMEM,
        out_shape=jax.ShapeDtypeStruct((64,), i32),
        cost_estimate=pl.CostEstimate(flops=1000, bytes_accessed=1000, transcendentals=0),
        name="request_layout",
    )(ids, req_blocks, dest_slot)


def pack_kernel(hidden_ref, down_ref, out_ref):
    per_x = hidden_ref.shape[1] // NX
    for i in range(NX):
        out_ref[i, :, :per_x] = hidden_ref[:, i * per_x : (i + 1) * per_x]
        out_ref[i, :, per_x:] = down_ref[...]


def pack(hidden_t, kv_down):
    features, rows = hidden_t.shape
    return pl.pallas_call(
        pack_kernel,
        in_specs=[VMEM] * 2,
        out_specs=VMEM,
        out_shape=jax.ShapeDtypeStruct((NX, features, rows // NX + kv_down.shape[1]), bf16),
        cost_estimate=pl.CostEstimate(flops=0, bytes_accessed=1_200_000, transcendentals=0),
        name="pack_hidden",
    )(hidden_t, kv_down)


def norm_kernel(layout_ref, pieces_ref, gain_ref, cos_ref, sin_ref, out_ref):
    latent = jnp.sum(pieces_ref[...], axis=0)
    content = latent[:, :KVL]
    scale = lax.rsqrt(jnp.mean(content * content, axis=1, keepdims=True) + 1e-06)
    content = (content * scale * gain_ref[...]).astype(bf16)
    at = pl.ds(pl.multiple_of(layout_ref[BASE], PAD), latent.shape[0])
    pe = jnp.concatenate([latent[:, KVL:]] * 2, axis=1)
    pe = rotate(pe, cos_ref[at, :], sin_ref[at, :]).astype(bf16)
    for i in range(out_ref.shape[0]):
        out_ref[i, :, :KVL] = content
        out_ref[i, :, KVL:] = pe


def norm_rows(layout, pieces, gain, cos_part, sin_part):
    count, chunk, _ = pieces.shape
    return pl.pallas_call(
        norm_kernel,
        in_specs=[SMEM] + [VMEM] * 4,
        out_specs=VMEM,
        out_shape=jax.ShapeDtypeStruct((count, chunk, WIDE), bf16),
        cost_estimate=pl.CostEstimate(flops=NORM_FLOPS, bytes_accessed=1_000_000, transcendentals=16),
        name="norm_rows",
    )(layout, pieces, gain, cos_part, sin_part)


def query_kernel(layout_ref, cq_ref, w_ref, cos_ref, sin_ref, out_ref):
    half = pl.program_id(0)
    rows = jnp.concatenate([cq_ref[:, d].reshape(BLK, -1) for d in range(NX)])
    u = jnp.dot(rows, w_ref[...], preferred_element_type=f32)
    first, second, pe = split_heads(u)
    low = lax.broadcasted_iota(i32, (BLK, 2 * ROPE), 1) < ROPE
    for d in range(NX):
        here = slice(d * BLK, (d + 1) * BLK)
        line = layout_ref[LINE + d]
        to = pl.ds(pl.multiple_of(line * BLK, BLK), BLK)
        at = pl.ds(pl.multiple_of(layout_ref[PLACE + half * NX + line] * BLK, BLK), BLK)
        turned = rotate(pe[here], cos_ref[at, :], sin_ref[at, :])
        out_ref[0, to, :NOPE] = first[here].astype(bf16)
        out_ref[0, to, NOPE:] = jnp.where(low, turned, 0.0).astype(bf16)
        out_ref[1, to, :NOPE] = second[here].astype(bf16)
        out_ref[1, to, NOPE:] = jnp.where(low, 0.0, turned).astype(bf16)


def project_queries(layout, cq, weights, cos_part, sin_part):
    width = cq.shape[-1]
    table = pl.BlockSpec(cos_part.shape, lambda j, place: (0, 0))
    return pl.pallas_call(
        query_kernel,
        grid_spec=pltpu.PrefetchScalarGridSpec(
            num_scalar_prefetch=1,
            grid=(2,),
            in_specs=[
                pl.BlockSpec((8, NX, PAD, width), lambda j, place: (0, place[HALF + j], 0, 0)),
                pl.BlockSpec(weights.shape, lambda j, place: (0, 0)),
                table,
                table,
            ],
            out_specs=pl.BlockSpec((HEADS, NX * BLK, 2 * NOPE), lambda j, place: (0, j, 0)),
        ),
        out_shape=jax.ShapeDtypeStruct((HEADS, 8 * BLK, 2 * NOPE), bf16),
        compiler_params=pltpu.CompilerParams(vmem_limit_bytes=60 * 1024 * 1024),
        cost_estimate=pl.CostEstimate(flops=1_200_000_000, bytes_accessed=5_000_000, transcendentals=0),
        name="project_queries",
    )(layout, cq, weights, cos_part, sin_part)


def prepare_kernel(layout_ref, rows_ref, w_ref, kv_ref, cos_ref, sin_ref, out_ref, in_ref, cos_at, sin_at):
    query_latent = w_ref.shape[0]
    in_ref[...] = jnp.zeros_like(in_ref)
    cos_at[...] = jnp.zeros_like(cos_at)
    sin_at[...] = jnp.zeros_like(sin_at)
    for r in range(NREQ):
        here = slice(r * STEPS, (r + 1) * STEPS)
        in_ref[here, :] = rows_ref[layout_ref[SLOT + r]].astype(f32)
        at = pl.ds(pl.multiple_of(layout_ref[LENGTH + r], BLK), 8)
        cos_at[here, :] = cos_ref[at, :][:STEPS]
        sin_at[here, :] = sin_ref[at, :][:STEPS]
    cos_part, sin_part = cos_at[...], sin_at[...]
    rows = in_ref[:, :query_latent].astype(bf16)
    u = jnp.dot(rows, w_ref[...], preferred_element_type=f32).astype(bf16).astype(f32)
    first, second, pe = split_heads(u)
    pe = rotate(pe, cos_part, sin_part)
    low = lax.broadcasted_iota(i32, pe.shape, 1) < ROPE
    for h, plain in enumerate((first, second)):
        here = slice(h * PAD, (h + 1) * PAD)
        base = h * (NOPE + VD)
        out_ref[here, :KVL] = dot_t(plain.astype(bf16), kv_ref[:, base : base + NOPE]).astype(bf16)
        out_ref[here, KVL:] = jnp.where(low == (h == 0), pe, 0.0).astype(bf16)
    new = slice(HEADS * PAD, (HEADS + 1) * PAD)
    out_ref[new, :KVL] = in_ref[:, query_latent : query_latent + KVL].astype(bf16)
    new_pe = jnp.concatenate([in_ref[:, query_latent + KVL :]] * 2, axis=1)
    out_ref[new, KVL:] = rotate(new_pe, cos_part, sin_part).astype(bf16)


def prepare_decode(layout, rows, q_up, kv_up, cos_part, sin_part):
    return pl.pallas_call(
        prepare_kernel,
        in_specs=[SMEM] + [VMEM] * 5,
        out_specs=VMEM,
        out_shape=jax.ShapeDtypeStruct(((HEADS + 1) * PAD, WIDE), bf16),
        scratch_shapes=[
            pltpu.VMEM((PAD, rows.shape[-1]), f32),
            pltpu.VMEM((PAD, 2 * ROPE), f32),
            pltpu.VMEM((PAD, 2 * ROPE), f32),
        ],
        compiler_params=pltpu.CompilerParams(vmem_limit_bytes=16 * 1024 * 1024),
        cost_estimate=pl.CostEstimate(flops=30_000_000, bytes_accessed=2_500_000, transcendentals=0),
        name="prepare_decode",
    )(layout, rows, q_up, kv_up, cos_part, sin_part)


def decode_kernel(layout_ref, ready_ref, cache_ref, kv_ref, out_ref):
    query = ready_ref[: HEADS * PAD, :]
    fresh = ready_ref[HEADS * PAD :, :]
    old = dot_t(query, cache_ref[...]) * SIGMA
    new = dot_t(query, fresh) * SIGMA
    request = lax.broadcasted_iota(i32, (HEADS * PAD, 1), 0) % PAD // STEPS

    def per_request(values):
        return jnp.where(request == 0, values[0], jnp.where(request == 1, values[1], values[2]))

    low = per_request([layout_ref[START + r] for r in range(NREQ)])
    high = per_request([layout_ref[START + r] + layout_ref[LENGTH + r] for r in range(NREQ)])
    column = lax.broadcasted_iota(i32, old.shape, 1)
    old = jnp.where((column >= low) & (column < high), old, -1e30)
    step = lax.broadcasted_iota(i32, new.shape, 0) % PAD
    other = lax.broadcasted_iota(i32, new.shape, 1)
    new = jnp.where((step // STEPS == other // STEPS) & (other <= step), new, -1e30)
    top = jnp.maximum(jnp.max(old, axis=1, keepdims=True), jnp.max(new, axis=1, keepdims=True))
    old = jnp.exp(old - top)
    new = jnp.exp(new - top)
    inverse = 1.0 / (jnp.sum(old, axis=1, keepdims=True) + jnp.sum(new, axis=1, keepdims=True))
    old = (old * inverse).astype(bf16)
    new = (new * inverse).astype(bf16)
    mixture = (
        jnp.dot(old, cache_ref[:, :KVL], preferred_element_type=f32)
        + jnp.dot(new, fresh[:, :KVL], preferred_element_type=f32)
    ).astype(bf16)
    for h in range(HEADS):
        base = h * (NOPE + VD) + NOPE
        value = jnp.dot(
            mixture[h * PAD : (h + 1) * PAD], kv_ref[:, base : base + VD], preferred_element_type=f32
        ).astype(bf16)
        for i in range(NREP):
            out_ref[i, :, h * VD : (h + 1) * VD] = value


def decode(layout, ready, cache, kv_up):
    return pl.pallas_call(
        decode_kernel,
        in_specs=[SMEM] + [VMEM] * 3,
        out_specs=VMEM,
        out_shape=jax.ShapeDtypeStruct((NREP, PAD, HEADS * VD), bf16),
        compiler_params=pltpu.CompilerParams(vmem_limit_bytes=16 * 1024 * 1024),
        cost_estimate=pl.CostEstimate(flops=100_000_000, bytes_accessed=2_000_000, transcendentals=40_000),
        name="decode_attention",
    )(layout, ready, cache, kv_up)


def select_kernel(layout_ref, pool_ref, out_ref):
    pool = pool_ref[...].reshape(NREP * PAD, -1)
    for r in range(NREQ):
        row = lax.broadcasted_iota(i32, (8, NREP * PAD), 0)
        column = lax.broadcasted_iota(i32, (8, NREP * PAD), 1)
        pick = jnp.where(column == layout_ref[SOURCE + r] + row, 1.0, 0.0).astype(bf16)
        out_ref[r] = jnp.dot(pick, pool, preferred_element_type=f32)[:STEPS].astype(bf16)


def select(layout, pool):
    return pl.pallas_call(
        select_kernel,
        in_specs=[SMEM, VMEM],
        out_specs=VMEM,
        out_shape=jax.ShapeDtypeStruct((NREQ, STEPS, HEADS * VD), bf16),
        cost_estimate=pl.CostEstimate(flops=1_000_000, bytes_accessed=50_000, transcendentals=0),
        name="select_slots",
    )(layout, pool)


def prefill_kernel(layout_ref, q_ref, cache_ref, kv_ref, out_ref, key_ref, value_ref):
    for j in range(4):
        rows = slice(j * 2 * BLK, (j + 1) * 2 * BLK)
        wide = jnp.dot(cache_ref[rows, :KVL], kv_ref[...], preferred_element_type=f32).astype(bf16)
        for h in range(HEADS):
            base = h * (NOPE + VD)
            key_ref[h, rows, :NOPE] = wide[:, base : base + NOPE]
            key_ref[h, rows, NOPE:] = cache_ref[rows, KVL:]
            value_ref[h, rows, :] = wide[:, base + NOPE : base + NOPE + VD]
    for i in range(8):
        first = max(0, i - REACH + 1) * BLK
        last = (i + 1) * BLK
        shape = (BLK, last - first)
        column = lax.broadcasted_iota(i32, shape, 1) + first
        row = lax.broadcasted_iota(i32, shape, 0) + i * BLK
        ok = (column >= layout_ref[FIRST + i]) & (column <= row)
        scores = [
            dot_t(q_ref[h, i * BLK : last, :], key_ref[h, first:last, :]) * SIGMA for h in range(HEADS)
        ]
        scores = [jnp.where(ok, s, -1e30) for s in scores]
        weights = [jnp.exp(s - jnp.max(s, axis=1, keepdims=True)) for s in scores]
        weights = [(w * (1.0 / jnp.sum(w, axis=1, keepdims=True))).astype(bf16) for w in weights]
        for h in range(HEADS):
            out_ref[i * BLK : last, h * VD : (h + 1) * VD] = jnp.dot(
                weights[h], value_ref[h, first:last, :], preferred_element_type=f32
            ).astype(bf16)


def prefill(layout, queries, cache, kv_up):
    rows = cache.shape[0]
    return pl.pallas_call(
        prefill_kernel,
        in_specs=[SMEM] + [VMEM] * 3,
        out_specs=VMEM,
        out_shape=jax.ShapeDtypeStruct((rows, HEADS * VD), bf16),
        scratch_shapes=[
            pltpu.VMEM((HEADS, rows, 2 * NOPE), bf16),
            pltpu.VMEM((HEADS, rows, VD), bf16),
        ],
        compiler_params=pltpu.CompilerParams(vmem_limit_bytes=32 * 1024 * 1024),
        cost_estimate=pl.CostEstimate(flops=1_500_000_000, bytes_accessed=4_000_000, transcendentals=1_000_000),
        name="prefill_attention",
    )(layout, queries, cache, kv_up)


def body(hidden, comp_query, kv_down, kv_gain, q_up, kv_up, req_blocks, dest_slot, dec_query, dec_latent):
    ids = jnp.stack(
        [lax.axis_index("rep"), lax.axis_index("x"), lax.axis_index("yh"), lax.axis_index(("yh", "z"))]
    ).astype(i32)
    rows, features = hidden.shape[1:]
    per_x = rows // NX
    chunk = per_x // 16
    cos_part, sin_part = rotary_table()

    own = comp_query[0]
    packed = lax.all_to_all(pack(hidden[0].T, kv_down), "x", 0, 0, tiled=True)
    layout = request_layout(ids, req_blocks, dest_slot)
    line = jnp.concatenate([own] + [lax.ppermute(own, "x", shift(NX, d)) for d in range(1, NX)])
    packed, line, dec_query, dec_latent = lax.optimization_barrier((packed, line, dec_query, dec_latent))
    line = jnp.concatenate([line, lax.ppermute(line, "yh", shift(2, 1))])
    cq = lax.all_gather(line, "z", axis=0, tiled=True)

    packed = packed.reshape(NX * features, -1)
    partial = lax.dot_general(
        packed[:, :per_x], packed[:, per_x:], (((0,), (0,)), ((), ())), preferred_element_type=f32
    )
    pieces = lax.all_to_all(partial.reshape(16, chunk, -1), ("yh", "z"), 0, 0, tiled=True)
    copies = norm_rows(layout, pieces, kv_gain[None, :], cos_part, sin_part)
    cache = lax.all_to_all(copies, ("yh", "z"), 0, 0, tiled=True).reshape(per_x, -1)

    rep_in = jnp.concatenate([dec_query, dec_latent], axis=2)
    for d in (1, 2):
        met = lax.ppermute(rep_in, "rep", [(i, i ^ d) for i in range(NREP)])
        rep_in = jnp.concatenate([rep_in, met])
    ready = prepare_decode(layout, rep_in, q_up, kv_up, cos_part, sin_part)
    cache, ready = lax.optimization_barrier((cache, ready))
    cache = spread(cache, "x", NX).reshape(rows, -1)

    queries = project_queries(layout, cq.reshape(8, 8, PAD, -1), q_up, cos_part, sin_part)
    cache, queries = lax.optimization_barrier((cache, queries))
    result = decode(layout, ready, cache, kv_up)
    pool = lax.all_to_all(result, "rep", 0, 0, tiled=True)
    prefill_out = prefill(layout, queries, cache, kv_up)[None]
    pool, prefill_out = lax.optimization_barrier((pool, prefill_out))
    return prefill_out, select(layout, pool)


def solution(mesh):
    fine = Mesh(mesh.devices.reshape(2, 2, 4, 8, 4), ("section", "yh", "x", "z", "rep"))
    tp = ("yh", "x", "z")
    group = ("section", "rep")
    in_specs = (
        P(group, None, tp),
        P(group, tp, None),
        P(tp, None),
        P(),
        P(None, tp),
        P(None, tp),
        P("section", None),
        P("section", None),
        P(group, None, None),
        P(group, None, None),
    )
    out_specs = (P(group, None, tp), P(group, None, tp))
    return jax.shard_map(body, mesh=fine, in_specs=in_specs, out_specs=out_specs, check_vma=False)
```

```python
import math

import jax
import jax.numpy as jnp
import numpy as np
from jax import lax
from jax.experimental import pallas as pl
from jax.experimental.pallas import tpu as pltpu
from jax.sharding import Mesh, PartitionSpec as P

KVL = 512
NOPE = 128
ROPE = 64
VD = 128
BLK = 128
NREQ = 3
STEPS = 4
REACH = 4
NREP = 4
NX = 4
HEADS = 2
PAD = 16
TABLE = 640
NORM_FLOPS = 30_000_000_000
WIDE = KVL + 2 * ROPE
START, LENGTH, BASE, PLACE, FIRST, SOURCE, SLOT, HALF, LINE = 0, 3, 6, 8, 16, 24, 28, 32, 40

SIGMA = (1.0 + 0.1 * math.log(40.0)) ** 2 * (NOPE + ROPE) ** (-0.5)
bf16 = jnp.bfloat16
f32 = jnp.float32
i32 = jnp.int32


def rotary_table():
    half = ROPE // 2
    frequency = np.float32(10000.0) ** (-np.arange(half, dtype=np.float32) * np.float32(2.0 / ROPE))
    angles = np.arange(TABLE, dtype=np.float32)[:, None] * frequency.astype(np.float32)
    cos_part, sin_part = np.cos(angles), np.sin(angles)
    return np.concatenate([cos_part] * 4, axis=1), np.concatenate([-sin_part, sin_part] * 2, axis=1)


def rotate(u, cos_part, sin_part):
    lane = lax.broadcasted_iota(i32, u.shape, 1)
    swapped = jnp.where(lane % ROPE < ROPE // 2, pltpu.roll(u, 96, 1), pltpu.roll(u, 32, 1))
    return u * cos_part + swapped * sin_part


def split_heads(u):
    a, b, c = u[:, :NOPE], u[:, NOPE : 2 * NOPE], u[:, 2 * NOPE :]
    low = lax.broadcasted_iota(i32, a.shape, 1) < ROPE
    return a, jnp.where(low, pltpu.roll(b, ROPE, 1), pltpu.roll(c, ROPE, 1)), jnp.where(low, b, c)


def spread(a, axes, count):
    copies = jnp.broadcast_to(a[None], (count,) + a.shape)
    return lax.all_to_all(copies, axes, 0, 0, tiled=True)


def shift(count, d):
    return [(i, (i + d) % count) for i in range(count)]


def dot_t(a, b):
    return lax.dot_general(a, b, (((1,), (1,)), ((), ())), preferred_element_type=f32)


def layout_kernel(ids_ref, req_ref, slot_ref, out_ref):
    rep, x, yh, yz = ids_ref[0], ids_ref[1], ids_ref[2], ids_ref[3]
    lengths = [req_ref[rep, r] for r in range(NREQ)]
    starts = [0, lengths[0], lengths[0] + lengths[1]]

    def start_of(block):
        return jnp.where(block >= starts[2], starts[2], jnp.where(block >= starts[1], starts[1], 0))

    for r in range(NREQ):
        out_ref[START + r] = starts[r] * BLK
        out_ref[LENGTH + r] = lengths[r] * BLK
        slot = slot_ref[0, rep * NREQ + r]
        out_ref[SLOT + r] = (lax.div(slot, NREQ) ^ rep) * NREQ + lax.rem(slot, NREQ)
        source = 0
        for m in range(NREP * NREQ):
            source += jnp.where(slot_ref[0, m] == rep * NREQ + r, m, 0)
        out_ref[SOURCE + r] = lax.div(source, NREQ) * PAD + lax.rem(source, NREQ) * STEPS
    for j in range(2):
        out_ref[HALF + j] = yh ^ j
    for d in range(NX):
        out_ref[LINE + d] = d
    out_ref[BASE] = x * 2 * BLK + yz * PAD - start_of(x * 2 + lax.div(yz, 8)) * BLK
    for i in range(8):
        out_ref[PLACE + i] = i - start_of(i)
        out_ref[FIRST + i] = start_of(i) * BLK


SMEM = pl.BlockSpec(memory_space=pltpu.SMEM)
VMEM = pl.BlockSpec(memory_space=pltpu.VMEM)


def request_layout(ids, req_blocks, dest_slot):
    return pl.pallas_call(
        layout_kernel,
        in_specs=[SMEM] * 3,
        out_specs=SMEM,
        out_shape=jax.ShapeDtypeStruct((64,), i32),
        cost_estimate=pl.CostEstimate(flops=1000, bytes_accessed=1000, transcendentals=0),
        name="request_layout",
    )(ids, req_blocks, dest_slot)


def pack_kernel(hidden_ref, down_ref, own_ref, out_ref):
    per_x = hidden_ref.shape[1] // NX
    count = own_ref.shape[1] // per_x
    for i in range(NX):
        out_ref[i, :, :per_x] = hidden_ref[:, i * per_x : (i + 1) * per_x]
        for j in range(count):
            out_ref[i, j * PAD : (j + 1) * PAD, per_x : 2 * per_x] = own_ref[:, j * per_x : (j + 1) * per_x]
        left = out_ref.shape[1] - count * PAD
        out_ref[i, count * PAD :, per_x : 2 * per_x] = jnp.zeros((left, per_x), bf16)
        out_ref[i, :, 2 * per_x :] = down_ref[...]


def pack(hidden_t, kv_down, own):
    features, rows = hidden_t.shape
    return pl.pallas_call(
        pack_kernel,
        in_specs=[VMEM] * 3,
        out_specs=VMEM,
        out_shape=jax.ShapeDtypeStruct((NX, features, 2 * (rows // NX) + kv_down.shape[1]), bf16),
        cost_estimate=pl.CostEstimate(flops=0, bytes_accessed=1_500_000, transcendentals=0),
        name="pack_hidden",
    )(hidden_t, kv_down, own)


def meet_kernel(packed_ref, partial_ref, line_ref):
    per_x = line_ref.shape[1] // 6
    packed = packed_ref[...].reshape(-1, packed_ref.shape[2])
    partial = lax.dot_general(
        packed[:, :per_x], packed[:, 2 * per_x :], (((0,), (0,)), ((), ())), preferred_element_type=f32
    )
    partial_ref[...] = partial.reshape(partial_ref.shape)
    for d in range(NX):
        for j in range(6):
            line_ref[d * PAD : (d + 1) * PAD, j * per_x : (j + 1) * per_x] = packed_ref[
                d, j * PAD : (j + 1) * PAD, per_x : 2 * per_x
            ]


def meet(packed, per_x, width):
    latent = packed.shape[2] - 2 * per_x
    return pl.pallas_call(
        meet_kernel,
        in_specs=[VMEM],
        out_specs=[VMEM, VMEM],
        out_shape=[
            jax.ShapeDtypeStruct((16, per_x // 16, latent), f32),
            jax.ShapeDtypeStruct((NX * PAD, width), bf16),
        ],
        compiler_params=pltpu.CompilerParams(vmem_limit_bytes=16 * 1024 * 1024),
        cost_estimate=pl.CostEstimate(flops=130_000_000, bytes_accessed=2_000_000, transcendentals=0),
        name="partial_and_rows",
    )(packed)


def norm_kernel(layout_ref, pieces_ref, gain_ref, cos_ref, sin_ref, out_ref):
    latent = jnp.sum(pieces_ref[...], axis=0)
    content = latent[:, :KVL]
    scale = lax.rsqrt(jnp.mean(content * content, axis=1, keepdims=True) + 1e-06)
    content = (content * scale * gain_ref[...]).astype(bf16)
    at = pl.ds(pl.multiple_of(layout_ref[BASE], PAD), latent.shape[0])
    pe = jnp.concatenate([latent[:, KVL:]] * 2, axis=1)
    pe = rotate(pe, cos_ref[at, :], sin_ref[at, :]).astype(bf16)
    for i in range(out_ref.shape[0]):
        out_ref[i, :, :KVL] = content
        out_ref[i, :, KVL:] = pe


def norm_rows(layout, pieces, gain, cos_part, sin_part):
    count, chunk, _ = pieces.shape
    return pl.pallas_call(
        norm_kernel,
        in_specs=[SMEM] + [VMEM] * 4,
        out_specs=VMEM,
        out_shape=jax.ShapeDtypeStruct((count, chunk, WIDE), bf16),
        cost_estimate=pl.CostEstimate(flops=NORM_FLOPS, bytes_accessed=1_000_000, transcendentals=16),
        name="norm_rows",
    )(layout, pieces, gain, cos_part, sin_part)


def query_kernel(layout_ref, cq_ref, w_ref, cos_ref, sin_ref, out_ref):
    half = pl.program_id(0)
    rows = jnp.concatenate([cq_ref[:, d].reshape(BLK, -1) for d in range(NX)])
    u = jnp.dot(rows, w_ref[...], preferred_element_type=f32)
    first, second, pe = split_heads(u)
    low = lax.broadcasted_iota(i32, (BLK, 2 * ROPE), 1) < ROPE
    for d in range(NX):
        here = slice(d * BLK, (d + 1) * BLK)
        line = layout_ref[LINE + d]
        to = pl.ds(pl.multiple_of(line * BLK, BLK), BLK)
        at = pl.ds(pl.multiple_of(layout_ref[PLACE + half * NX + line] * BLK, BLK), BLK)
        turned = rotate(pe[here], cos_ref[at, :], sin_ref[at, :])
        out_ref[0, to, :NOPE] = first[here].astype(bf16)
        out_ref[0, to, NOPE:] = jnp.where(low, turned, 0.0).astype(bf16)
        out_ref[1, to, :NOPE] = second[here].astype(bf16)
        out_ref[1, to, NOPE:] = jnp.where(low, 0.0, turned).astype(bf16)


def project_queries(layout, cq, weights, cos_part, sin_part):
    width = cq.shape[-1]
    table = pl.BlockSpec(cos_part.shape, lambda j, place: (0, 0))
    return pl.pallas_call(
        query_kernel,
        grid_spec=pltpu.PrefetchScalarGridSpec(
            num_scalar_prefetch=1,
            grid=(2,),
            in_specs=[
                pl.BlockSpec((8, NX, PAD, width), lambda j, place: (0, place[HALF + j], 0, 0)),
                pl.BlockSpec(weights.shape, lambda j, place: (0, 0)),
                table,
                table,
            ],
            out_specs=pl.BlockSpec((HEADS, NX * BLK, 2 * NOPE), lambda j, place: (0, j, 0)),
        ),
        out_shape=jax.ShapeDtypeStruct((HEADS, 8 * BLK, 2 * NOPE), bf16),
        compiler_params=pltpu.CompilerParams(vmem_limit_bytes=60 * 1024 * 1024),
        cost_estimate=pl.CostEstimate(flops=1_200_000_000, bytes_accessed=5_000_000, transcendentals=0),
        name="project_queries",
    )(layout, cq, weights, cos_part, sin_part)


def prepare_kernel(layout_ref, rows_ref, w_ref, kv_ref, cos_ref, sin_ref, out_ref, in_ref, cos_at, sin_at):
    query_latent = w_ref.shape[0]
    in_ref[...] = jnp.zeros_like(in_ref)
    cos_at[...] = jnp.zeros_like(cos_at)
    sin_at[...] = jnp.zeros_like(sin_at)
    for r in range(NREQ):
        here = slice(r * STEPS, (r + 1) * STEPS)
        in_ref[here, :] = rows_ref[layout_ref[SLOT + r]].astype(f32)
        at = pl.ds(pl.multiple_of(layout_ref[LENGTH + r], BLK), 8)
        cos_at[here, :] = cos_ref[at, :][:STEPS]
        sin_at[here, :] = sin_ref[at, :][:STEPS]
    cos_part, sin_part = cos_at[...], sin_at[...]
    rows = in_ref[:, :query_latent].astype(bf16)
    u = jnp.dot(rows, w_ref[...], preferred_element_type=f32).astype(bf16).astype(f32)
    first, second, pe = split_heads(u)
    pe = rotate(pe, cos_part, sin_part)
    low = lax.broadcasted_iota(i32, pe.shape, 1) < ROPE
    for h, plain in enumerate((first, second)):
        here = slice(h * PAD, (h + 1) * PAD)
        base = h * (NOPE + VD)
        out_ref[here, :KVL] = dot_t(plain.astype(bf16), kv_ref[:, base : base + NOPE]).astype(bf16)
        out_ref[here, KVL:] = jnp.where(low == (h == 0), pe, 0.0).astype(bf16)
    new = slice(HEADS * PAD, (HEADS + 1) * PAD)
    out_ref[new, :KVL] = in_ref[:, query_latent : query_latent + KVL].astype(bf16)
    new_pe = jnp.concatenate([in_ref[:, query_latent + KVL :]] * 2, axis=1)
    out_ref[new, KVL:] = rotate(new_pe, cos_part, sin_part).astype(bf16)


def prepare_decode(layout, rows, q_up, kv_up, cos_part, sin_part):
    return pl.pallas_call(
        prepare_kernel,
        in_specs=[SMEM] + [VMEM] * 5,
        out_specs=VMEM,
        out_shape=jax.ShapeDtypeStruct(((HEADS + 1) * PAD, WIDE), bf16),
        scratch_shapes=[
            pltpu.VMEM((PAD, rows.shape[-1]), f32),
            pltpu.VMEM((PAD, 2 * ROPE), f32),
            pltpu.VMEM((PAD, 2 * ROPE), f32),
        ],
        compiler_params=pltpu.CompilerParams(vmem_limit_bytes=16 * 1024 * 1024),
        cost_estimate=pl.CostEstimate(flops=30_000_000, bytes_accessed=2_500_000, transcendentals=0),
        name="prepare_decode",
    )(layout, rows, q_up, kv_up, cos_part, sin_part)


def decode_kernel(layout_ref, ready_ref, cache_ref, kv_ref, out_ref):
    query = ready_ref[: HEADS * PAD, :]
    fresh = ready_ref[HEADS * PAD :, :]
    old = dot_t(query, cache_ref[...]) * SIGMA
    new = dot_t(query, fresh) * SIGMA
    request = lax.broadcasted_iota(i32, (HEADS * PAD, 1), 0) % PAD // STEPS

    def per_request(values):
        return jnp.where(request == 0, values[0], jnp.where(request == 1, values[1], values[2]))

    low = per_request([layout_ref[START + r] for r in range(NREQ)])
    high = per_request([layout_ref[START + r] + layout_ref[LENGTH + r] for r in range(NREQ)])
    column = lax.broadcasted_iota(i32, old.shape, 1)
    old = jnp.where((column >= low) & (column < high), old, -1e30)
    step = lax.broadcasted_iota(i32, new.shape, 0) % PAD
    other = lax.broadcasted_iota(i32, new.shape, 1)
    new = jnp.where((step // STEPS == other // STEPS) & (other <= step), new, -1e30)
    top = jnp.maximum(jnp.max(old, axis=1, keepdims=True), jnp.max(new, axis=1, keepdims=True))
    old = jnp.exp(old - top)
    new = jnp.exp(new - top)
    inverse = 1.0 / (jnp.sum(old, axis=1, keepdims=True) + jnp.sum(new, axis=1, keepdims=True))
    old = (old * inverse).astype(bf16)
    new = (new * inverse).astype(bf16)
    mixture = (
        jnp.dot(old, cache_ref[:, :KVL], preferred_element_type=f32)
        + jnp.dot(new, fresh[:, :KVL], preferred_element_type=f32)
    ).astype(bf16)
    for h in range(HEADS):
        base = h * (NOPE + VD) + NOPE
        value = jnp.dot(
            mixture[h * PAD : (h + 1) * PAD], kv_ref[:, base : base + VD], preferred_element_type=f32
        ).astype(bf16)
        for i in range(NREP):
            out_ref[i, :, h * VD : (h + 1) * VD] = value


def decode(layout, ready, cache, kv_up):
    return pl.pallas_call(
        decode_kernel,
        in_specs=[SMEM] + [VMEM] * 3,
        out_specs=VMEM,
        out_shape=jax.ShapeDtypeStruct((NREP, PAD, HEADS * VD), bf16),
        compiler_params=pltpu.CompilerParams(vmem_limit_bytes=16 * 1024 * 1024),
        cost_estimate=pl.CostEstimate(flops=100_000_000, bytes_accessed=2_000_000, transcendentals=40_000),
        name="decode_attention",
    )(layout, ready, cache, kv_up)


def select_kernel(layout_ref, pool_ref, out_ref):
    pool = pool_ref[...].reshape(NREP * PAD, -1)
    for r in range(NREQ):
        row = lax.broadcasted_iota(i32, (8, NREP * PAD), 0)
        column = lax.broadcasted_iota(i32, (8, NREP * PAD), 1)
        pick = jnp.where(column == layout_ref[SOURCE + r] + row, 1.0, 0.0).astype(bf16)
        out_ref[r] = jnp.dot(pick, pool, preferred_element_type=f32)[:STEPS].astype(bf16)


def select(layout, pool):
    return pl.pallas_call(
        select_kernel,
        in_specs=[SMEM, VMEM],
        out_specs=VMEM,
        out_shape=jax.ShapeDtypeStruct((NREQ, STEPS, HEADS * VD), bf16),
        cost_estimate=pl.CostEstimate(flops=1_000_000, bytes_accessed=50_000, transcendentals=0),
        name="select_slots",
    )(layout, pool)


def prefill_kernel(layout_ref, q_ref, cache_ref, kv_ref, out_ref, key_ref, value_ref):
    for j in range(4):
        rows = slice(j * 2 * BLK, (j + 1) * 2 * BLK)
        wide = jnp.dot(cache_ref[rows, :KVL], kv_ref[...], preferred_element_type=f32).astype(bf16)
        for h in range(HEADS):
            base = h * (NOPE + VD)
            key_ref[h, rows, :NOPE] = wide[:, base : base + NOPE]
            key_ref[h, rows, NOPE:] = cache_ref[rows, KVL:]
            value_ref[h, rows, :] = wide[:, base + NOPE : base + NOPE + VD]
    for i in range(8):
        first = max(0, i - REACH + 1) * BLK
        last = (i + 1) * BLK
        shape = (BLK, last - first)
        column = lax.broadcasted_iota(i32, shape, 1) + first
        row = lax.broadcasted_iota(i32, shape, 0) + i * BLK
        ok = (column >= layout_ref[FIRST + i]) & (column <= row)
        scores = [
            dot_t(q_ref[h, i * BLK : last, :], key_ref[h, first:last, :]) * SIGMA for h in range(HEADS)
        ]
        scores = [jnp.where(ok, s, -1e30) for s in scores]
        weights = [jnp.exp(s - jnp.max(s, axis=1, keepdims=True)) for s in scores]
        weights = [(w * (1.0 / jnp.sum(w, axis=1, keepdims=True))).astype(bf16) for w in weights]
        for h in range(HEADS):
            out_ref[i * BLK : last, h * VD : (h + 1) * VD] = jnp.dot(
                weights[h], value_ref[h, first:last, :], preferred_element_type=f32
            ).astype(bf16)


def prefill(layout, queries, cache, kv_up):
    rows = cache.shape[0]
    return pl.pallas_call(
        prefill_kernel,
        in_specs=[SMEM] + [VMEM] * 3,
        out_specs=VMEM,
        out_shape=jax.ShapeDtypeStruct((rows, HEADS * VD), bf16),
        scratch_shapes=[
            pltpu.VMEM((HEADS, rows, 2 * NOPE), bf16),
            pltpu.VMEM((HEADS, rows, VD), bf16),
        ],
        compiler_params=pltpu.CompilerParams(vmem_limit_bytes=32 * 1024 * 1024),
        cost_estimate=pl.CostEstimate(flops=1_500_000_000, bytes_accessed=4_000_000, transcendentals=1_000_000),
        name="prefill_attention",
    )(layout, queries, cache, kv_up)


def body(hidden, comp_query, kv_down, kv_gain, q_up, kv_up, req_blocks, dest_slot, dec_query, dec_latent):
    ids = jnp.stack(
        [lax.axis_index("rep"), lax.axis_index("x"), lax.axis_index("yh"), lax.axis_index(("yh", "z"))]
    ).astype(i32)
    rows = hidden.shape[1]
    per_x = rows // NX
    cos_part, sin_part = rotary_table()

    own = comp_query[0]
    packed = lax.all_to_all(pack(hidden[0].T, kv_down, own), "x", 0, 0, tiled=True)
    layout = request_layout(ids, req_blocks, dest_slot)
    packed, dec_query, dec_latent = lax.optimization_barrier((packed, dec_query, dec_latent))
    partial, line = meet(packed, per_x, own.shape[1])
    line = jnp.concatenate([line, lax.ppermute(line, "yh", shift(2, 1))])
    cq = lax.all_gather(line, "z", axis=0, tiled=True)

    pieces = lax.all_to_all(partial, ("yh", "z"), 0, 0, tiled=True)
    copies = norm_rows(layout, pieces, kv_gain[None, :], cos_part, sin_part)
    cache = lax.all_to_all(copies, ("yh", "z"), 0, 0, tiled=True).reshape(per_x, -1)

    rep_in = jnp.concatenate([dec_query, dec_latent], axis=2)
    for d in (1, 2):
        met = lax.ppermute(rep_in, "rep", [(i, i ^ d) for i in range(NREP)])
        rep_in = jnp.concatenate([rep_in, met])
    ready = prepare_decode(layout, rep_in, q_up, kv_up, cos_part, sin_part)
    cache, ready = lax.optimization_barrier((cache, ready))
    cache = spread(cache, "x", NX).reshape(rows, -1)

    queries = project_queries(layout, cq.reshape(8, 8, PAD, -1), q_up, cos_part, sin_part)
    cache, queries = lax.optimization_barrier((cache, queries))
    result = decode(layout, ready, cache, kv_up)
    pool = lax.all_to_all(result, "rep", 0, 0, tiled=True)
    prefill_out = prefill(layout, queries, cache, kv_up)[None]
    pool, prefill_out = lax.optimization_barrier((pool, prefill_out))
    return prefill_out, select(layout, pool)


def solution(mesh):
    fine = Mesh(mesh.devices.reshape(2, 2, 4, 8, 4), ("section", "yh", "x", "z", "rep"))
    tp = ("yh", "x", "z")
    group = ("section", "rep")
    in_specs = (
        P(group, None, tp),
        P(group, tp, None),
        P(tp, None),
        P(),
        P(None, tp),
        P(None, tp),
        P("section", None),
        P("section", None),
        P(group, None, None),
        P(group, None, None),
    )
    out_specs = (P(group, None, tp), P(group, None, tp))
    return jax.shard_map(body, mesh=fine, in_specs=in_specs, out_specs=out_specs, check_vma=False)
```

```python
import math

import jax
import jax.numpy as jnp
import numpy as np
from jax import lax
from jax.experimental import pallas as pl
from jax.experimental.pallas import tpu as pltpu
from jax.sharding import Mesh, PartitionSpec as P

KVL = 512
NOPE = 128
ROPE = 64
VD = 128
BLK = 128
NREQ = 3
STEPS = 4
REACH = 4
NREP = 4
NX = 4
HEADS = 2
PAD = 16
TABLE = 640
NORM_FLOPS = 35_000_000_000
WIDE = KVL + 2 * ROPE
START, LENGTH, BASE, PLACE, FIRST, SOURCE, SLOT, HALF, LINE = 0, 3, 6, 8, 16, 24, 28, 32, 40

SIGMA = (1.0 + 0.1 * math.log(40.0)) ** 2 * (NOPE + ROPE) ** (-0.5)
bf16 = jnp.bfloat16
f32 = jnp.float32
i32 = jnp.int32


def rotary_table():
    half = ROPE // 2
    frequency = np.float32(10000.0) ** (-np.arange(half, dtype=np.float32) * np.float32(2.0 / ROPE))
    angles = np.arange(TABLE, dtype=np.float32)[:, None] * frequency.astype(np.float32)
    cos_part, sin_part = np.cos(angles), np.sin(angles)
    return np.concatenate([cos_part] * 4, axis=1), np.concatenate([-sin_part, sin_part] * 2, axis=1)


def rotate(u, cos_part, sin_part):
    lane = lax.broadcasted_iota(i32, u.shape, 1)
    swapped = jnp.where(lane % ROPE < ROPE // 2, pltpu.roll(u, 96, 1), pltpu.roll(u, 32, 1))
    return u * cos_part + swapped * sin_part


def split_heads(u):
    a, b, c = u[:, :NOPE], u[:, NOPE : 2 * NOPE], u[:, 2 * NOPE :]
    low = lax.broadcasted_iota(i32, a.shape, 1) < ROPE
    return a, jnp.where(low, pltpu.roll(b, ROPE, 1), pltpu.roll(c, ROPE, 1)), jnp.where(low, b, c)


def spread(a, axes, count):
    copies = jnp.broadcast_to(a[None], (count,) + a.shape)
    return lax.all_to_all(copies, axes, 0, 0, tiled=True)


def shift(count, d):
    return [(i, (i + d) % count) for i in range(count)]


def dot_t(a, b):
    return lax.dot_general(a, b, (((1,), (1,)), ((), ())), preferred_element_type=f32)


def layout_kernel(ids_ref, req_ref, slot_ref, out_ref):
    rep, x, yh, yz = ids_ref[0], ids_ref[1], ids_ref[2], ids_ref[3]
    lengths = [req_ref[rep, r] for r in range(NREQ)]
    starts = [0, lengths[0], lengths[0] + lengths[1]]

    def start_of(block):
        return jnp.where(block >= starts[2], starts[2], jnp.where(block >= starts[1], starts[1], 0))

    for r in range(NREQ):
        out_ref[START + r] = starts[r] * BLK
        out_ref[LENGTH + r] = lengths[r] * BLK
        slot = slot_ref[0, rep * NREQ + r]
        out_ref[SLOT + r] = (lax.div(slot, NREQ) ^ rep) * NREQ + lax.rem(slot, NREQ)
        source = 0
        for m in range(NREP * NREQ):
            source += jnp.where(slot_ref[0, m] == rep * NREQ + r, m, 0)
        out_ref[SOURCE + r] = lax.div(source, NREQ) * PAD + lax.rem(source, NREQ) * STEPS
    for j in range(2):
        out_ref[HALF + j] = yh ^ j
    for d in range(NX):
        out_ref[LINE + d] = d
    out_ref[BASE] = x * 2 * BLK + yz * PAD - start_of(x * 2 + lax.div(yz, 8)) * BLK
    for i in range(8):
        out_ref[PLACE + i] = i - start_of(i)
        out_ref[FIRST + i] = start_of(i) * BLK


SMEM = pl.BlockSpec(memory_space=pltpu.SMEM)
VMEM = pl.BlockSpec(memory_space=pltpu.VMEM)


def request_layout(ids, req_blocks, dest_slot):
    return pl.pallas_call(
        layout_kernel,
        in_specs=[SMEM] * 3,
        out_specs=SMEM,
        out_shape=jax.ShapeDtypeStruct((64,), i32),
        cost_estimate=pl.CostEstimate(flops=1000, bytes_accessed=1000, transcendentals=0),
        name="request_layout",
    )(ids, req_blocks, dest_slot)


def pack_kernel(hidden_ref, down_ref, own_ref, out_ref):
    per_x = hidden_ref.shape[1] // NX
    count = own_ref.shape[1] // per_x
    for i in range(NX):
        out_ref[i, :, :per_x] = hidden_ref[:, i * per_x : (i + 1) * per_x]
        for j in range(count):
            out_ref[i, j * PAD : (j + 1) * PAD, per_x : 2 * per_x] = own_ref[:, j * per_x : (j + 1) * per_x]
        left = out_ref.shape[1] - count * PAD
        out_ref[i, count * PAD :, per_x : 2 * per_x] = jnp.zeros((left, per_x), bf16)
        out_ref[i, :, 2 * per_x :] = down_ref[...]


def pack(hidden_t, kv_down, own):
    features, rows = hidden_t.shape
    return pl.pallas_call(
        pack_kernel,
        in_specs=[VMEM] * 3,
        out_specs=VMEM,
        out_shape=jax.ShapeDtypeStruct((NX, features, 2 * (rows // NX) + kv_down.shape[1]), bf16),
        cost_estimate=pl.CostEstimate(flops=0, bytes_accessed=1_500_000, transcendentals=0),
        name="pack_hidden",
    )(hidden_t, kv_down, own)


def meet_kernel(packed_ref, partial_ref, line_ref):
    per_x = line_ref.shape[1] // 6
    packed = packed_ref[...].reshape(-1, packed_ref.shape[2])
    partial = lax.dot_general(
        packed[:, :per_x], packed[:, 2 * per_x :], (((0,), (0,)), ((), ())), preferred_element_type=f32
    )
    partial_ref[...] = partial.reshape(partial_ref.shape)
    for d in range(NX):
        for j in range(6):
            line_ref[d * PAD : (d + 1) * PAD, j * per_x : (j + 1) * per_x] = packed_ref[
                d, j * PAD : (j + 1) * PAD, per_x : 2 * per_x
            ]


def meet(packed, per_x, width):
    latent = packed.shape[2] - 2 * per_x
    return pl.pallas_call(
        meet_kernel,
        in_specs=[VMEM],
        out_specs=[VMEM, VMEM],
        out_shape=[
            jax.ShapeDtypeStruct((16, per_x // 16, latent), f32),
            jax.ShapeDtypeStruct((NX * PAD, width), bf16),
        ],
        compiler_params=pltpu.CompilerParams(vmem_limit_bytes=16 * 1024 * 1024),
        cost_estimate=pl.CostEstimate(flops=130_000_000, bytes_accessed=2_000_000, transcendentals=0),
        name="partial_and_rows",
    )(packed)


def norm_kernel(layout_ref, pieces_ref, gain_ref, cos_ref, sin_ref, out_ref):
    latent = jnp.sum(pieces_ref[...], axis=0)
    content = latent[:, :KVL]
    scale = lax.rsqrt(jnp.mean(content * content, axis=1, keepdims=True) + 1e-06)
    content = (content * scale * gain_ref[...]).astype(bf16)
    at = pl.ds(pl.multiple_of(layout_ref[BASE], PAD), latent.shape[0])
    pe = jnp.concatenate([latent[:, KVL:]] * 2, axis=1)
    pe = rotate(pe, cos_ref[at, :], sin_ref[at, :]).astype(bf16)
    for i in range(out_ref.shape[0]):
        out_ref[i, :, :KVL] = content
        out_ref[i, :, KVL:] = pe


def norm_rows(layout, pieces, gain, cos_part, sin_part):
    count, chunk, _ = pieces.shape
    return pl.pallas_call(
        norm_kernel,
        in_specs=[SMEM] + [VMEM] * 4,
        out_specs=VMEM,
        out_shape=jax.ShapeDtypeStruct((count, chunk, WIDE), bf16),
        cost_estimate=pl.CostEstimate(flops=NORM_FLOPS, bytes_accessed=1_000_000, transcendentals=16),
        name="norm_rows",
    )(layout, pieces, gain, cos_part, sin_part)


def query_kernel(layout_ref, cq_ref, w_ref, cos_ref, sin_ref, out_ref):
    half = pl.program_id(0)
    rows = jnp.concatenate([cq_ref[:, d].reshape(BLK, -1) for d in range(NX)])
    u = jnp.dot(rows, w_ref[...], preferred_element_type=f32)
    first, second, pe = split_heads(u)
    low = lax.broadcasted_iota(i32, (BLK, 2 * ROPE), 1) < ROPE
    for d in range(NX):
        here = slice(d * BLK, (d + 1) * BLK)
        line = layout_ref[LINE + d]
        to = pl.ds(pl.multiple_of(line * BLK, BLK), BLK)
        at = pl.ds(pl.multiple_of(layout_ref[PLACE + half * NX + line] * BLK, BLK), BLK)
        turned = rotate(pe[here], cos_ref[at, :], sin_ref[at, :])
        out_ref[0, to, :NOPE] = first[here].astype(bf16)
        out_ref[0, to, NOPE:] = jnp.where(low, turned, 0.0).astype(bf16)
        out_ref[1, to, :NOPE] = second[here].astype(bf16)
        out_ref[1, to, NOPE:] = jnp.where(low, 0.0, turned).astype(bf16)


def project_queries(layout, cq, weights, cos_part, sin_part):
    width = cq.shape[-1]
    table = pl.BlockSpec(cos_part.shape, lambda j, place: (0, 0))
    return pl.pallas_call(
        query_kernel,
        grid_spec=pltpu.PrefetchScalarGridSpec(
            num_scalar_prefetch=1,
            grid=(2,),
            in_specs=[
                pl.BlockSpec((8, NX, PAD, width), lambda j, place: (0, place[HALF + j], 0, 0)),
                pl.BlockSpec(weights.shape, lambda j, place: (0, 0)),
                table,
                table,
            ],
            out_specs=pl.BlockSpec((HEADS, NX * BLK, 2 * NOPE), lambda j, place: (0, j, 0)),
        ),
        out_shape=jax.ShapeDtypeStruct((HEADS, 8 * BLK, 2 * NOPE), bf16),
        compiler_params=pltpu.CompilerParams(vmem_limit_bytes=60 * 1024 * 1024),
        cost_estimate=pl.CostEstimate(flops=1_200_000_000, bytes_accessed=5_000_000, transcendentals=0),
        name="project_queries",
    )(layout, cq, weights, cos_part, sin_part)


def prepare_kernel(layout_ref, rows_ref, w_ref, kv_ref, cos_ref, sin_ref, out_ref, in_ref, cos_at, sin_at):
    query_latent = w_ref.shape[0]
    in_ref[...] = jnp.zeros_like(in_ref)
    cos_at[...] = jnp.zeros_like(cos_at)
    sin_at[...] = jnp.zeros_like(sin_at)
    for r in range(NREQ):
        here = slice(r * STEPS, (r + 1) * STEPS)
        in_ref[here, :] = rows_ref[layout_ref[SLOT + r]].astype(f32)
        at = pl.ds(pl.multiple_of(layout_ref[LENGTH + r], BLK), 8)
        cos_at[here, :] = cos_ref[at, :][:STEPS]
        sin_at[here, :] = sin_ref[at, :][:STEPS]
    cos_part, sin_part = cos_at[...], sin_at[...]
    rows = in_ref[:, :query_latent].astype(bf16)
    u = jnp.dot(rows, w_ref[...], preferred_element_type=f32).astype(bf16).astype(f32)
    first, second, pe = split_heads(u)
    pe = rotate(pe, cos_part, sin_part)
    low = lax.broadcasted_iota(i32, pe.shape, 1) < ROPE
    for h, plain in enumerate((first, second)):
        here = slice(h * PAD, (h + 1) * PAD)
        base = h * (NOPE + VD)
        out_ref[here, :KVL] = dot_t(plain.astype(bf16), kv_ref[:, base : base + NOPE]).astype(bf16)
        out_ref[here, KVL:] = jnp.where(low == (h == 0), pe, 0.0).astype(bf16)
    new = slice(HEADS * PAD, (HEADS + 1) * PAD)
    out_ref[new, :KVL] = in_ref[:, query_latent : query_latent + KVL].astype(bf16)
    new_pe = jnp.concatenate([in_ref[:, query_latent + KVL :]] * 2, axis=1)
    out_ref[new, KVL:] = rotate(new_pe, cos_part, sin_part).astype(bf16)


def prepare_decode(layout, rows, q_up, kv_up, cos_part, sin_part):
    return pl.pallas_call(
        prepare_kernel,
        in_specs=[SMEM] + [VMEM] * 5,
        out_specs=VMEM,
        out_shape=jax.ShapeDtypeStruct(((HEADS + 1) * PAD, WIDE), bf16),
        scratch_shapes=[
            pltpu.VMEM((PAD, rows.shape[-1]), f32),
            pltpu.VMEM((PAD, 2 * ROPE), f32),
            pltpu.VMEM((PAD, 2 * ROPE), f32),
        ],
        compiler_params=pltpu.CompilerParams(vmem_limit_bytes=16 * 1024 * 1024),
        cost_estimate=pl.CostEstimate(flops=30_000_000, bytes_accessed=2_500_000, transcendentals=0),
        name="prepare_decode",
    )(layout, rows, q_up, kv_up, cos_part, sin_part)


def decode_kernel(layout_ref, ready_ref, cache_ref, kv_ref, out_ref):
    query = ready_ref[: HEADS * PAD, :]
    fresh = ready_ref[HEADS * PAD :, :]
    old = dot_t(query, cache_ref[...]) * SIGMA
    new = dot_t(query, fresh) * SIGMA
    request = lax.broadcasted_iota(i32, (HEADS * PAD, 1), 0) % PAD // STEPS

    def per_request(values):
        return jnp.where(request == 0, values[0], jnp.where(request == 1, values[1], values[2]))

    low = per_request([layout_ref[START + r] for r in range(NREQ)])
    high = per_request([layout_ref[START + r] + layout_ref[LENGTH + r] for r in range(NREQ)])
    column = lax.broadcasted_iota(i32, old.shape, 1)
    old = jnp.where((column >= low) & (column < high), old, -1e30)
    step = lax.broadcasted_iota(i32, new.shape, 0) % PAD
    other = lax.broadcasted_iota(i32, new.shape, 1)
    new = jnp.where((step // STEPS == other // STEPS) & (other <= step), new, -1e30)
    top = jnp.maximum(jnp.max(old, axis=1, keepdims=True), jnp.max(new, axis=1, keepdims=True))
    old = jnp.exp(old - top)
    new = jnp.exp(new - top)
    inverse = 1.0 / (jnp.sum(old, axis=1, keepdims=True) + jnp.sum(new, axis=1, keepdims=True))
    old = (old * inverse).astype(bf16)
    new = (new * inverse).astype(bf16)
    mixture = (
        jnp.dot(old, cache_ref[:, :KVL], preferred_element_type=f32)
        + jnp.dot(new, fresh[:, :KVL], preferred_element_type=f32)
    ).astype(bf16)
    for h in range(HEADS):
        base = h * (NOPE + VD) + NOPE
        value = jnp.dot(
            mixture[h * PAD : (h + 1) * PAD], kv_ref[:, base : base + VD], preferred_element_type=f32
        ).astype(bf16)
        for i in range(NREP):
            out_ref[i, :, h * VD : (h + 1) * VD] = value


def decode(layout, ready, cache, kv_up):
    return pl.pallas_call(
        decode_kernel,
        in_specs=[SMEM] + [VMEM] * 3,
        out_specs=VMEM,
        out_shape=jax.ShapeDtypeStruct((NREP, PAD, HEADS * VD), bf16),
        compiler_params=pltpu.CompilerParams(vmem_limit_bytes=16 * 1024 * 1024),
        cost_estimate=pl.CostEstimate(flops=100_000_000, bytes_accessed=2_000_000, transcendentals=40_000),
        name="decode_attention",
    )(layout, ready, cache, kv_up)


def select_kernel(layout_ref, pool_ref, out_ref):
    pool = pool_ref[...].reshape(NREP * PAD, -1)
    for r in range(NREQ):
        row = lax.broadcasted_iota(i32, (8, NREP * PAD), 0)
        column = lax.broadcasted_iota(i32, (8, NREP * PAD), 1)
        pick = jnp.where(column == layout_ref[SOURCE + r] + row, 1.0, 0.0).astype(bf16)
        out_ref[r] = jnp.dot(pick, pool, preferred_element_type=f32)[:STEPS].astype(bf16)


def select(layout, pool):
    return pl.pallas_call(
        select_kernel,
        in_specs=[SMEM, VMEM],
        out_specs=VMEM,
        out_shape=jax.ShapeDtypeStruct((NREQ, STEPS, HEADS * VD), bf16),
        cost_estimate=pl.CostEstimate(flops=1_000_000, bytes_accessed=50_000, transcendentals=0),
        name="select_slots",
    )(layout, pool)


def prefill_kernel(layout_ref, q_ref, cache_ref, kv_ref, out_ref, key_ref, value_ref):
    for j in range(4):
        rows = slice(j * 2 * BLK, (j + 1) * 2 * BLK)
        wide = jnp.dot(cache_ref[rows, :KVL], kv_ref[...], preferred_element_type=f32).astype(bf16)
        for h in range(HEADS):
            base = h * (NOPE + VD)
            key_ref[h, rows, :NOPE] = wide[:, base : base + NOPE]
            key_ref[h, rows, NOPE:] = cache_ref[rows, KVL:]
            value_ref[h, rows, :] = wide[:, base + NOPE : base + NOPE + VD]
    for i in range(8):
        first = max(0, i - REACH + 1) * BLK
        last = (i + 1) * BLK
        shape = (BLK, last - first)
        column = lax.broadcasted_iota(i32, shape, 1) + first
        row = lax.broadcasted_iota(i32, shape, 0) + i * BLK
        ok = (column >= layout_ref[FIRST + i]) & (column <= row)
        scores = [
            dot_t(q_ref[h, i * BLK : last, :], key_ref[h, first:last, :]) * SIGMA for h in range(HEADS)
        ]
        scores = [jnp.where(ok, s, -1e30) for s in scores]
        weights = [jnp.exp(s - jnp.max(s, axis=1, keepdims=True)) for s in scores]
        weights = [(w * (1.0 / jnp.sum(w, axis=1, keepdims=True))).astype(bf16) for w in weights]
        for h in range(HEADS):
            out_ref[i * BLK : last, h * VD : (h + 1) * VD] = jnp.dot(
                weights[h], value_ref[h, first:last, :], preferred_element_type=f32
            ).astype(bf16)


def prefill(layout, queries, cache, kv_up):
    rows = cache.shape[0]
    return pl.pallas_call(
        prefill_kernel,
        in_specs=[SMEM] + [VMEM] * 3,
        out_specs=VMEM,
        out_shape=jax.ShapeDtypeStruct((rows, HEADS * VD), bf16),
        scratch_shapes=[
            pltpu.VMEM((HEADS, rows, 2 * NOPE), bf16),
            pltpu.VMEM((HEADS, rows, VD), bf16),
        ],
        compiler_params=pltpu.CompilerParams(vmem_limit_bytes=32 * 1024 * 1024),
        cost_estimate=pl.CostEstimate(flops=1_500_000_000, bytes_accessed=4_000_000, transcendentals=1_000_000),
        name="prefill_attention",
    )(layout, queries, cache, kv_up)


def body(hidden, comp_query, kv_down, kv_gain, q_up, kv_up, req_blocks, dest_slot, dec_query, dec_latent):
    ids = jnp.stack(
        [lax.axis_index("rep"), lax.axis_index("x"), lax.axis_index("yh"), lax.axis_index(("yh", "z"))]
    ).astype(i32)
    rows = hidden.shape[1]
    per_x = rows // NX
    cos_part, sin_part = rotary_table()

    own = comp_query[0]
    packed = lax.all_to_all(pack(hidden[0].T, kv_down, own), "x", 0, 0, tiled=True)
    layout = request_layout(ids, req_blocks, dest_slot)
    rep_in = jnp.concatenate([dec_query, dec_latent], axis=2)

    def rep_step(part, d):
        met = lax.ppermute(part, "rep", [(i, i ^ d) for i in range(NREP)])
        return jnp.concatenate([part, met])

    rep_in = rep_step(rep_in, 1)
    packed, rep_in, layout = lax.optimization_barrier((packed, rep_in, layout))
    partial, line = meet(packed, per_x, own.shape[1])
    line = jnp.concatenate([line, lax.ppermute(line, "yh", shift(2, 1))])
    cq = lax.all_gather(line, "z", axis=0, tiled=True)

    ready = prepare_decode(layout, rep_step(rep_in, 2), q_up, kv_up, cos_part, sin_part)
    pieces = lax.all_to_all(partial, ("yh", "z"), 0, 0, tiled=True)
    pieces, ready = lax.optimization_barrier((pieces, ready))
    copies = norm_rows(layout, pieces, kv_gain[None, :], cos_part, sin_part)
    cache = lax.all_to_all(copies, ("yh", "z"), 0, 0, tiled=True).reshape(per_x, -1)

    cache = spread(cache, "x", NX).reshape(rows, -1)

    queries = project_queries(layout, cq.reshape(8, 8, PAD, -1), q_up, cos_part, sin_part)
    cache, queries = lax.optimization_barrier((cache, queries))
    result = decode(layout, ready, cache, kv_up)
    pool = lax.all_to_all(result, "rep", 0, 0, tiled=True)
    prefill_out = prefill(layout, queries, cache, kv_up)[None]
    pool, prefill_out = lax.optimization_barrier((pool, prefill_out))
    return prefill_out, select(layout, pool)


def solution(mesh):
    fine = Mesh(mesh.devices.reshape(2, 2, 4, 8, 4), ("section", "yh", "x", "z", "rep"))
    tp = ("yh", "x", "z")
    group = ("section", "rep")
    in_specs = (
        P(group, None, tp),
        P(group, tp, None),
        P(tp, None),
        P(),
        P(None, tp),
        P(None, tp),
        P("section", None),
        P("section", None),
        P(group, None, None),
        P(group, None, None),
    )
    out_specs = (P(group, None, tp), P(group, None, tp))
    return jax.shard_map(body, mesh=fine, in_specs=in_specs, out_specs=out_specs, check_vma=False)
```

```python
import math

import jax
import jax.numpy as jnp
import numpy as np
from jax import lax
from jax.experimental import pallas as pl
from jax.experimental.pallas import tpu as pltpu
from jax.sharding import Mesh, PartitionSpec as P

KVL = 512
NOPE = 128
ROPE = 64
VD = 128
BLK = 128
NREQ = 3
STEPS = 4
REACH = 4
NREP = 4
NX = 4
HEADS = 2
PAD = 16
TABLE = 640
NORM_FLOPS = 30_000_000_000
WIDE = KVL + 2 * ROPE
START, LENGTH, BASE, PLACE, FIRST, SOURCE, SLOT, HALF, LINE = 0, 3, 6, 8, 16, 24, 28, 32, 40

SIGMA = (1.0 + 0.1 * math.log(40.0)) ** 2 * (NOPE + ROPE) ** (-0.5)
bf16 = jnp.bfloat16
f32 = jnp.float32
i32 = jnp.int32


def rotary_table():
    half = ROPE // 2
    frequency = np.float32(10000.0) ** (-np.arange(half, dtype=np.float32) * np.float32(2.0 / ROPE))
    angles = np.arange(TABLE, dtype=np.float32)[:, None] * frequency.astype(np.float32)
    cos_part, sin_part = np.cos(angles), np.sin(angles)
    return np.concatenate([cos_part] * 4, axis=1), np.concatenate([-sin_part, sin_part] * 2, axis=1)


def rotate(u, cos_part, sin_part):
    lane = lax.broadcasted_iota(i32, u.shape, 1)
    swapped = jnp.where(lane % ROPE < ROPE // 2, pltpu.roll(u, 96, 1), pltpu.roll(u, 32, 1))
    return u * cos_part + swapped * sin_part


def split_heads(u):
    a, b, c = u[:, :NOPE], u[:, NOPE : 2 * NOPE], u[:, 2 * NOPE :]
    low = lax.broadcasted_iota(i32, a.shape, 1) < ROPE
    return a, jnp.where(low, pltpu.roll(b, ROPE, 1), pltpu.roll(c, ROPE, 1)), jnp.where(low, b, c)


def spread(a, axes, count):
    copies = jnp.broadcast_to(a[None], (count,) + a.shape)
    return lax.all_to_all(copies, axes, 0, 0, tiled=True)


def shift(count, d):
    return [(i, (i + d) % count) for i in range(count)]


def dot_t(a, b):
    return lax.dot_general(a, b, (((1,), (1,)), ((), ())), preferred_element_type=f32)


def layout_kernel(ids_ref, req_ref, slot_ref, out_ref):
    rep, x, yh, yz = ids_ref[0], ids_ref[1], ids_ref[2], ids_ref[3]
    lengths = [req_ref[rep, r] for r in range(NREQ)]
    starts = [0, lengths[0], lengths[0] + lengths[1]]

    def start_of(block):
        return jnp.where(block >= starts[2], starts[2], jnp.where(block >= starts[1], starts[1], 0))

    for r in range(NREQ):
        out_ref[START + r] = starts[r] * BLK
        out_ref[LENGTH + r] = lengths[r] * BLK
        slot = slot_ref[0, rep * NREQ + r]
        out_ref[SLOT + r] = (lax.div(slot, NREQ) ^ rep) * NREQ + lax.rem(slot, NREQ)
        source = 0
        for m in range(NREP * NREQ):
            source += jnp.where(slot_ref[0, m] == rep * NREQ + r, m, 0)
        out_ref[SOURCE + r] = lax.div(source, NREQ) * PAD + lax.rem(source, NREQ) * STEPS
    for j in range(2):
        out_ref[HALF + j] = yh ^ j
    for d in range(NX):
        out_ref[LINE + d] = lax.rem(x + NX - d, NX)
    out_ref[BASE] = x * 2 * BLK + yz * PAD - start_of(x * 2 + lax.div(yz, 8)) * BLK
    for i in range(8):
        out_ref[PLACE + i] = i - start_of(i)
        out_ref[FIRST + i] = start_of(i) * BLK


SMEM = pl.BlockSpec(memory_space=pltpu.SMEM)
VMEM = pl.BlockSpec(memory_space=pltpu.VMEM)


def request_layout(ids, req_blocks, dest_slot):
    return pl.pallas_call(
        layout_kernel,
        in_specs=[SMEM] * 3,
        out_specs=SMEM,
        out_shape=jax.ShapeDtypeStruct((64,), i32),
        cost_estimate=pl.CostEstimate(flops=1000, bytes_accessed=1000, transcendentals=0),
        name="request_layout",
    )(ids, req_blocks, dest_slot)


def pack_kernel(hidden_ref, down_ref, out_ref):
    per_x = hidden_ref.shape[1] // NX
    for i in range(NX):
        out_ref[i, :, :per_x] = hidden_ref[:, i * per_x : (i + 1) * per_x]
        out_ref[i, :, per_x:] = down_ref[...]


def pack(hidden_t, kv_down):
    features, rows = hidden_t.shape
    return pl.pallas_call(
        pack_kernel,
        in_specs=[VMEM] * 2,
        out_specs=VMEM,
        out_shape=jax.ShapeDtypeStruct((NX, features, rows // NX + kv_down.shape[1]), bf16),
        cost_estimate=pl.CostEstimate(flops=0, bytes_accessed=1_200_000, transcendentals=0),
        name="pack_hidden",
    )(hidden_t, kv_down)


def norm_kernel(layout_ref, pieces_ref, gain_ref, cos_ref, sin_ref, out_ref):
    latent = jnp.sum(pieces_ref[...], axis=0)
    content = latent[:, :KVL]
    scale = lax.rsqrt(jnp.mean(content * content, axis=1, keepdims=True) + 1e-06)
    content = (content * scale * gain_ref[...]).astype(bf16)
    at = pl.ds(pl.multiple_of(layout_ref[BASE], PAD), latent.shape[0])
    pe = jnp.concatenate([latent[:, KVL:]] * 2, axis=1)
    pe = rotate(pe, cos_ref[at, :], sin_ref[at, :]).astype(bf16)
    for i in range(out_ref.shape[0]):
        out_ref[i, :, :KVL] = content
        out_ref[i, :, KVL:] = pe


def norm_rows(layout, pieces, gain, cos_part, sin_part):
    count, chunk, _ = pieces.shape
    return pl.pallas_call(
        norm_kernel,
        in_specs=[SMEM] + [VMEM] * 4,
        out_specs=VMEM,
        out_shape=jax.ShapeDtypeStruct((count, chunk, WIDE), bf16),
        cost_estimate=pl.CostEstimate(flops=NORM_FLOPS, bytes_accessed=1_000_000, transcendentals=16),
        name="norm_rows",
    )(layout, pieces, gain, cos_part, sin_part)


def query_kernel(layout_ref, cq_ref, w_ref, cos_ref, sin_ref, out_ref):
    half = pl.program_id(0)
    rows = jnp.concatenate([cq_ref[:, d].reshape(BLK, -1) for d in range(NX)])
    u = jnp.dot(rows, w_ref[...], preferred_element_type=f32)
    first, second, pe = split_heads(u)
    low = lax.broadcasted_iota(i32, (BLK, 2 * ROPE), 1) < ROPE
    for d in range(NX):
        here = slice(d * BLK, (d + 1) * BLK)
        line = layout_ref[LINE + d]
        to = pl.ds(pl.multiple_of(line * BLK, BLK), BLK)
        at = pl.ds(pl.multiple_of(layout_ref[PLACE + half * NX + line] * BLK, BLK), BLK)
        turned = rotate(pe[here], cos_ref[at, :], sin_ref[at, :])
        out_ref[0, to, :NOPE] = first[here].astype(bf16)
        out_ref[0, to, NOPE:] = jnp.where(low, turned, 0.0).astype(bf16)
        out_ref[1, to, :NOPE] = second[here].astype(bf16)
        out_ref[1, to, NOPE:] = jnp.where(low, 0.0, turned).astype(bf16)


def project_queries(layout, cq, weights, cos_part, sin_part):
    width = cq.shape[-1]
    table = pl.BlockSpec(cos_part.shape, lambda j, place: (0, 0))
    return pl.pallas_call(
        query_kernel,
        grid_spec=pltpu.PrefetchScalarGridSpec(
            num_scalar_prefetch=1,
            grid=(2,),
            in_specs=[
                pl.BlockSpec((8, NX, PAD, width), lambda j, place: (0, place[HALF + j], 0, 0)),
                pl.BlockSpec(weights.shape, lambda j, place: (0, 0)),
                table,
                table,
            ],
            out_specs=pl.BlockSpec((HEADS, NX * BLK, 2 * NOPE), lambda j, place: (0, j, 0)),
        ),
        out_shape=jax.ShapeDtypeStruct((HEADS, 8 * BLK, 2 * NOPE), bf16),
        compiler_params=pltpu.CompilerParams(vmem_limit_bytes=60 * 1024 * 1024),
        cost_estimate=pl.CostEstimate(flops=1_200_000_000, bytes_accessed=5_000_000, transcendentals=0),
        name="project_queries",
    )(layout, cq, weights, cos_part, sin_part)


def prepare_kernel(layout_ref, rows_ref, w_ref, kv_ref, cos_ref, sin_ref, out_ref, in_ref, cos_at, sin_at):
    query_latent = w_ref.shape[0]
    in_ref[...] = jnp.zeros_like(in_ref)
    cos_at[...] = jnp.zeros_like(cos_at)
    sin_at[...] = jnp.zeros_like(sin_at)
    for r in range(NREQ):
        here = slice(r * STEPS, (r + 1) * STEPS)
        in_ref[here, :] = rows_ref[layout_ref[SLOT + r]].astype(f32)
        at = pl.ds(pl.multiple_of(layout_ref[LENGTH + r], BLK), 8)
        cos_at[here, :] = cos_ref[at, :][:STEPS]
        sin_at[here, :] = sin_ref[at, :][:STEPS]
    cos_part, sin_part = cos_at[...], sin_at[...]
    rows = in_ref[:, :query_latent].astype(bf16)
    u = jnp.dot(rows, w_ref[...], preferred_element_type=f32).astype(bf16).astype(f32)
    first, second, pe = split_heads(u)
    pe = rotate(pe, cos_part, sin_part)
    low = lax.broadcasted_iota(i32, pe.shape, 1) < ROPE
    for h, plain in enumerate((first, second)):
        here = slice(h * PAD, (h + 1) * PAD)
        base = h * (NOPE + VD)
        out_ref[here, :KVL] = dot_t(plain.astype(bf16), kv_ref[:, base : base + NOPE]).astype(bf16)
        out_ref[here, KVL:] = jnp.where(low == (h == 0), pe, 0.0).astype(bf16)
    new = slice(HEADS * PAD, (HEADS + 1) * PAD)
    out_ref[new, :KVL] = in_ref[:, query_latent : query_latent + KVL].astype(bf16)
    new_pe = jnp.concatenate([in_ref[:, query_latent + KVL :]] * 2, axis=1)
    out_ref[new, KVL:] = rotate(new_pe, cos_part, sin_part).astype(bf16)


def prepare_decode(layout, rows, q_up, kv_up, cos_part, sin_part):
    return pl.pallas_call(
        prepare_kernel,
        in_specs=[SMEM] + [VMEM] * 5,
        out_specs=VMEM,
        out_shape=jax.ShapeDtypeStruct(((HEADS + 1) * PAD, WIDE), bf16),
        scratch_shapes=[
            pltpu.VMEM((PAD, rows.shape[-1]), f32),
            pltpu.VMEM((PAD, 2 * ROPE), f32),
            pltpu.VMEM((PAD, 2 * ROPE), f32),
        ],
        compiler_params=pltpu.CompilerParams(vmem_limit_bytes=16 * 1024 * 1024),
        cost_estimate=pl.CostEstimate(flops=30_000_000, bytes_accessed=2_500_000, transcendentals=0),
        name="prepare_decode",
    )(layout, rows, q_up, kv_up, cos_part, sin_part)


def decode_kernel(layout_ref, ready_ref, cache_ref, kv_ref, out_ref):
    query = ready_ref[: HEADS * PAD, :]
    fresh = ready_ref[HEADS * PAD :, :]
    old = dot_t(query, cache_ref[...]) * SIGMA
    new = dot_t(query, fresh) * SIGMA
    request = lax.broadcasted_iota(i32, (HEADS * PAD, 1), 0) % PAD // STEPS

    def per_request(values):
        return jnp.where(request == 0, values[0], jnp.where(request == 1, values[1], values[2]))

    low = per_request([layout_ref[START + r] for r in range(NREQ)])
    high = per_request([layout_ref[START + r] + layout_ref[LENGTH + r] for r in range(NREQ)])
    column = lax.broadcasted_iota(i32, old.shape, 1)
    old = jnp.where((column >= low) & (column < high), old, -1e30)
    step = lax.broadcasted_iota(i32, new.shape, 0) % PAD
    other = lax.broadcasted_iota(i32, new.shape, 1)
    new = jnp.where((step // STEPS == other // STEPS) & (other <= step), new, -1e30)
    top = jnp.maximum(jnp.max(old, axis=1, keepdims=True), jnp.max(new, axis=1, keepdims=True))
    old = jnp.exp(old - top)
    new = jnp.exp(new - top)
    inverse = 1.0 / (jnp.sum(old, axis=1, keepdims=True) + jnp.sum(new, axis=1, keepdims=True))
    old = (old * inverse).astype(bf16)
    new = (new * inverse).astype(bf16)
    mixture = (
        jnp.dot(old, cache_ref[:, :KVL], preferred_element_type=f32)
        + jnp.dot(new, fresh[:, :KVL], preferred_element_type=f32)
    ).astype(bf16)
    for h in range(HEADS):
        base = h * (NOPE + VD) + NOPE
        value = jnp.dot(
            mixture[h * PAD : (h + 1) * PAD], kv_ref[:, base : base + VD], preferred_element_type=f32
        ).astype(bf16)
        for i in range(NREP):
            out_ref[i, :, h * VD : (h + 1) * VD] = value


def decode(layout, ready, cache, kv_up):
    return pl.pallas_call(
        decode_kernel,
        in_specs=[SMEM] + [VMEM] * 3,
        out_specs=VMEM,
        out_shape=jax.ShapeDtypeStruct((NREP, PAD, HEADS * VD), bf16),
        compiler_params=pltpu.CompilerParams(vmem_limit_bytes=16 * 1024 * 1024),
        cost_estimate=pl.CostEstimate(flops=100_000_000, bytes_accessed=2_000_000, transcendentals=40_000),
        name="decode_attention",
    )(layout, ready, cache, kv_up)


def select_kernel(layout_ref, pool_ref, out_ref):
    pool = pool_ref[...].reshape(NREP * PAD, -1)
    for r in range(NREQ):
        row = lax.broadcasted_iota(i32, (8, NREP * PAD), 0)
        column = lax.broadcasted_iota(i32, (8, NREP * PAD), 1)
        pick = jnp.where(column == layout_ref[SOURCE + r] + row, 1.0, 0.0).astype(bf16)
        out_ref[r] = jnp.dot(pick, pool, preferred_element_type=f32)[:STEPS].astype(bf16)


def select(layout, pool):
    return pl.pallas_call(
        select_kernel,
        in_specs=[SMEM, VMEM],
        out_specs=VMEM,
        out_shape=jax.ShapeDtypeStruct((NREQ, STEPS, HEADS * VD), bf16),
        cost_estimate=pl.CostEstimate(flops=1_000_000, bytes_accessed=50_000, transcendentals=0),
        name="select_slots",
    )(layout, pool)


def prefill_kernel(layout_ref, q_ref, cache_ref, kv_ref, out_ref, key_ref, value_ref):
    for j in range(4):
        rows = slice(j * 2 * BLK, (j + 1) * 2 * BLK)
        wide = jnp.dot(cache_ref[rows, :KVL], kv_ref[...], preferred_element_type=f32).astype(bf16)
        for h in range(HEADS):
            base = h * (NOPE + VD)
            key_ref[h, rows, :NOPE] = wide[:, base : base + NOPE]
            key_ref[h, rows, NOPE:] = cache_ref[rows, KVL:]
            value_ref[h, rows, :] = wide[:, base + NOPE : base + NOPE + VD]
    for i in range(8):
        first = max(0, i - REACH + 1) * BLK
        last = (i + 1) * BLK
        shape = (BLK, last - first)
        column = lax.broadcasted_iota(i32, shape, 1) + first
        row = lax.broadcasted_iota(i32, shape, 0) + i * BLK
        ok = (column >= layout_ref[FIRST + i]) & (column <= row)
        scores = [
            dot_t(q_ref[h, i * BLK : last, :], key_ref[h, first:last, :]) * SIGMA for h in range(HEADS)
        ]
        scores = [jnp.where(ok, s, -1e30) for s in scores]
        weights = [jnp.exp(s - jnp.max(s, axis=1, keepdims=True)) for s in scores]
        weights = [(w * (1.0 / jnp.sum(w, axis=1, keepdims=True))).astype(bf16) for w in weights]
        for h in range(HEADS):
            out_ref[i * BLK : last, h * VD : (h + 1) * VD] = jnp.dot(
                weights[h], value_ref[h, first:last, :], preferred_element_type=f32
            ).astype(bf16)


def prefill(layout, queries, cache, kv_up):
    rows = cache.shape[0]
    return pl.pallas_call(
        prefill_kernel,
        in_specs=[SMEM] + [VMEM] * 3,
        out_specs=VMEM,
        out_shape=jax.ShapeDtypeStruct((rows, HEADS * VD), bf16),
        scratch_shapes=[
            pltpu.VMEM((HEADS, rows, 2 * NOPE), bf16),
            pltpu.VMEM((HEADS, rows, VD), bf16),
        ],
        compiler_params=pltpu.CompilerParams(vmem_limit_bytes=32 * 1024 * 1024),
        cost_estimate=pl.CostEstimate(flops=1_500_000_000, bytes_accessed=4_000_000, transcendentals=1_000_000),
        name="prefill_attention",
    )(layout, queries, cache, kv_up)


def body(hidden, comp_query, kv_down, kv_gain, q_up, kv_up, req_blocks, dest_slot, dec_query, dec_latent):
    ids = jnp.stack(
        [lax.axis_index("rep"), lax.axis_index("x"), lax.axis_index("yh"), lax.axis_index(("yh", "z"))]
    ).astype(i32)
    rows, features = hidden.shape[1:]
    per_x = rows // NX
    chunk = per_x // 16
    cos_part, sin_part = rotary_table()

    own = comp_query[0]
    packed = lax.all_to_all(pack(hidden[0].T, kv_down), "x", 0, 0, tiled=True)
    layout = request_layout(ids, req_blocks, dest_slot)
    line = jnp.concatenate([own] + [lax.ppermute(own, "x", shift(NX, d)) for d in range(1, NX)])
    packed, line, dec_query, dec_latent = lax.optimization_barrier((packed, line, dec_query, dec_latent))
    line = jnp.concatenate([line, lax.ppermute(line, "yh", shift(2, 1))])
    cq = lax.all_gather(line, "z", axis=0, tiled=True)

    packed = packed.reshape(NX * features, -1)
    partial = lax.dot_general(
        packed[:, :per_x], packed[:, per_x:], (((0,), (0,)), ((), ())), preferred_element_type=f32
    )
    pieces = lax.all_to_all(partial.reshape(16, chunk, -1), ("yh", "z"), 0, 0, tiled=True)
    copies = norm_rows(layout, pieces, kv_gain[None, :], cos_part, sin_part)
    cache = lax.all_to_all(copies, ("yh", "z"), 0, 0, tiled=True).reshape(per_x, -1)

    rep_in = jnp.concatenate([dec_query, dec_latent], axis=2)

    def rep_step(part, d):
        met = lax.ppermute(part, "rep", [(i, i ^ d) for i in range(NREP)])
        return jnp.concatenate([part, met])

    cache, rep_in = lax.optimization_barrier((cache, rep_step(rep_in, 1)))
    ready = prepare_decode(layout, rep_step(rep_in, 2), q_up, kv_up, cos_part, sin_part)
    cache = spread(cache, "x", NX).reshape(rows, -1)

    queries = project_queries(layout, cq.reshape(8, 8, PAD, -1), q_up, cos_part, sin_part)
    cache, queries = lax.optimization_barrier((cache, queries))
    result = decode(layout, ready, cache, kv_up)
    pool = lax.all_to_all(result, "rep", 0, 0, tiled=True)
    prefill_out = prefill(layout, queries, cache, kv_up)[None]
    pool, prefill_out = lax.optimization_barrier((pool, prefill_out))
    return prefill_out, select(layout, pool)


def solution(mesh):
    fine = Mesh(mesh.devices.reshape(2, 2, 4, 8, 4), ("section", "yh", "x", "z", "rep"))
    tp = ("yh", "x", "z")
    group = ("section", "rep")
    in_specs = (
        P(group, None, tp),
        P(group, tp, None),
        P(tp, None),
        P(),
        P(None, tp),
        P(None, tp),
        P("section", None),
        P("section", None),
        P(group, None, None),
        P(group, None, None),
    )
    out_specs = (P(group, None, tp), P(group, None, tp))
    return jax.shard_map(body, mesh=fine, in_specs=in_specs, out_specs=out_specs, check_vma=False)
```
